32 devices in a mesh: shots: 2 (over x), xline: 8 (over z, y), inline: 2 (over core).
Axes of the slice: x: 2, y: 2, z: 4, core: 2. Of those that a mesh axis runs over, the one named last changes fastest.
Arguments:
- fwd_now: float32 [128, 64, 256], P(('shots', 'inline'), 'xline'), parts along dimension 0, may hold values from -6 to 6
- fwd_before: float32 [128, 64, 256], P(('shots', 'inline'), 'xline'), parts along dimension 0, may hold values from -6 to 6
- adj_now: float32 [128, 64, 256], P(('shots', 'inline'), 'xline'), parts along dimension 0, may hold values from -6 to 6
- adj_before: float32 [128, 64, 256], P(('shots', 'inline'), 'xline'), parts along dimension 0, may hold values from -6 to 6
- velocity: float32 [64, 64, 256], P('inline', 'xline'), may hold values from 0.2 to 0.4
- log_density: float32 [64, 64, 256], P('inline', 'xline'), may hold values from -0.3 to 0.3
- observed: float32 [16, 2048], P('shots', ('xline', 'inline')), parts along dimension 0, may hold values from -48 to 48
- rec_cells: int32 [16, 128], P(('xline', 'inline')), may hold values from 0 to 65535
- rec_counts: int32 [16, 16], P(('xline', 'inline')), may hold values from 0 to 8, as said below
- src_cell: int32 [32], P('shots'), parts along dimension 0, may hold values from 0 to 1048575
- wavelet: float32 [16, 16], P('shots'), parts along dimension 0, may hold values from -144 to 144
Outputs:
- gradient: float32 [512, 64, 64], P(('shots', 'xline'), 'inline'), parts along dimension 0
- adjoint_state: float32 [128, 64, 256], P(('shots', 'inline'), 'xline'), parts along dimension 0
- adjoint_previous: float32 [128, 64, 256], P(('shots', 'inline'), 'xline'), parts along dimension 0
The draws below stay inside these ranges and needn't reach their ends.
There are 2 independent parts, one for each index of `shots`. The reference program is written for one: setup_inputs(seed, part) draws one part's arguments, and reference() takes and returns one part's arrays. A program takes and returns all parts, laid end to end along the dimension named above; an argument that names none is the same for every part. Nothing has to cross between parts.
Inputs may be any that keep to these rules, and one draw needn't show every extreme that they name: rec_counts[o, s] live slots of the 8 that device s sends to subdomain o; in every draw one subdomain receives 8 live slots from every device.
All inputs are finite; a program needn't handle non-finite values.
Results may differ from the reference program's by a relative error of at most 0.04.
Values sent between devices are 32-bit elements; how exact they have to be, the bound alone decides.
A program may use at most 64 MiB of HBM per device.

```python
import jax
import jax.numpy as jnp
from jax import lax

CI = 32
CX = 8
NZ = 256
NT = 8
NSRC = 16
CAP = 8
NI = 64
NX = 64
SUBS = 16
SMOOTH = 16
N_INLINE = 2


def draw_rec_counts(key, part):
    key_top, key_raw, key_full = jax.random.split(key, 3)
    ceiling = jax.random.randint(key_top, (SUBS, 1), 1, CAP + 1)
    spread = jax.random.randint(key_raw, (SUBS, SUBS), 0, 1 << 20) % (ceiling + 1)
    counts = (ceiling + spread) // 2
    owner = jax.random.randint(key_full, (), 0, SUBS)
    return jnp.where(jnp.arange(SUBS)[:, None] == owner, CAP, counts).astype(jnp.int32)


def plant(entries, own_key, least, largest):
    dims = entries.shape
    index_at = [jax.random.randint(jax.random.fold_in(own_key, axis), (), 0, dims[axis]) for axis in range(len(dims))]
    entries = entries.at[tuple(index_at)].set(least)
    longest = dims.index(max(dims))
    index_at[longest] = (index_at[longest] + 1) % dims[longest]
    return entries.at[tuple(index_at)].set(largest)


def shard_levels(rng, shape, pieces, smallest, top_value):
    level, own = 1.0, jax.random.fold_in(rng, 6)
    for axis_at, shards_of in pieces:
        steps = jnp.exp(jax.random.uniform(jax.random.fold_in(own, axis_at), (shards_of,), jnp.float32, smallest / len(pieces), top_value / len(pieces)))
        level = level * jnp.repeat(steps, shape[axis_at] // shards_of).reshape([-1 if axis == axis_at else 1 for axis in range(len(shape))])
    return level


def noise(stream_key, shape, scale, bound, shards=(), dtype=jnp.bfloat16):
    array = scale * jax.random.normal(stream_key, shape, jnp.float32)
    if shards:
        array = array * shard_levels(stream_key, shape, shards, -0.22, 0.18)
    return jnp.clip(array, -bound, bound).astype(dtype)


def setup_inputs(seed: int = 0, part: int = 0) -> dict:
    key_list = jax.random.split(jax.random.key(seed), 12)
    part_splits = jax.random.split(jax.random.fold_in(key_list[11], part), 12)
    return {
        "fwd_now": noise(part_splits[0], (NI, NX, NZ), 1.0, 6.0, ((0, 2), (1, 8)), jnp.float32),
        "fwd_before": noise(part_splits[1], (NI, NX, NZ), 1.0, 6.0, ((0, 2), (1, 8)), jnp.float32),
        "adj_now": noise(part_splits[2], (NI, NX, NZ), 1.0, 6.0, ((0, 2), (1, 8)), jnp.float32),
        "adj_before": noise(part_splits[3], (NI, NX, NZ), 1.0, 6.0, ((0, 2), (1, 8)), jnp.float32),
        "velocity": jnp.clip(0.2 + 0.2 * jax.random.uniform(key_list[4], (NI, NX, NZ), jnp.float32) ** shard_levels(key_list[4], (NI, NX, NZ), ((0, 2), (1, 8)), -0.2, 0.2), 0.2, 0.4),
        "log_density": jnp.clip(jax.random.uniform(key_list[5], (NI, NX, NZ), jnp.float32, -0.3, 0.3) * shard_levels(key_list[5], (NI, NX, NZ), ((0, 2), (1, 8)), -0.4, 0.0), -0.3, 0.3),
        "observed": noise(part_splits[6], (NT, SUBS * SUBS * CAP), 8.0, 48.0, ((1, 16),), jnp.float32),
        "rec_cells": plant(jax.random.randint(key_list[7], (SUBS, SUBS * CAP), 0, CI * CX * NZ), jax.random.fold_in(key_list[7], 1), 0, (CI * CX * NZ) - 1).astype(jnp.int32),
        "rec_counts": draw_rec_counts(jax.random.fold_in(key_list[11], 71), part),
        "src_cell": plant(jax.random.randint(part_splits[9], (NSRC,), 0, NI * NX * NZ), jax.random.fold_in(part_splits[9], 1), 0, (NI * NX * NZ) - 1).astype(jnp.int32),
        "wavelet": noise(part_splits[10], (NT, NSRC), 24.0, 144.0, (), jnp.float32),
    }


SECOND_COEFFS = (-205.0 / 72.0, 8.0 / 5.0, -1.0 / 5.0, 8.0 / 315.0, -1.0 / 560.0)
FIRST_COEFFS = (4.0 / 5.0, -1.0 / 5.0, 4.0 / 105.0, -1.0 / 280.0)


def differences(padded):
    inner_a = padded.shape[0] - 8
    inner_b = padded.shape[1] - 8
    center = padded[4:4 + inner_a, 4:4 + inner_b]
    extent = center.shape[2]
    deep_pad = jnp.pad(center, ((0, 0), (0, 0), (4, 4)))
    laplace = (3.0 * SECOND_COEFFS[0]) * center
    slope_i = jnp.zeros_like(center)
    slope_x = jnp.zeros_like(center)
    slope_z = jnp.zeros_like(center)
    for offset in range(1, 5):
        plus_i = padded[4 + offset:4 + offset + inner_a, 4:4 + inner_b]
        minus_i = padded[4 - offset:4 - offset + inner_a, 4:4 + inner_b]
        plus_x = padded[4:4 + inner_a, 4 + offset:4 + offset + inner_b]
        minus_x = padded[4:4 + inner_a, 4 - offset:4 - offset + inner_b]
        plus_z = deep_pad[:, :, 4 + offset:4 + offset + extent]
        minus_z = deep_pad[:, :, 4 - offset:4 - offset + extent]
        weight_first = FIRST_COEFFS[offset - 1]
        slope_i = slope_i + weight_first * (plus_i - minus_i)
        slope_x = slope_x + weight_first * (plus_x - minus_x)
        slope_z = slope_z + weight_first * (plus_z - minus_z)
        laplace = laplace + SECOND_COEFFS[offset] * (plus_i + minus_i + plus_x + minus_x + plus_z + minus_z)
    return laplace, (slope_i, slope_x, slope_z)


def wave_operator(padded, density_slopes, speed_sq):
    laplace, slopes = differences(padded)
    coupling = density_slopes[0] * slopes[0] + density_slopes[1] * slopes[1] + density_slopes[2] * slopes[2]
    return speed_sq * (laplace - coupling)


def pad_four(values):
    return jnp.pad(values, ((4, 4), (4, 4), (0, 0)))


def reference(fwd_now, fwd_before, adj_now, adj_before, velocity, log_density, observed, rec_cells, rec_counts, src_cell, wavelet):
    cell_total = NI * NX * NZ
    spare_term, density_slopes = differences(pad_four(log_density))
    speed_sq = velocity * velocity
    history = [fwd_before, fwd_now]
    for moment in range(NT):
        current = history[-1]
        source_field = jnp.zeros((cell_total,), jnp.float32).at[src_cell].add(wavelet[moment]).reshape(NI, NX, NZ)
        history.append(2.0 * current - history[-2] + wave_operator(pad_four(current), density_slopes, speed_sq) + source_field)
    owner_ids = jnp.arange(SUBS).astype(jnp.int32)
    owner_x = owner_ids // N_INLINE
    owner_i = owner_ids % N_INLINE
    local_i = rec_cells // (CX * NZ)
    local_x = (rec_cells // NZ) % CX
    local_z = rec_cells % NZ
    global_cell = ((owner_i[:, None] * CI + local_i) * NX + owner_x[:, None] * CX + local_x) * NZ + local_z
    live_mask = (jnp.arange(CAP).astype(jnp.int32)[None, None, :] < rec_counts[:, :, None]).astype(jnp.float32).reshape(SUBS, SUBS * CAP)
    routed = observed.reshape(NT, SUBS, SUBS, CAP).transpose(0, 2, 1, 3).reshape(NT, SUBS, SUBS * CAP)
    predicted = jnp.stack([history[moment + 2].reshape(-1)[global_cell] for moment in range(NT)])
    residual = live_mask[None] * (predicted - routed)
    flat_cells = global_cell.reshape(-1)
    adjoint = [adj_before, adj_now]
    image_sum = jnp.zeros_like(fwd_now)
    for back_step in range(NT):
        moment = NT - 1 - back_step
        current = adjoint[-1]
        injected = jnp.zeros((cell_total,), jnp.float32).at[flat_cells].add(residual[moment].reshape(-1)).reshape(NI, NX, NZ)
        fresh_state = 2.0 * current - adjoint[-2] + wave_operator(pad_four(current), density_slopes, speed_sq) + injected
        adjoint.append(fresh_state)
        image_sum = image_sum + fresh_state * (history[moment + 2] - 2.0 * history[moment + 1] + history[moment])
    raw_gradient = image_sum * (2.0 / NT) / velocity
    positions = jnp.arange(NX).astype(jnp.float32)
    kernel = jnp.exp(-jnp.abs(positions[:, None] - positions[None, :]) / SMOOTH)
    kernel = kernel / jnp.sum(kernel, axis=1, keepdims=True)
    gradient = jnp.einsum("ixz,yx->ziy", raw_gradient, kernel, precision=lax.Precision.HIGHEST)
    return gradient, adjoint[-1], adjoint[-2]
```

```python
import functools

import jax
import jax.numpy as jnp
from jax import lax
from jax.experimental import pallas as pl
from jax.experimental.pallas import tpu as pltpu
from jax.sharding import PartitionSpec as P

CAP = 8
SMOOTH = 16
MESH = pl.DeviceIdType.MESH

SECOND_COEFFS = (-205.0 / 72.0, 8.0 / 5.0, -1.0 / 5.0, 8.0 / 315.0, -1.0 / 560.0)
FIRST_COEFFS = (4.0 / 5.0, -1.0 / 5.0, 4.0 / 105.0, -1.0 / 280.0)
LEFT, RIGHT, UP, DOWN = 0, 1, 2, 3
DENSITY = 4
RHO, NOW, SPEED, BEFORE, ADJ_NOW, ADJ_BEFORE = range(6)


def split_bf16(value):
    high = value.astype(jnp.bfloat16)
    low = (value - high.astype(jnp.float32)).astype(jnp.bfloat16)
    return high, low


def dot(a, b):
    return jnp.dot(a, b, preferred_element_type=jnp.float32)


def dot_nt(a, b):
    return lax.dot_general(a, b, (((1,), (1,)), ((), ())), preferred_element_type=jnp.float32)


def dot_tn_exact(a, b):
    dims = (((0,), (0,)), ((), ()))
    ah, al = split_bf16(a)
    bh, bl = split_bf16(b)
    one = lax.dot_general(ah, bh, dims, preferred_element_type=jnp.float32)
    two = lax.dot_general(al, bh, dims, preferred_element_type=jnp.float32)
    three = lax.dot_general(ah, bl, dims, preferred_element_type=jnp.float32)
    return one + (two + three)


def div(value, n):
    return lax.shift_right_arithmetic(value, jnp.full_like(value, n.bit_length() - 1))


def mod(value, n):
    return value & (n - 1)


def wave_kernel(
    sizes,
    log_density, fwd_now, velocity, fwd_before, adj_now, adj_before,
    observed, rec_cells, rec_counts, src_cell, wavelet,
    grad_out, last_out, previous_out,
    field, vel, x_in, x_out, i_in, accel, base, image, slopes, speed_sq, wx,
    row_map, zmap_t, z_mat, residual_ref, traces, list_out, list_in, obs_in, g_send, g_in, kern_t,
    send_sem, recv_sem, rt_send, rt_recv, rt_local, list_send, list_recv, obs_send, obs_recv,
    ret_send, ret_recv, ret_local, g_ssem, g_rsem,
):
    tile_i, tile_x, n_i, n_x, depth, steps, n_xline, fused = sizes
    rows = n_i * n_x
    slots = rec_cells.shape[1]
    n_group = 2 * n_xline
    xl = lax.axis_index("xline")
    core = lax.axis_index("inline")
    me = xl * 2 + core
    y = lax.rem(xl, 2)
    plane = xl // 2
    z_odd = lax.rem(plane, 2)
    mate = xl + 1 - 2 * y
    cp = lax.rem(core + z_odd, 2)
    origin = lax.rem(y + cp, 2)
    q = 2 * origin + cp
    stays = y == z_odd
    has = (xl >= 2, xl < n_xline - 2, q > 0, q < 3)
    other_core = 1 - core
    target = (
        {"xline": xl - 2, "inline": other_core},
        {"xline": xl + 2, "inline": other_core},
        {"xline": jnp.where(q == 2, xl, mate), "inline": other_core},
        {"xline": jnp.where(q == 1, xl, mate), "inline": other_core},
    )
    inner_i = pl.ds(4, n_i)
    inner_x = pl.ds(8, n_x)
    middle = n_i // 2

    barrier = pltpu.get_barrier_semaphore()

    @pl.loop(1, n_group)
    def _(r):
        peer = lax.rem(me + r, n_group)
        pl.semaphore_signal(
            barrier, inc=1, device_id={"xline": peer // 2, "inline": lax.rem(peer, 2)}, device_id_type=MESH
        )

    def copy_of(idx, way, part):
        part_rows = pl.ds(part * middle, middle)
        sem = way
        if way == LEFT:
            src, dst = x_out.at[idx, 0, part_rows], x_in.at[idx, 1, part_rows]
            sem = way + 4 * part
        elif way == RIGHT:
            src, dst = x_out.at[idx, 1, part_rows], x_in.at[idx, 0, part_rows]
            sem = way + 4 * part
        elif way == UP:
            src, dst = field.at[idx, pl.ds(4, 4), inner_x, :], i_in.at[idx, 1]
        else:
            src, dst = field.at[idx, pl.ds(n_i, 4), inner_x, :], i_in.at[idx, 0]
        return pltpu.make_async_remote_copy(
            src_ref=src, dst_ref=dst,
            send_sem=send_sem.at[idx, sem], recv_sem=recv_sem.at[idx, sem],
            device_id=target[way], device_id_type=MESH,
        )

    def send(idx, part):
        for way in (LEFT, RIGHT, UP + part):
            @pl.when(has[way])
            def _():
                copy_of(idx, way, part).start()

    def stage(idx, part):
        part_rows = pl.ds(part * middle, middle)
        field_rows = pl.ds(4 + part * middle, middle)
        x_out[idx, 0, part_rows] = field[idx, field_rows, pl.ds(8, 4), :]
        x_out[idx, 1, part_rows] = field[idx, field_rows, pl.ds(4 + n_x, 4), :]

    def finish(idx, part):
        for way in (LEFT, RIGHT, UP + part):
            @pl.when(has[way])
            def _():
                copy_of(idx, way, part).wait_send()
                copy_of(idx, way ^ 1, part).wait_recv()

    sources = (log_density, fwd_now, velocity, fwd_before, adj_now, adj_before)
    places = (DENSITY, 0, None, 1, 2, 3)

    def landing(n, from_y):
        columns = pl.multiple_of(from_y * tile_x, tile_x)
        if n == SPEED:
            return vel.at[:, pl.ds(columns, tile_x), :]
        return field.at[places[n], inner_i, pl.ds(pl.multiple_of(8 + columns, 8), tile_x), :]

    def tile_copy(n, a):
        return pltpu.make_async_remote_copy(
            src_ref=sources[n].at[pl.ds(a * n_i, n_i)], dst_ref=landing(n, y),
            send_sem=rt_send.at[n, a], recv_sem=rt_recv.at[n, y],
            device_id={"xline": 2 * plane + lax.rem(core + a, 2), "inline": lax.rem(a + z_odd, 2)},
            device_id_type=MESH,
        )

    def tile_arrival(n, from_y):
        return pltpu.make_async_remote_copy(
            src_ref=sources[n].at[pl.ds(0, n_i)], dst_ref=landing(n, from_y),
            send_sem=rt_send.at[n, 0], recv_sem=rt_recv.at[n, from_y],
            device_id={"xline": mate}, device_id_type=MESH,
        )

    def own_copy(n):
        return pltpu.make_async_copy(
            sources[n].at[pl.ds(cp * n_i, n_i)], landing(n, y), rt_local.at[n]
        )

    def leaves(a):
        return jnp.logical_not(jnp.logical_and(stays, cp == a))

    def arrives(from_y):
        return jnp.logical_not(jnp.logical_and(stays, y == from_y))

    def tile_start(n):
        for a in range(2):
            @pl.when(leaves(a))
            def _():
                tile_copy(n, a).start()

        @pl.when(stays)
        def _():
            own_copy(n).start()

    def tile_finish(n):
        for from_y in range(2):
            @pl.when(arrives(from_y))
            def _():
                tile_arrival(n, from_y).wait_recv()
        for a in range(2):
            @pl.when(leaves(a))
            def _():
                tile_copy(n, a).wait_send()

        @pl.when(stays)
        def _():
            own_copy(n).wait()

    def list_copy(a):
        return pltpu.make_async_remote_copy(
            src_ref=list_out, dst_ref=list_in.at[y],
            send_sem=list_send.at[a], recv_sem=list_recv.at[y],
            device_id={"xline": 2 * plane + lax.rem(core + a, 2), "inline": lax.rem(a + z_odd, 2)},
            device_id_type=MESH,
        )

    def list_arrival(from_y):
        return pltpu.make_async_remote_copy(
            src_ref=list_out, dst_ref=list_in.at[from_y],
            send_sem=list_send.at[0], recv_sem=list_recv.at[from_y],
            device_id={"xline": mate}, device_id_type=MESH,
        )

    def obs_copy(peer, slot):
        return pltpu.make_async_remote_copy(
            src_ref=observed, dst_ref=obs_in.at[slot],
            send_sem=obs_send.at[peer], recv_sem=obs_recv.at[slot],
            device_id={"xline": peer // 2, "inline": lax.rem(peer, 2)}, device_id_type=MESH,
        )

    finals = (previous_out, last_out)
    final_idx = (2 + (steps - 1) % 2, 2 + steps % 2)

    def home_copy(n, to_y):
        return pltpu.make_async_remote_copy(
            src_ref=field.at[final_idx[n], inner_i, pl.ds(8 + to_y * tile_x, tile_x), :],
            dst_ref=finals[n].at[pl.ds(cp * n_i, n_i)],
            send_sem=ret_send.at[n, to_y], recv_sem=ret_recv.at[n, cp],
            device_id={"xline": 2 * plane + to_y, "inline": origin}, device_id_type=MESH,
        )

    def home_arrival(n, a):
        return pltpu.make_async_remote_copy(
            src_ref=field.at[final_idx[n], inner_i, pl.ds(8, tile_x), :],
            dst_ref=finals[n].at[pl.ds(a * n_i, n_i)],
            send_sem=ret_send.at[n, 0], recv_sem=ret_recv.at[n, a],
            device_id={"xline": mate}, device_id_type=MESH,
        )

    def home_own(n):
        columns = pl.multiple_of(8 + y * tile_x, 8)
        return pltpu.make_async_copy(
            field.at[final_idx[n], inner_i, pl.ds(columns, tile_x), :],
            finals[n].at[pl.ds(cp * n_i, n_i)], ret_local.at[n],
        )

    def home_start(n):
        for to_y in range(2):
            @pl.when(arrives(to_y))
            def _():
                home_copy(n, to_y).start()

        @pl.when(stays)
        def _():
            home_own(n).start()

    def home_finish(n):
        for to_y in range(2):
            @pl.when(arrives(to_y))
            def _():
                home_copy(n, to_y).wait_send()
        for a in range(2):
            @pl.when(leaves(a))
            def _():
                home_arrival(n, a).wait_recv()

        @pl.when(stays)
        def _():
            home_own(n).wait()

    dz = depth // n_xline
    planes_n = n_xline // 2

    def slab_copy(d):
        return pltpu.make_async_remote_copy(
            src_ref=g_send.at[d],
            dst_ref=g_in.at[cp, :, pl.ds(pl.multiple_of(plane * n_x, 8), n_x), :],
            send_sem=g_ssem.at[d], recv_sem=g_rsem.at[cp, plane],
            device_id={"xline": d, "inline": origin}, device_id_type=MESH,
        )

    def slab_arrival(a, p):
        return pltpu.make_async_remote_copy(
            src_ref=g_send.at[0],
            dst_ref=g_in.at[a, :, pl.ds(pl.multiple_of(p * n_x, 8), n_x), :],
            send_sem=g_ssem.at[0], recv_sem=g_rsem.at[a, p],
            device_id={"xline": mate}, device_id_type=MESH,
        )

    def fused_gradient():
        group = 128 // dz
        lane = div(lax.broadcasted_iota(jnp.int32, (n_x, 128), 1), dz)
        for chunk in range(depth // 128):
            for ig in range(n_i // group):
                planes = [image[ig * group + j, :, pl.ds(chunk * 128, 128)] for j in range(group)]
                for dd in range(group):
                    out = None
                    for j in range(group):
                        shift = (j - dd) * dz % 128
                        moved = pltpu.roll(planes[j], shift, axis=1) if shift else planes[j]
                        out = moved if out is None else jnp.where(lane == j, moved, out)
                    g_send[chunk * group + dd, ig] = out

        @pl.loop(1, n_xline + 1)
        def _(r):
            d = lax.rem(xl + r, n_xline)

            @pl.when(jnp.logical_or(d != xl, origin != core))
            def _():
                slab_copy(d).start()

        home_start(1)

        @pl.when(origin == core)
        def _():
            g_in[cp, :, pl.ds(pl.multiple_of(plane * n_x, 8), n_x), :] = g_send[xl]

        @pl.loop(0, n_xline)
        def _(r):
            a, p = lax.rem(r, 2), r // 2
            mine = jnp.logical_and(origin == core, jnp.logical_and(a == cp, p == plane))

            @pl.when(jnp.logical_not(mine))
            def _():
                slab_arrival(a, p).wait_recv()

        for a in range(2):
            for ig in range(n_i // group):
                lines = dot_tn_exact(g_in[a, ig], kern_t[...])
                for j in range(group):
                    grad_out[a * n_i + ig * group + j] = lines[j * dz:(j + 1) * dz]

        @pl.loop(1, n_xline + 1)
        def _(r):
            d = lax.rem(xl + r, n_xline)

            @pl.when(jnp.logical_or(d != xl, origin != core))
            def _():
                slab_copy(d).wait_send()

    for idx in range(5):
        field[idx, pl.ds(0, 4)] = jnp.zeros((4,) + field.shape[2:], jnp.float32)
        field[idx, pl.ds(n_i + 4, 4)] = jnp.zeros((4,) + field.shape[2:], jnp.float32)
        field[idx, inner_i, pl.ds(0, 8)] = jnp.zeros((n_i, 8, depth), jnp.float32)
        field[idx, inner_i, pl.ds(8 + n_x, 8)] = jnp.zeros((n_i, 8, depth), jnp.float32)
    for way in (LEFT, RIGHT, UP, DOWN):
        @pl.when(jnp.logical_not(has[way]))
        def _():
            halo = x_in if way < UP else i_in
            halo[:, way % 2] = jnp.zeros(halo.shape[:1] + halo.shape[2:], jnp.float32)
    image[...] = jnp.zeros(image.shape, jnp.float32)
    accel[steps] = jnp.zeros(accel.shape[1:], jnp.float32)

    n_counts = rec_counts.shape[1]
    spread = (
        div(lax.broadcasted_iota(jnp.int32, (n_counts, slots), 1), CAP)
        == lax.broadcasted_iota(jnp.int32, (n_counts, slots), 0)
    ).astype(jnp.float32).astype(jnp.bfloat16)
    counts = jnp.broadcast_to(rec_counts[...].astype(jnp.float32), (8, n_counts)).astype(jnp.bfloat16)
    live = dot(counts, spread)
    place = mod(lax.broadcasted_iota(jnp.int32, (8, slots), 1), CAP).astype(jnp.float32)
    list_out[...] = jnp.where(place < live, jnp.broadcast_to(rec_cells[...], (8, slots)), -1)

    pl.semaphore_wait(barrier, n_group - 1)

    for n in (RHO, NOW):
        tile_start(n)
    for a in range(2):
        @pl.when(leaves(a))
        def _():
            list_copy(a).start()

    for n in (SPEED, BEFORE):
        tile_start(n)

    @pl.loop(1, n_group)
    def _(r):
        obs_copy(lax.rem(me + r, n_group), me).start()

    obs_in[me] = observed[...]

    @pl.when(stays)
    def _():
        list_in[y] = list_out[...]

    offset = lax.broadcasted_iota(jnp.int32, (depth, depth), 0) - lax.broadcasted_iota(jnp.int32, (depth, depth), 1)
    second = jnp.zeros((depth, depth), jnp.float32)
    first = jnp.zeros((depth, depth), jnp.float32)
    for k in range(1, 5):
        second = jnp.where((offset == k) | (offset == -k), SECOND_COEFFS[k] / SECOND_COEFFS[1], second)
        first = jnp.where(offset == k, FIRST_COEFFS[k - 1] / FIRST_COEFFS[0], first)
        first = jnp.where(offset == -k, -FIRST_COEFFS[k - 1] / FIRST_COEFFS[0], first)
    z_mat[:, pl.ds(0, depth)] = second.astype(jnp.bfloat16)
    z_mat[:, pl.ds(depth, depth)] = first.astype(jnp.bfloat16)

    full_x = tile_x * n_xline
    cells = src_cell[...]
    src_i = div(cells, full_x * depth) - q * n_i
    src_x = mod(div(cells, depth), full_x) - plane * n_x
    inside = (src_i >= 0) & (src_i < n_i) & (src_x >= 0) & (src_x < n_x)
    src_row = jnp.where(inside, src_i * n_x + src_x, -1)
    n_src = cells.shape[1]
    src_rows = (lax.broadcasted_iota(jnp.int32, (rows, n_src), 0) == src_row).astype(jnp.float32)
    src_cols = (lax.broadcasted_iota(jnp.int32, (depth, n_src), 0) == mod(cells, depth)).astype(jnp.float32).astype(jnp.bfloat16)

    if fused:
        far = (
            lax.broadcasted_iota(jnp.int32, (full_x, full_x), 0) - lax.broadcasted_iota(jnp.int32, (full_x, full_x), 1)
        ).astype(jnp.float32)
        weights = jnp.exp(-jnp.abs(far) / SMOOTH)
        kern_t[...] = weights / jnp.sum(weights, axis=0, keepdims=True)

    def flat(idx):
        return field[idx, inner_i, inner_x, :].reshape(rows, depth)

    def along_depth(idx):
        high, low = split_bf16(flat(idx))
        both = dot(high, z_mat[...]) + dot(low, z_mat[...])
        return both[:, :depth], both[:, depth:]

    def across(idx, i):
        lap = slope_i = slope_x = None
        for k in range(1, 5):
            plus_i = field[idx, i + 4 + k, inner_x, :]
            minus_i = field[idx, i + 4 - k, inner_x, :]
            plus_x = field[idx, i + 4, pl.ds(8 + k, n_x), :]
            minus_x = field[idx, i + 4, pl.ds(8 - k, n_x), :]
            terms = (
                SECOND_COEFFS[k] * ((plus_i + minus_i) + (plus_x + minus_x)),
                FIRST_COEFFS[k - 1] * (plus_i - minus_i),
                FIRST_COEFFS[k - 1] * (plus_x - minus_x),
            )
            if lap is None:
                lap, slope_i, slope_x = terms
            else:
                lap, slope_i, slope_x = lap + terms[0], slope_i + terms[1], slope_x + terms[2]
        return lap, slope_i, slope_x

    tile_finish(RHO)
    for part in range(2):
        stage(DENSITY, part)
        send(DENSITY, part)
    tile_finish(NOW)
    for part in range(2):
        stage(0, part)
        send(0, part)

    slopes[2] = (FIRST_COEFFS[0] * FIRST_COEFFS[0] * along_depth(DENSITY)[1]).reshape(n_i, n_x, depth)

    for from_y in range(2):
        @pl.when(arrives(from_y))
        def _():
            list_arrival(from_y).wait_recv()
    for a in range(2):
        @pl.when(leaves(a))
        def _():
            list_copy(a).wait_send()
    for from_y in range(2):
        spot = list_in[from_y][:1]
        cell_i = div(spot, tile_x * depth) - cp * n_i
        cell_x = mod(div(spot, depth), tile_x) + from_y * tile_x
        row = jnp.where((spot >= 0) & (cell_i >= 0) & (cell_i < n_i), cell_i * n_x + cell_x, -1)
        columns = pl.ds(from_y * slots, slots)
        row_map[:, columns] = (lax.broadcasted_iota(jnp.int32, (rows, slots), 0) == row).astype(jnp.float32)
        zmap_t[:, columns] = (
            lax.broadcasted_iota(jnp.int32, (depth, slots), 0) == mod(spot, depth)
        ).astype(jnp.float32).astype(jnp.bfloat16)

    finish(DENSITY, 0)
    finish(DENSITY, 1)
    field[DENSITY, pl.ds(0, 4), inner_x, :] = i_in[DENSITY, 0]
    field[DENSITY, pl.ds(n_i + 4, 4), inner_x, :] = i_in[DENSITY, 1]
    field[DENSITY, inner_i, pl.ds(4, 4), :] = x_in[DENSITY, 0]
    field[DENSITY, inner_i, pl.ds(8 + n_x, 4), :] = x_in[DENSITY, 1]

    @pl.loop(0, n_i)
    def _(i):
        _, slope_i, slope_x = across(DENSITY, i)
        slopes[0, i] = slope_i
        slopes[1, i] = slope_x

    tile_finish(SPEED)
    speed_sq[...] = vel[...] * vel[...]
    column = lax.broadcasted_iota(jnp.int32, (n_x, depth), 0)

    @pl.loop(0, n_i)
    def _(i):
        for k in range(1, 5):
            weight = jnp.where(
                column < k, SECOND_COEFFS[k] + FIRST_COEFFS[k - 1] * slopes[1, i],
                jnp.where(column >= n_x - k, SECOND_COEFFS[k] - FIRST_COEFFS[k - 1] * slopes[1, i], 0.0),
            )
            wx[k - 1, i] = speed_sq[i] * weight

    tile_finish(BEFORE)

    def prepare(idx, term):
        lap, slope = along_depth(idx)
        partial = term + speed_sq[...].reshape(rows, depth) * (
            SECOND_COEFFS[1] * lap - slopes[2].reshape(rows, depth) * slope
        )
        base[...] = partial.reshape(n_i, n_x, depth)

    def interior(now, other, i):
        lap, slope_i, slope_x = across(now, i)
        center = field[now, i + 4, inner_x, :]
        change = base[i] + speed_sq[i] * (
            3.0 * SECOND_COEFFS[0] * center + lap - slopes[0, i] * slope_i - slopes[1, i] * slope_x
        )
        field[other, i + 4, inner_x, :] = 2.0 * center - field[other, i + 4, inner_x, :] + change
        return center, change

    def correction(now, i):
        beside = jnp.concatenate([x_in[now, 1, i], x_in[now, 0, i]], axis=0)
        total = None
        for k in range(1, 5):
            pieces = [pltpu.roll(beside, k, axis=0)]
            if n_x > 16:
                pieces.append(jnp.zeros((n_x - 16, depth), jnp.float32))
            pieces.append(pltpu.roll(beside, 8 - k, axis=0))
            term = wx[k - 1, i] * jnp.concatenate(pieces, axis=0)
            total = term if total is None else total + term
        if i < 4 or i >= n_i - 4:
            lap = None
            for h in range(4):
                k = i + 4 - h if i < 4 else n_i + h - i
                if k > 4:
                    continue
                sign = 1.0 if i < 4 else -1.0
                halo = i_in[now, 0 if i < 4 else 1, h]
                terms = SECOND_COEFFS[k] * halo, (sign * FIRST_COEFFS[k - 1]) * halo
                lap, slope = terms if lap is None else (lap + terms[0], slope + terms[1])
            total = total + speed_sq[i] * (lap + slopes[0, i] * slope)
        return total

    def correct(now, other, part, t):
        for i in range(part * middle, (part + 1) * middle):
            change = correction(now, i)
            fresh = field[other, i + 4, inner_x, :] + change
            field[other, i + 4, inner_x, :] = fresh
            x_out[other, 0, i] = fresh[:4]
            x_out[other, 1, i] = fresh[n_x - 4:]
            if t is not None:
                accel[t, i] += change

    def sample(idx, t):
        high, low = split_bf16(flat(idx))
        picked = dot(high, zmap_t[...]) + dot(low, zmap_t[...])
        predicted = jnp.sum(picked * row_map[...], axis=0, keepdims=True)
        residual_ref[t] = predicted - traces[pl.ds(t, 1), :]

    @pl.loop(0, steps)
    def _(t):
        now = lax.rem(t, 2)
        other = 1 - now
        high, low = split_bf16(src_rows * wavelet[pl.ds(t, 1), :])
        prepare(now, dot_nt(high, src_cols) + dot_nt(low, src_cols))

        @pl.loop(0, n_i)
        def _(i):
            _, change = interior(now, other, i)
            accel[t, i] = change

        @pl.when(t == 1)
        def _():
            tile_start(ADJ_NOW)

            @pl.loop(1, n_group)
            def _(r):
                peer = lax.rem(me + r, n_group)
                obs_copy(peer, peer).wait_recv()
                obs_copy(peer, me).wait_send()

            lane = div(lax.broadcasted_iota(jnp.int32, (8, slots), 1), CAP)
            for from_y in range(2):
                owner = (2 * plane + from_y) * 2 + origin

                def place_one(s, total):
                    moved = pltpu.roll(obs_in[s], lax.rem(s - owner + n_group, n_group) * CAP, axis=1)
                    return jnp.where(lane == s, moved, total)

                traces[:, pl.ds(from_y * slots, slots)] = lax.fori_loop(
                    0, n_group, place_one, jnp.zeros((8, slots), jnp.float32)
                )

        @pl.when(t == 3)
        def _():
            tile_start(ADJ_BEFORE)

        @pl.when(t >= 1)
        def _():
            sample(now, t - 1)

        @pl.when(t == steps - 1)
        def _():
            tile_finish(ADJ_NOW)
            for part in range(2):
                stage(2, part)
                send(2, part)

        for part in range(2):
            finish(now, part)
            correct(now, other, part, t)

            @pl.when(t < steps - 1)
            def _():
                send(other, part)

    sample(steps % 2, steps - 1)
    tile_finish(ADJ_BEFORE)

    @pl.loop(0, steps)
    def _(j):
        now = 2 + lax.rem(j, 2)
        other = 5 - now
        t = steps - 1 - j
        high, low = split_bf16(row_map[...] * residual_ref[t])
        prepare(now, dot_nt(high, zmap_t[...]) + dot_nt(low, zmap_t[...]))

        @pl.loop(0, n_i)
        def _(i):
            center, _ = interior(now, other, i)
            image[i] += center * accel[t + 1, i]

        @pl.when(j == steps - 1)
        def _():
            home_start(0)

        for part in range(2):
            finish(now, part)
            correct(now, other, part, None)

            @pl.when(j < steps - 1)
            def _():
                send(other, part)

    @pl.loop(0, n_i)
    def _(i):
        total = image[i] + field[final_idx[1], i + 4, inner_x, :] * accel[0, i]
        image[i] = total * (2.0 / steps) / vel[i]

    if fused:
        fused_gradient()
    else:
        grad_out[...] = image[...]
        home_start(1)
    home_finish(0)
    home_finish(1)


def per_device(
    fwd_now, fwd_before, adj_now, adj_before, velocity, log_density,
    observed, rec_cells, rec_counts, src_cell, wavelet,
):
    tile_i, tile_x, depth = fwd_now.shape
    steps = wavelet.shape[0]
    n_xline = lax.axis_size("xline")
    full_x = tile_x * n_xline
    n_i, n_x = tile_i // 2, tile_x * 2
    rows = n_i * n_x
    slots = rec_cells.shape[1]
    n_group = 2 * n_xline
    dz = depth // n_xline
    fused = dz >= 8 and 128 % dz == 0 and depth % 128 == 0 and n_i % (128 // dz) == 0
    group = 128 // dz if fused else 1

    block = (n_i, n_x, depth)
    vmem = pl.BlockSpec(memory_space=pltpu.VMEM)
    anywhere = pl.BlockSpec(memory_space=pl.ANY)
    dma = pltpu.SemaphoreType.DMA
    kernel = functools.partial(wave_kernel, (tile_i, tile_x, n_i, n_x, depth, steps, n_xline, fused))
    grad_shape = (tile_i, dz, full_x) if fused else block
    if fused:
        g_shapes = (n_xline, n_i // group, n_x, 128), (2, n_i // group, full_x, 128), (full_x, full_x)
    else:
        g_shapes = ((8, 128),) * 3
    raw, last, previous = pl.pallas_call(
        kernel,
        out_shape=[
            jax.ShapeDtypeStruct(grad_shape, jnp.float32),
            jax.ShapeDtypeStruct(fwd_now.shape, jnp.float32),
            jax.ShapeDtypeStruct(fwd_now.shape, jnp.float32),
        ],
        in_specs=[anywhere] * 6 + [vmem] * 5,
        out_specs=[vmem, anywhere, anywhere],
        scratch_shapes=[
            pltpu.VMEM((5, n_i + 8, n_x + 16, depth), jnp.float32),
            pltpu.VMEM(block, jnp.float32),
            pltpu.VMEM((5, 2, n_i, 4, depth), jnp.float32),
            pltpu.VMEM((5, 2, n_i, 4, depth), jnp.float32),
            pltpu.VMEM((5, 2, 4, n_x, depth), jnp.float32),
            pltpu.VMEM((steps + 1,) + block, jnp.float32),
            pltpu.VMEM(block, jnp.float32),
            pltpu.VMEM(block, jnp.float32),
            pltpu.VMEM((3,) + block, jnp.float32),
            pltpu.VMEM(block, jnp.float32),
            pltpu.VMEM((4,) + block, jnp.float32),
            pltpu.VMEM((rows, 2 * slots), jnp.float32),
            pltpu.VMEM((depth, 2 * slots), jnp.bfloat16),
            pltpu.VMEM((depth, 2 * depth), jnp.bfloat16),
            pltpu.VMEM((steps, 1, 2 * slots), jnp.float32),
            pltpu.VMEM((steps, 2 * slots), jnp.float32),
            pltpu.VMEM((8, slots), jnp.int32),
            pltpu.VMEM((2, 8, slots), jnp.int32),
            pltpu.VMEM((n_group,) + observed.shape, jnp.float32),
            pltpu.VMEM(g_shapes[0], jnp.float32),
            pltpu.VMEM(g_shapes[1], jnp.float32),
            pltpu.VMEM(g_shapes[2], jnp.float32),
            dma((5, 6)), dma((5, 6)),
            dma((6, 2)), dma((6, 2)), dma((6,)),
            dma((2,)), dma((2,)),
            dma((n_group,)), dma((n_group,)),
            dma((2, 2)), dma((2, 2)), dma((2,)),
            dma((n_xline,)), dma((2, n_xline // 2)),
        ],
        compiler_params=pltpu.CompilerParams(
            collective_id=0, has_side_effects=True, vmem_limit_bytes=56 * 1024 * 1024
        ),
    )(
        log_density, fwd_now, velocity, fwd_before, adj_now, adj_before,
        observed, rec_cells, rec_counts, src_cell[None, :], wavelet,
    )
    if fused:
        return raw.transpose(1, 0, 2), last, previous

    places = []
    for xl in range(n_xline):
        for core in range(2):
            y, plane = xl % 2, xl // 2
            cp = (core + plane % 2) % 2
            origin = (y + cp) % 2
            places.append((xl * 2 + core, (2 * plane + cp) * 2 + origin))
    raw = lax.ppermute(raw, ("xline", "inline"), places)
    columns = lax.all_to_all(
        raw.reshape(n_i, n_x, n_xline, dz).transpose(2, 0, 1, 3),
        "xline", split_axis=0, concat_axis=0, tiled=True,
    ).reshape(n_xline // 2, 2, n_i, n_x, dz)
    positions = jnp.arange(full_x).astype(jnp.float32)
    weights = jnp.exp(-jnp.abs(positions[:, None] - positions[None, :]) / SMOOTH)
    weights = weights / jnp.sum(weights, axis=1, keepdims=True)
    gradient = jnp.einsum(
        "phixz,ypx->zhiy", columns, weights.reshape(full_x, n_xline // 2, n_x),
        precision=lax.Precision.HIGHEST,
    ).reshape(dz, tile_i, full_x)
    return gradient, last, previous


def solution(mesh):
    return jax.shard_map(
        per_device,
        mesh=mesh,
        in_specs=(
            P(("shots", "inline"), "xline", None),
            P(("shots", "inline"), "xline", None),
            P(("shots", "inline"), "xline", None),
            P(("shots", "inline"), "xline", None),
            P("inline", "xline", None),
            P("inline", "xline", None),
            P("shots", ("xline", "inline")),
            P(("xline", "inline"), None),
            P(("xline", "inline"), None),
            P("shots"),
            P("shots", None),
        ),
        out_specs=(
            P(("shots", "xline"), "inline", None),
            P(("shots", "inline"), "xline", None),
            P(("shots", "inline"), "xline", None),
        ),
        check_vma=False,
    )
```

```python
import functools

import jax
import jax.numpy as jnp
from jax import lax
from jax.experimental import pallas as pl
from jax.experimental.pallas import tpu as pltpu
from jax.sharding import PartitionSpec as P

CAP = 8
SMOOTH = 16
MESH = pl.DeviceIdType.MESH

SECOND_COEFFS = (-205.0 / 72.0, 8.0 / 5.0, -1.0 / 5.0, 8.0 / 315.0, -1.0 / 560.0)
FIRST_COEFFS = (4.0 / 5.0, -1.0 / 5.0, 4.0 / 105.0, -1.0 / 280.0)
LEFT, RIGHT, UP, DOWN = 0, 1, 2, 3
DENSITY = 4
RHO, NOW, SPEED, BEFORE, ADJ_NOW, ADJ_BEFORE = range(6)


def split_bf16(value):
    high = value.astype(jnp.bfloat16)
    low = (value - high.astype(jnp.float32)).astype(jnp.bfloat16)
    return high, low


def dot(a, b):
    return jnp.dot(a, b, preferred_element_type=jnp.float32)


def dot_nt(a, b):
    return lax.dot_general(a, b, (((1,), (1,)), ((), ())), preferred_element_type=jnp.float32)


def dot_tn_exact(a, b):
    dims = (((0,), (0,)), ((), ()))
    ah, al = split_bf16(a)
    bh, bl = split_bf16(b)
    one = lax.dot_general(ah, bh, dims, preferred_element_type=jnp.float32)
    two = lax.dot_general(al, bh, dims, preferred_element_type=jnp.float32)
    three = lax.dot_general(ah, bl, dims, preferred_element_type=jnp.float32)
    return one + (two + three)


def div(value, n):
    return lax.shift_right_arithmetic(value, jnp.full_like(value, n.bit_length() - 1))


def mod(value, n):
    return value & (n - 1)


def wave_kernel(
    sizes,
    log_density, fwd_now, velocity, fwd_before, adj_now, adj_before,
    observed, rec_cells, rec_counts, src_cell, wavelet,
    grad_out, last_out, previous_out,
    field, vel, x_in, x_out, i_in, accel, base, image, slopes, speed_sq, wx,
    row_map, zmap_t, z_mat, residual_ref, traces, list_out, list_in, obs_in, g_send, g_in, kern_t,
    send_sem, recv_sem, rt_send, rt_recv, rt_local, list_send, list_recv, obs_send, obs_recv,
    ret_send, ret_recv, ret_local, g_ssem, g_rsem,
):
    tile_i, tile_x, n_i, n_x, depth, steps, n_xline, fused = sizes
    rows = n_i * n_x
    slots = rec_cells.shape[1]
    n_group = 2 * n_xline
    xl = lax.axis_index("xline")
    core = lax.axis_index("inline")
    me = xl * 2 + core
    y = lax.rem(xl, 2)
    plane = xl // 2
    z_odd = lax.rem(plane, 2)
    mate = xl + 1 - 2 * y
    cp = lax.rem(core + z_odd, 2)
    origin = y
    q = 2 * y + cp
    stays = y == core
    has = (xl >= 2, xl < n_xline - 2, q > 0, q < 3)
    other_core = 1 - core
    target = (
        {"xline": xl - 2, "inline": other_core},
        {"xline": xl + 2, "inline": other_core},
        {"xline": jnp.where(q == 2, mate, xl), "inline": other_core},
        {"xline": jnp.where(q == 1, mate, xl), "inline": other_core},
    )
    inner_i = pl.ds(4, n_i)
    inner_x = pl.ds(8, n_x)
    middle = n_i // 2

    barrier = pltpu.get_barrier_semaphore()

    @pl.loop(1, n_group)
    def _(r):
        peer = lax.rem(me + r, n_group)
        pl.semaphore_signal(
            barrier, inc=1, device_id={"xline": peer // 2, "inline": lax.rem(peer, 2)}, device_id_type=MESH
        )

    def beside(idx, way, part):
        part_rows = pl.ds(part * middle, middle)
        sem = way + 4 * part
        return pltpu.make_async_remote_copy(
            src_ref=x_out.at[idx, way, part_rows], dst_ref=x_in.at[idx, 1 - way, part_rows],
            send_sem=send_sem.at[idx, sem], recv_sem=recv_sem.at[idx, sem],
            device_id=target[way], device_id_type=MESH,
        )

    def above(idx, part, side):
        up = part == 0
        return pltpu.make_async_remote_copy(
            src_ref=field.at[idx, pl.ds(4 + part * (n_i - 4), 4), inner_x, :],
            dst_ref=i_in.at[idx, part if side else 1 - part],
            send_sem=send_sem.at[idx, 2 + part], recv_sem=recv_sem.at[idx, 3 - part if side else 2 + part],
            device_id={
                "xline": jnp.where(up, target[UP]["xline"], target[DOWN]["xline"]), "inline": other_core
            },
            device_id_type=MESH,
        )

    def has_row(part):
        return jnp.where(part == 0, q, 3 - q) > 0

    def send(idx, part):
        for way in (LEFT, RIGHT):
            @pl.when(has[way])
            def _():
                beside(idx, way, part).start()

        @pl.when(has_row(part))
        def _():
            above(idx, part, False).start()

    def stage(idx, part):
        part_rows = pl.ds(part * middle, middle)
        field_rows = pl.ds(4 + part * middle, middle)
        x_out[idx, 0, part_rows] = field[idx, field_rows, pl.ds(8, 4), :]
        x_out[idx, 1, part_rows] = field[idx, field_rows, pl.ds(4 + n_x, 4), :]

    def finish(idx, part):
        for way in (LEFT, RIGHT):
            @pl.when(has[way])
            def _():
                beside(idx, way, part).wait_send()
                beside(idx, 1 - way, part).wait_recv()

        @pl.when(has_row(part))
        def _():
            above(idx, part, False).wait_send()
            above(idx, part, True).wait_recv()

    halves = (1 - y, y)

    sources = (log_density, fwd_now, velocity, fwd_before, adj_now, adj_before)
    places = (DENSITY, 0, None, 1, 2, 3)

    def landing(n, from_y):
        columns = pl.multiple_of(from_y * tile_x, tile_x)
        if n == SPEED:
            return vel.at[:, pl.ds(columns, tile_x), :]
        return field.at[places[n], inner_i, pl.ds(pl.multiple_of(8 + columns, 8), tile_x), :]

    def tile_copy(n, a):
        return pltpu.make_async_remote_copy(
            src_ref=sources[n].at[pl.ds(a * n_i, n_i)], dst_ref=landing(n, y),
            send_sem=rt_send.at[n, a], recv_sem=rt_recv.at[n, y],
            device_id={"xline": 2 * plane + core, "inline": lax.rem(a + z_odd, 2)},
            device_id_type=MESH,
        )

    def tile_arrival(n, from_y):
        return pltpu.make_async_remote_copy(
            src_ref=sources[n].at[pl.ds(0, n_i)], dst_ref=landing(n, from_y),
            send_sem=rt_send.at[n, 0], recv_sem=rt_recv.at[n, from_y],
            device_id={"xline": mate}, device_id_type=MESH,
        )

    def own_copy(n):
        return pltpu.make_async_copy(
            sources[n].at[pl.ds(cp * n_i, n_i)], landing(n, y), rt_local.at[n]
        )

    def leaves(a):
        return jnp.logical_not(jnp.logical_and(stays, cp == a))

    def arrives(from_y):
        return jnp.logical_not(jnp.logical_and(stays, y == from_y))

    def tile_start(n):
        for a in range(2):
            @pl.when(leaves(a))
            def _():
                tile_copy(n, a).start()

        @pl.when(stays)
        def _():
            own_copy(n).start()

    def tile_finish(n):
        for from_y in range(2):
            @pl.when(arrives(from_y))
            def _():
                tile_arrival(n, from_y).wait_recv()
        for a in range(2):
            @pl.when(leaves(a))
            def _():
                tile_copy(n, a).wait_send()

        @pl.when(stays)
        def _():
            own_copy(n).wait()

    def list_copy(a):
        return pltpu.make_async_remote_copy(
            src_ref=list_out, dst_ref=list_in.at[y],
            send_sem=list_send.at[a], recv_sem=list_recv.at[y],
            device_id={"xline": 2 * plane + core, "inline": lax.rem(a + z_odd, 2)},
            device_id_type=MESH,
        )

    def list_arrival(from_y):
        return pltpu.make_async_remote_copy(
            src_ref=list_out, dst_ref=list_in.at[from_y],
            send_sem=list_send.at[0], recv_sem=list_recv.at[from_y],
            device_id={"xline": mate}, device_id_type=MESH,
        )

    def obs_copy(peer, slot):
        return pltpu.make_async_remote_copy(
            src_ref=observed, dst_ref=obs_in.at[slot],
            send_sem=obs_send.at[peer], recv_sem=obs_recv.at[slot],
            device_id={"xline": peer // 2, "inline": lax.rem(peer, 2)}, device_id_type=MESH,
        )

    finals = (previous_out, last_out)
    final_idx = (2 + (steps - 1) % 2, 2 + steps % 2)

    def home_copy(n, to_y):
        return pltpu.make_async_remote_copy(
            src_ref=field.at[final_idx[n], inner_i, pl.ds(8 + to_y * tile_x, tile_x), :],
            dst_ref=finals[n].at[pl.ds(cp * n_i, n_i)],
            send_sem=ret_send.at[n, to_y], recv_sem=ret_recv.at[n, cp],
            device_id={"xline": 2 * plane + to_y, "inline": origin}, device_id_type=MESH,
        )

    def home_arrival(n, a):
        return pltpu.make_async_remote_copy(
            src_ref=field.at[final_idx[n], inner_i, pl.ds(8, tile_x), :],
            dst_ref=finals[n].at[pl.ds(a * n_i, n_i)],
            send_sem=ret_send.at[n, 0], recv_sem=ret_recv.at[n, a],
            device_id={"xline": mate}, device_id_type=MESH,
        )

    def home_own(n):
        columns = pl.multiple_of(8 + y * tile_x, 8)
        return pltpu.make_async_copy(
            field.at[final_idx[n], inner_i, pl.ds(columns, tile_x), :],
            finals[n].at[pl.ds(cp * n_i, n_i)], ret_local.at[n],
        )

    def home_start(n):
        for to_y in range(2):
            @pl.when(arrives(to_y))
            def _():
                home_copy(n, to_y).start()

        @pl.when(stays)
        def _():
            home_own(n).start()

    def home_finish(n):
        for to_y in range(2):
            @pl.when(arrives(to_y))
            def _():
                home_copy(n, to_y).wait_send()
        for a in range(2):
            @pl.when(leaves(a))
            def _():
                home_arrival(n, a).wait_recv()

        @pl.when(stays)
        def _():
            home_own(n).wait()

    dz = depth // n_xline
    planes_n = n_xline // 2

    def slab_copy(d):
        return pltpu.make_async_remote_copy(
            src_ref=g_send.at[d],
            dst_ref=g_in.at[cp, :, pl.ds(pl.multiple_of(plane * n_x, 8), n_x), :],
            send_sem=g_ssem.at[d], recv_sem=g_rsem.at[cp, plane],
            device_id={"xline": d, "inline": origin}, device_id_type=MESH,
        )

    def slab_arrival(a, p):
        return pltpu.make_async_remote_copy(
            src_ref=g_send.at[0],
            dst_ref=g_in.at[a, :, pl.ds(pl.multiple_of(p * n_x, 8), n_x), :],
            send_sem=g_ssem.at[0], recv_sem=g_rsem.at[a, p],
            device_id={"xline": mate}, device_id_type=MESH,
        )

    def fused_gradient():
        group = 128 // dz
        lane = div(lax.broadcasted_iota(jnp.int32, (n_x, 128), 1), dz)
        for chunk in range(depth // 128):
            for ig in range(n_i // group):
                planes = [image[ig * group + j, :, pl.ds(chunk * 128, 128)] for j in range(group)]
                for dd in range(group):
                    out = None
                    for j in range(group):
                        shift = (j - dd) * dz % 128
                        moved = pltpu.roll(planes[j], shift, axis=1) if shift else planes[j]
                        out = moved if out is None else jnp.where(lane == j, moved, out)
                    g_send[chunk * group + dd, ig] = out

        @pl.loop(1, n_xline + 1)
        def _(r):
            d = lax.rem(xl + r, n_xline)

            @pl.when(jnp.logical_or(d != xl, origin != core))
            def _():
                slab_copy(d).start()

        home_start(1)

        @pl.when(origin == core)
        def _():
            g_in[cp, :, pl.ds(pl.multiple_of(plane * n_x, 8), n_x), :] = g_send[xl]

        @pl.loop(0, n_xline)
        def _(r):
            a, p = lax.rem(r, 2), r // 2
            mine = jnp.logical_and(origin == core, jnp.logical_and(a == cp, p == plane))

            @pl.when(jnp.logical_not(mine))
            def _():
                slab_arrival(a, p).wait_recv()

        for a in range(2):
            for ig in range(n_i // group):
                lines = dot_tn_exact(g_in[a, ig], kern_t[...])
                for j in range(group):
                    grad_out[:, a * n_i + ig * group + j, :] = lines[j * dz:(j + 1) * dz]

        @pl.loop(1, n_xline + 1)
        def _(r):
            d = lax.rem(xl + r, n_xline)

            @pl.when(jnp.logical_or(d != xl, origin != core))
            def _():
                slab_copy(d).wait_send()

    for idx in range(5):
        field[idx, pl.ds(0, 4)] = jnp.zeros((4,) + field.shape[2:], jnp.float32)
        field[idx, pl.ds(n_i + 4, 4)] = jnp.zeros((4,) + field.shape[2:], jnp.float32)
        field[idx, inner_i, pl.ds(0, 8)] = jnp.zeros((n_i, 8, depth), jnp.float32)
        field[idx, inner_i, pl.ds(8 + n_x, 8)] = jnp.zeros((n_i, 8, depth), jnp.float32)
    for way in (LEFT, RIGHT, UP, DOWN):
        @pl.when(jnp.logical_not(has[way]))
        def _():
            halo = x_in if way < UP else i_in
            halo[:, way % 2] = jnp.zeros(halo.shape[:1] + halo.shape[2:], jnp.float32)
    image[...] = jnp.zeros(image.shape, jnp.float32)
    accel[steps] = jnp.zeros(accel.shape[1:], jnp.float32)

    n_counts = rec_counts.shape[1]
    spread = (
        div(lax.broadcasted_iota(jnp.int32, (n_counts, slots), 1), CAP)
        == lax.broadcasted_iota(jnp.int32, (n_counts, slots), 0)
    ).astype(jnp.float32).astype(jnp.bfloat16)
    counts = jnp.broadcast_to(rec_counts[...].astype(jnp.float32), (8, n_counts)).astype(jnp.bfloat16)
    live = dot(counts, spread)
    place = mod(lax.broadcasted_iota(jnp.int32, (8, slots), 1), CAP).astype(jnp.float32)
    list_out[...] = jnp.where(place < live, jnp.broadcast_to(rec_cells[...], (8, slots)), -1)

    pl.semaphore_wait(barrier, n_group - 1)

    for a in range(2):
        @pl.when(leaves(a))
        def _():
            list_copy(a).start()

    for n in (RHO, NOW):
        tile_start(n)
    for n in (SPEED, BEFORE):
        tile_start(n)

    @pl.loop(1, n_group)
    def _(r):
        obs_copy(lax.rem(me + r, n_group), me).start()

    obs_in[me] = observed[...]

    @pl.when(stays)
    def _():
        list_in[y] = list_out[...]

    offset = lax.broadcasted_iota(jnp.int32, (depth, depth), 0) - lax.broadcasted_iota(jnp.int32, (depth, depth), 1)
    second = jnp.zeros((depth, depth), jnp.float32)
    first = jnp.zeros((depth, depth), jnp.float32)
    for k in range(1, 5):
        second = jnp.where((offset == k) | (offset == -k), SECOND_COEFFS[k] / SECOND_COEFFS[1], second)
        first = jnp.where(offset == k, FIRST_COEFFS[k - 1] / FIRST_COEFFS[0], first)
        first = jnp.where(offset == -k, -FIRST_COEFFS[k - 1] / FIRST_COEFFS[0], first)
    z_mat[:, pl.ds(0, depth)] = second.astype(jnp.bfloat16)
    z_mat[:, pl.ds(depth, depth)] = first.astype(jnp.bfloat16)

    full_x = tile_x * n_xline
    cells = src_cell[...]
    src_i = div(cells, full_x * depth) - q * n_i
    src_x = mod(div(cells, depth), full_x) - plane * n_x
    inside = (src_i >= 0) & (src_i < n_i) & (src_x >= 0) & (src_x < n_x)
    src_row = jnp.where(inside, src_i * n_x + src_x, -1)
    n_src = cells.shape[1]
    src_rows = (lax.broadcasted_iota(jnp.int32, (rows, n_src), 0) == src_row).astype(jnp.float32)
    src_cols = (lax.broadcasted_iota(jnp.int32, (depth, n_src), 0) == mod(cells, depth)).astype(jnp.float32).astype(jnp.bfloat16)

    if fused:
        far = (
            lax.broadcasted_iota(jnp.int32, (full_x, full_x), 0) - lax.broadcasted_iota(jnp.int32, (full_x, full_x), 1)
        ).astype(jnp.float32)
        weights = jnp.exp(-jnp.abs(far) / SMOOTH)
        kern_t[...] = weights / jnp.sum(weights, axis=0, keepdims=True)

    def flat(idx):
        return field[idx, inner_i, inner_x, :].reshape(rows, depth)

    def along_depth(idx):
        high, low = split_bf16(flat(idx))
        both = dot(high, z_mat[...]) + dot(low, z_mat[...])
        return both[:, :depth], both[:, depth:]

    def across(idx, i):
        lap = slope_i = slope_x = None
        for k in range(1, 5):
            plus_i = field[idx, i + 4 + k, inner_x, :]
            minus_i = field[idx, i + 4 - k, inner_x, :]
            plus_x = field[idx, i + 4, pl.ds(8 + k, n_x), :]
            minus_x = field[idx, i + 4, pl.ds(8 - k, n_x), :]
            terms = (
                SECOND_COEFFS[k] * ((plus_i + minus_i) + (plus_x + minus_x)),
                FIRST_COEFFS[k - 1] * (plus_i - minus_i),
                FIRST_COEFFS[k - 1] * (plus_x - minus_x),
            )
            if lap is None:
                lap, slope_i, slope_x = terms
            else:
                lap, slope_i, slope_x = lap + terms[0], slope_i + terms[1], slope_x + terms[2]
        return lap, slope_i, slope_x

    tile_finish(RHO)
    for part in halves:
        stage(DENSITY, part)
        send(DENSITY, part)
    tile_finish(NOW)
    for part in halves:
        stage(0, part)
        send(0, part)

    slopes[2] = (FIRST_COEFFS[0] * FIRST_COEFFS[0] * along_depth(DENSITY)[1]).reshape(n_i, n_x, depth)

    finish(DENSITY, 0)
    finish(DENSITY, 1)
    field[DENSITY, pl.ds(0, 4), inner_x, :] = i_in[DENSITY, 0]
    field[DENSITY, pl.ds(n_i + 4, 4), inner_x, :] = i_in[DENSITY, 1]
    field[DENSITY, inner_i, pl.ds(4, 4), :] = x_in[DENSITY, 0]
    field[DENSITY, inner_i, pl.ds(8 + n_x, 4), :] = x_in[DENSITY, 1]

    @pl.loop(0, n_i)
    def _(i):
        _, slope_i, slope_x = across(DENSITY, i)
        slopes[0, i] = slope_i
        slopes[1, i] = slope_x

    tile_finish(SPEED)
    speed_sq[...] = vel[...] * vel[...]
    column = lax.broadcasted_iota(jnp.int32, (n_x, depth), 0)

    @pl.loop(0, n_i)
    def _(i):
        for k in range(1, 5):
            weight = jnp.where(
                column < k, SECOND_COEFFS[k] + FIRST_COEFFS[k - 1] * slopes[1, i],
                jnp.where(column >= n_x - k, SECOND_COEFFS[k] - FIRST_COEFFS[k - 1] * slopes[1, i], 0.0),
            )
            wx[k - 1, i] = speed_sq[i] * weight

    tile_finish(BEFORE)

    def make_maps():
        for from_y in range(2):
            @pl.when(arrives(from_y))
            def _():
                list_arrival(from_y).wait_recv()
        for a in range(2):
            @pl.when(leaves(a))
            def _():
                list_copy(a).wait_send()
        for from_y in range(2):
            spot = list_in[from_y][:1]
            cell_i = div(spot, tile_x * depth) - cp * n_i
            cell_x = mod(div(spot, depth), tile_x) + from_y * tile_x
            row = jnp.where((spot >= 0) & (cell_i >= 0) & (cell_i < n_i), cell_i * n_x + cell_x, -1)
            columns = pl.ds(from_y * slots, slots)
            row_map[:, columns] = (lax.broadcasted_iota(jnp.int32, (rows, slots), 0) == row).astype(jnp.float32)
            zmap_t[:, columns] = (
                lax.broadcasted_iota(jnp.int32, (depth, slots), 0) == mod(spot, depth)
            ).astype(jnp.float32).astype(jnp.bfloat16)

    def make_traces():
        @pl.loop(1, n_group)
        def _(r):
            peer = lax.rem(me + r, n_group)
            obs_copy(peer, peer).wait_recv()
            obs_copy(peer, me).wait_send()

        lane = div(lax.broadcasted_iota(jnp.int32, (8, slots), 1), CAP)
        for from_y in range(2):
            owner = (2 * plane + from_y) * 2 + origin

            def place_one(s, total):
                moved = pltpu.roll(obs_in[s], lax.rem(s - owner + n_group, n_group) * CAP, axis=1)
                return jnp.where(lane == s, moved, total)

            traces[:, pl.ds(from_y * slots, slots)] = lax.fori_loop(
                0, n_group, place_one, jnp.zeros((8, slots), jnp.float32)
            )

    def prepare(idx, term):
        lap, slope = along_depth(idx)
        partial = term + speed_sq[...].reshape(rows, depth) * (
            SECOND_COEFFS[1] * lap - slopes[2].reshape(rows, depth) * slope
        )
        base[...] = partial.reshape(n_i, n_x, depth)

    def interior(now, other, i):
        lap, slope_i, slope_x = across(now, i)
        center = field[now, i + 4, inner_x, :]
        change = base[i] + speed_sq[i] * (
            3.0 * SECOND_COEFFS[0] * center + lap - slopes[0, i] * slope_i - slopes[1, i] * slope_x
        )
        field[other, i + 4, inner_x, :] = 2.0 * center - field[other, i + 4, inner_x, :] + change
        return center, change

    def correction(now, i):
        pair = jnp.concatenate([x_in[now, 1, i], x_in[now, 0, i]], axis=0)
        total = None
        for k in range(1, 5):
            pieces = [pltpu.roll(pair, k, axis=0)]
            if n_x > 16:
                pieces.append(jnp.zeros((n_x - 16, depth), jnp.float32))
            pieces.append(pltpu.roll(pair, 8 - k, axis=0))
            term = wx[k - 1, i] * jnp.concatenate(pieces, axis=0)
            total = term if total is None else total + term
        return total

    def correct(now, other, part, t):
        up = part == 0
        sign = jnp.where(up, 1.0, -1.0)
        for r in range(middle):
            i = jnp.where(up, r, n_i - 1 - r)
            change = correction(now, i)
            lap = None
            for h in range(4 - r):
                k = r + 1 + h
                halo = i_in[now, part, jnp.where(up, 3 - h, h)]
                terms = SECOND_COEFFS[k] * halo, FIRST_COEFFS[k - 1] * halo
                lap, slope = terms if lap is None else (lap + terms[0], slope + terms[1])
            if lap is not None:
                change = change + speed_sq[i] * (lap + (sign * slopes[0, i]) * slope)
            fresh = field[other, i + 4, inner_x, :] + change
            field[other, i + 4, inner_x, :] = fresh
            x_out[other, 0, i] = fresh[:4]
            x_out[other, 1, i] = fresh[n_x - 4:]
            if t is not None:
                accel[t, i] += change

    def sample(idx, t):
        high, low = split_bf16(flat(idx))
        picked = dot(high, zmap_t[...]) + dot(low, zmap_t[...])
        predicted = jnp.sum(picked * row_map[...], axis=0, keepdims=True)
        residual_ref[t] = predicted

    @pl.loop(0, steps)
    def _(t):
        now = lax.rem(t, 2)
        other = 1 - now
        high, low = split_bf16(src_rows * wavelet[pl.ds(t, 1), :])
        prepare(now, dot_nt(high, src_cols) + dot_nt(low, src_cols))

        @pl.loop(0, n_i)
        def _(i):
            _, change = interior(now, other, i)
            accel[t, i] = change

        @pl.when(t == 1)
        def _():
            tile_start(ADJ_NOW)
            make_maps()

        @pl.when(t == 4)
        def _():
            make_traces()

        @pl.when(t == 3)
        def _():
            tile_start(ADJ_BEFORE)

        @pl.when(t >= 1)
        def _():
            sample(now, t - 1)

        @pl.when(t == steps - 1)
        def _():
            tile_finish(ADJ_NOW)
            for part in halves:
                stage(2, part)
                send(2, part)

        for part in halves:
            finish(now, part)
            correct(now, other, part, t)

            @pl.when(t < steps - 1)
            def _():
                send(other, part)

    sample(steps % 2, steps - 1)
    tile_finish(ADJ_BEFORE)

    @pl.loop(0, steps)
    def _(j):
        now = 2 + lax.rem(j, 2)
        other = 5 - now
        t = steps - 1 - j
        high, low = split_bf16(row_map[...] * (residual_ref[t] - traces[pl.ds(t, 1), :]))
        prepare(now, dot_nt(high, zmap_t[...]) + dot_nt(low, zmap_t[...]))

        @pl.loop(0, n_i)
        def _(i):
            center, _ = interior(now, other, i)
            image[i] += center * accel[t + 1, i]

        @pl.when(j == steps - 1)
        def _():
            home_start(0)

        for part in halves:
            finish(now, part)
            correct(now, other, part, None)

            @pl.when(j < steps - 1)
            def _():
                send(other, part)

    @pl.loop(0, n_i)
    def _(i):
        total = image[i] + field[final_idx[1], i + 4, inner_x, :] * accel[0, i]
        image[i] = total * (2.0 / steps) / vel[i]

    if fused:
        fused_gradient()
    else:
        grad_out[...] = image[...]
        home_start(1)
    home_finish(0)
    home_finish(1)


def hand_over(*arrays):
    count = len(arrays)

    def kernel(*refs):
        copies = [
            pltpu.make_async_copy(refs[n], refs[count + n], refs[2 * count].at[n]) for n in range(count)
        ]
        for copy in copies:
            copy.start()
        for copy in copies:
            copy.wait()

    return pl.pallas_call(
        kernel,
        out_shape=[jax.ShapeDtypeStruct(array.shape, array.dtype) for array in arrays],
        in_specs=[pl.BlockSpec(memory_space=pltpu.VMEM)] * count,
        out_specs=[pl.BlockSpec(memory_space=pl.ANY)] * count,
        scratch_shapes=[pltpu.SemaphoreType.DMA((count,))],
    )(*arrays)


def per_device(
    fwd_now, fwd_before, adj_now, adj_before, velocity, log_density,
    observed, rec_cells, rec_counts, src_cell, wavelet,
):
    tile_i, tile_x, depth = fwd_now.shape
    steps = wavelet.shape[0]
    n_xline = lax.axis_size("xline")
    full_x = tile_x * n_xline
    n_i, n_x = tile_i // 2, tile_x * 2
    rows = n_i * n_x
    slots = rec_cells.shape[1]
    n_group = 2 * n_xline
    dz = depth // n_xline
    fused = dz >= 8 and 128 % dz == 0 and depth % 128 == 0 and n_i % (128 // dz) == 0
    group = 128 // dz if fused else 1

    block = (n_i, n_x, depth)
    vmem = pl.BlockSpec(memory_space=pltpu.VMEM)
    anywhere = pl.BlockSpec(memory_space=pl.ANY)
    dma = pltpu.SemaphoreType.DMA
    kernel = functools.partial(wave_kernel, (tile_i, tile_x, n_i, n_x, depth, steps, n_xline, fused))
    grad_shape = (dz, tile_i, full_x) if fused else block
    if fused:
        g_shapes = (n_xline, n_i // group, n_x, 128), (2, n_i // group, full_x, 128), (full_x, full_x)
    else:
        g_shapes = ((8, 128),) * 3
    raw, last, previous = pl.pallas_call(
        kernel,
        out_shape=[
            jax.ShapeDtypeStruct(grad_shape, jnp.float32),
            jax.ShapeDtypeStruct(fwd_now.shape, jnp.float32),
            jax.ShapeDtypeStruct(fwd_now.shape, jnp.float32),
        ],
        in_specs=[anywhere] * 6 + [vmem] * 5,
        out_specs=[vmem, anywhere, anywhere],
        scratch_shapes=[
            pltpu.VMEM((5, n_i + 8, n_x + 16, depth), jnp.float32),
            pltpu.VMEM(block, jnp.float32),
            pltpu.VMEM((5, 2, n_i, 4, depth), jnp.float32),
            pltpu.VMEM((5, 2, n_i, 4, depth), jnp.float32),
            pltpu.VMEM((5, 2, 4, n_x, depth), jnp.float32),
            pltpu.VMEM((steps + 1,) + block, jnp.float32),
            pltpu.VMEM(block, jnp.float32),
            pltpu.VMEM(block, jnp.float32),
            pltpu.VMEM((3,) + block, jnp.float32),
            pltpu.VMEM(block, jnp.float32),
            pltpu.VMEM((4,) + block, jnp.float32),
            pltpu.VMEM((rows, 2 * slots), jnp.float32),
            pltpu.VMEM((depth, 2 * slots), jnp.bfloat16),
            pltpu.VMEM((depth, 2 * depth), jnp.bfloat16),
            pltpu.VMEM((steps, 1, 2 * slots), jnp.float32),
            pltpu.VMEM((steps, 2 * slots), jnp.float32),
            pltpu.VMEM((8, slots), jnp.int32),
            pltpu.VMEM((2, 8, slots), jnp.int32),
            pltpu.VMEM((n_group,) + observed.shape, jnp.float32),
            pltpu.VMEM(g_shapes[0], jnp.float32),
            pltpu.VMEM(g_shapes[1], jnp.float32),
            pltpu.VMEM(g_shapes[2], jnp.float32),
            dma((5, 6)), dma((5, 6)),
            dma((6, 2)), dma((6, 2)), dma((6,)),
            dma((2,)), dma((2,)),
            dma((n_group,)), dma((n_group,)),
            dma((2, 2)), dma((2, 2)), dma((2,)),
            dma((n_xline,)), dma((2, n_xline // 2)),
        ],
        compiler_params=pltpu.CompilerParams(
            collective_id=0, has_side_effects=True, vmem_limit_bytes=56 * 1024 * 1024
        ),
    )(
        log_density, fwd_now, velocity, fwd_before, adj_now, adj_before,
        observed, rec_cells, rec_counts, src_cell[None, :], wavelet,
    )
    if fused:
        return hand_over(raw, last, previous)

    places = []
    for xl in range(n_xline):
        for core in range(2):
            y, plane = xl % 2, xl // 2
            cp = (core + plane % 2) % 2
            places.append((xl * 2 + core, (2 * plane + cp) * 2 + y))
    raw = lax.ppermute(raw, ("xline", "inline"), places)
    columns = lax.all_to_all(
        raw.reshape(n_i, n_x, n_xline, dz).transpose(2, 0, 1, 3),
        "xline", split_axis=0, concat_axis=0, tiled=True,
    ).reshape(n_xline // 2, 2, n_i, n_x, dz)
    positions = jnp.arange(full_x).astype(jnp.float32)
    weights = jnp.exp(-jnp.abs(positions[:, None] - positions[None, :]) / SMOOTH)
    weights = weights / jnp.sum(weights, axis=1, keepdims=True)
    gradient = jnp.einsum(
        "phixz,ypx->zhiy", columns, weights.reshape(full_x, n_xline // 2, n_x),
        precision=lax.Precision.HIGHEST,
    ).reshape(dz, tile_i, full_x)
    return (gradient,) + tuple(hand_over(last, previous))


def solution(mesh):
    return jax.shard_map(
        per_device,
        mesh=mesh,
        in_specs=(
            P(("shots", "inline"), "xline", None),
            P(("shots", "inline"), "xline", None),
            P(("shots", "inline"), "xline", None),
            P(("shots", "inline"), "xline", None),
            P("inline", "xline", None),
            P("inline", "xline", None),
            P("shots", ("xline", "inline")),
            P(("xline", "inline"), None),
            P(("xline", "inline"), None),
            P("shots"),
            P("shots", None),
        ),
        out_specs=(
            P(("shots", "xline"), "inline", None),
            P(("shots", "inline"), "xline", None),
            P(("shots", "inline"), "xline", None),
        ),
        check_vma=False,
    )
```

```python
import functools

import jax
import jax.numpy as jnp
from jax import lax
from jax.experimental import pallas as pl
from jax.experimental.pallas import tpu as pltpu
from jax.sharding import PartitionSpec as P

CAP = 8
SMOOTH = 16
MESH = pl.DeviceIdType.MESH

SECOND_COEFFS = (-205.0 / 72.0, 8.0 / 5.0, -1.0 / 5.0, 8.0 / 315.0, -1.0 / 560.0)
FIRST_COEFFS = (4.0 / 5.0, -1.0 / 5.0, 4.0 / 105.0, -1.0 / 280.0)
LEFT, RIGHT, UP, DOWN = 0, 1, 2, 3
DENSITY = 4
RHO, NOW, SPEED, BEFORE, ADJ_NOW, ADJ_BEFORE = range(6)


def split_bf16(value):
    high = value.astype(jnp.bfloat16)
    low = (value - high.astype(jnp.float32)).astype(jnp.bfloat16)
    return high, low


def dot(a, b):
    return jnp.dot(a, b, preferred_element_type=jnp.float32)


def dot_nt(a, b):
    return lax.dot_general(a, b, (((1,), (1,)), ((), ())), preferred_element_type=jnp.float32)


def dot_tn_exact(a, b):
    dims = (((0,), (0,)), ((), ()))
    ah, al = split_bf16(a)
    bh, bl = split_bf16(b)
    one = lax.dot_general(ah, bh, dims, preferred_element_type=jnp.float32)
    two = lax.dot_general(al, bh, dims, preferred_element_type=jnp.float32)
    three = lax.dot_general(ah, bl, dims, preferred_element_type=jnp.float32)
    return one + (two + three)


def div(value, n):
    return lax.shift_right_arithmetic(value, jnp.full_like(value, n.bit_length() - 1))


def mod(value, n):
    return value & (n - 1)


def wave_kernel(
    sizes,
    log_density, fwd_now, velocity, fwd_before, adj_now, adj_before,
    given_observed, given_cells, given_counts, given_src, given_wavelet,
    grad_out, last_out, previous_out,
    field, vel, x_in, x_out, i_in, accel, base, image, slopes, speed_sq, wx,
    row_map, zmap_t, z_mat, residual_ref, traces, list_out, list_in, obs_in, g_send,
    held_observed, held_cells, held_counts, held_src, held_wavelet, adj_base,
    send_sem, recv_sem, rt_send, rt_recv, rt_local, list_send, list_recv, obs_send, obs_recv,
    ret_send, ret_recv, ret_local, g_ssem, g_rsem, g_local, small_sem,
):
    tile_i, tile_x, n_i, n_x, depth, steps, n_xline, fused = sizes
    rows = n_i * n_x
    small_in = (given_observed, given_cells, given_counts, given_src, given_wavelet)
    small_held = (held_observed, held_cells, held_counts, held_src, held_wavelet)
    slots = held_cells.shape[1]
    n_group = 2 * n_xline
    xl = lax.axis_index("xline")
    core = lax.axis_index("inline")
    me = xl * 2 + core
    y = lax.rem(xl, 2)
    plane = xl // 2
    z_odd = lax.rem(plane, 2)
    mate = xl + 1 - 2 * y
    cp = lax.rem(core + z_odd, 2)
    origin = y
    q = 2 * y + cp
    stays = y == core
    has = (xl >= 2, xl < n_xline - 2, q > 0, q < 3)
    other_core = 1 - core
    target = (
        {"xline": xl - 2, "inline": other_core},
        {"xline": xl + 2, "inline": other_core},
        {"xline": jnp.where(q == 2, mate, xl), "inline": other_core},
        {"xline": jnp.where(q == 1, mate, xl), "inline": other_core},
    )
    inner_i = pl.ds(4, n_i)
    inner_x = pl.ds(8, n_x)
    middle = n_i // 2

    barrier = pltpu.get_barrier_semaphore()

    def greet(device):
        pl.semaphore_signal(barrier, inc=1, device_id=device, device_id_type=MESH)

    near = n_xline // 2 <= 4
    if near:
        greet({"inline": other_core})
        greet({"xline": mate})
        greet({"xline": mate, "inline": other_core})
        for way in (LEFT, RIGHT):
            @pl.when(has[way])
            def _():
                greet(target[way])
        greeted = 3 + has[LEFT].astype(jnp.int32) + has[RIGHT].astype(jnp.int32)
    else:
        @pl.loop(1, n_group)
        def _(r):
            peer = lax.rem(me + r, n_group)
            greet({"xline": peer // 2, "inline": lax.rem(peer, 2)})
        greeted = n_group - 1

    small = [
        pltpu.make_async_copy(given, held, small_sem.at[n])
        for n, (given, held) in enumerate(zip(small_in, small_held))
    ]
    for copy in small:
        copy.start()
    observed, rec_cells, rec_counts, src_cell, wavelet = small_held

    def beside(idx, way, part):
        part_rows = pl.ds(part * middle, middle)
        sem = way + 4 * part
        return pltpu.make_async_remote_copy(
            src_ref=x_out.at[idx, way, part_rows], dst_ref=x_in.at[idx, 1 - way, part_rows],
            send_sem=send_sem.at[idx, sem], recv_sem=recv_sem.at[idx, sem],
            device_id=target[way], device_id_type=MESH,
        )

    def above(idx, part, side):
        up = part == 0
        return pltpu.make_async_remote_copy(
            src_ref=field.at[idx, pl.ds(4 + part * (n_i - 4), 4), inner_x, :],
            dst_ref=i_in.at[idx, part if side else 1 - part],
            send_sem=send_sem.at[idx, 2 + part], recv_sem=recv_sem.at[idx, 3 - part if side else 2 + part],
            device_id={
                "xline": jnp.where(up, target[UP]["xline"], target[DOWN]["xline"]), "inline": other_core
            },
            device_id_type=MESH,
        )

    def has_row(part):
        return jnp.where(part == 0, q, 3 - q) > 0

    def send(idx, part):
        for way in (LEFT, RIGHT):
            @pl.when(has[way])
            def _():
                beside(idx, way, part).start()

        @pl.when(has_row(part))
        def _():
            above(idx, part, False).start()

    def stage(idx, part):
        part_rows = pl.ds(part * middle, middle)
        field_rows = pl.ds(4 + part * middle, middle)
        x_out[idx, 0, part_rows] = field[idx, field_rows, pl.ds(8, 4), :]
        x_out[idx, 1, part_rows] = field[idx, field_rows, pl.ds(4 + n_x, 4), :]

    def finish(idx, part):
        for way in (LEFT, RIGHT):
            @pl.when(has[way])
            def _():
                beside(idx, way, part).wait_send()
                beside(idx, 1 - way, part).wait_recv()

        @pl.when(has_row(part))
        def _():
            above(idx, part, False).wait_send()
            above(idx, part, True).wait_recv()

    halves = (1 - y, y)

    sources = (log_density, fwd_now, velocity, fwd_before, adj_now, adj_before)
    places = (DENSITY, 0, None, 1, 2, 3)

    def landing(n, from_y):
        columns = pl.multiple_of(from_y * tile_x, tile_x)
        if n == SPEED:
            return vel.at[:, pl.ds(columns, tile_x), :]
        return field.at[places[n], inner_i, pl.ds(pl.multiple_of(8 + columns, 8), tile_x), :]

    def tile_copy(n, a):
        return pltpu.make_async_remote_copy(
            src_ref=sources[n].at[pl.ds(a * n_i, n_i)], dst_ref=landing(n, y),
            send_sem=rt_send.at[n, a], recv_sem=rt_recv.at[n, y],
            device_id={"xline": 2 * plane + core, "inline": lax.rem(a + z_odd, 2)},
            device_id_type=MESH,
        )

    def tile_arrival(n, from_y):
        return pltpu.make_async_remote_copy(
            src_ref=sources[n].at[pl.ds(0, n_i)], dst_ref=landing(n, from_y),
            send_sem=rt_send.at[n, 0], recv_sem=rt_recv.at[n, from_y],
            device_id={"xline": mate}, device_id_type=MESH,
        )

    def own_copy(n):
        return pltpu.make_async_copy(
            sources[n].at[pl.ds(cp * n_i, n_i)], landing(n, y), rt_local.at[n]
        )

    def leaves(a):
        return jnp.logical_not(jnp.logical_and(stays, cp == a))

    def arrives(from_y):
        return jnp.logical_not(jnp.logical_and(stays, y == from_y))

    def tile_start(n):
        for a in range(2):
            @pl.when(leaves(a))
            def _():
                tile_copy(n, a).start()

        @pl.when(stays)
        def _():
            own_copy(n).start()

    def tile_finish(n):
        for from_y in range(2):
            @pl.when(arrives(from_y))
            def _():
                tile_arrival(n, from_y).wait_recv()
        for a in range(2):
            @pl.when(leaves(a))
            def _():
                tile_copy(n, a).wait_send()

        @pl.when(stays)
        def _():
            own_copy(n).wait()

    def list_copy(a):
        return pltpu.make_async_remote_copy(
            src_ref=list_out, dst_ref=list_in.at[y],
            send_sem=list_send.at[a], recv_sem=list_recv.at[y],
            device_id={"xline": 2 * plane + core, "inline": lax.rem(a + z_odd, 2)},
            device_id_type=MESH,
        )

    def list_arrival(from_y):
        return pltpu.make_async_remote_copy(
            src_ref=list_out, dst_ref=list_in.at[from_y],
            send_sem=list_send.at[0], recv_sem=list_recv.at[from_y],
            device_id={"xline": mate}, device_id_type=MESH,
        )

    def obs_copy(peer, slot):
        return pltpu.make_async_remote_copy(
            src_ref=observed, dst_ref=obs_in.at[slot],
            send_sem=obs_send.at[peer], recv_sem=obs_recv.at[slot],
            device_id={"xline": peer // 2, "inline": lax.rem(peer, 2)}, device_id_type=MESH,
        )

    finals = (previous_out, last_out)
    final_idx = (2 + (steps - 1) % 2, 2 + steps % 2)

    def home_copy(n, to_y):
        return pltpu.make_async_remote_copy(
            src_ref=field.at[final_idx[n], inner_i, pl.ds(8 + to_y * tile_x, tile_x), :],
            dst_ref=finals[n].at[pl.ds(cp * n_i, n_i)],
            send_sem=ret_send.at[n, to_y], recv_sem=ret_recv.at[n, cp],
            device_id={"xline": 2 * plane + to_y, "inline": origin}, device_id_type=MESH,
        )

    def home_arrival(n, a):
        return pltpu.make_async_remote_copy(
            src_ref=field.at[final_idx[n], inner_i, pl.ds(8, tile_x), :],
            dst_ref=finals[n].at[pl.ds(a * n_i, n_i)],
            send_sem=ret_send.at[n, 0], recv_sem=ret_recv.at[n, a],
            device_id={"xline": mate}, device_id_type=MESH,
        )

    def home_own(n):
        columns = pl.multiple_of(8 + y * tile_x, 8)
        return pltpu.make_async_copy(
            field.at[final_idx[n], inner_i, pl.ds(columns, tile_x), :],
            finals[n].at[pl.ds(cp * n_i, n_i)], ret_local.at[n],
        )

    def home_start(n):
        for to_y in range(2):
            @pl.when(arrives(to_y))
            def _():
                home_copy(n, to_y).start()

        @pl.when(stays)
        def _():
            home_own(n).start()

    def home_finish(n):
        for to_y in range(2):
            @pl.when(arrives(to_y))
            def _():
                home_copy(n, to_y).wait_send()
        for a in range(2):
            @pl.when(leaves(a))
            def _():
                home_arrival(n, a).wait_recv()

        @pl.when(stays)
        def _():
            home_own(n).wait()

    dz = depth // n_xline
    planes_n = n_xline // 2

    def slab_copy(d):
        return pltpu.make_async_remote_copy(
            src_ref=g_send.at[d],
            dst_ref=grad_out.at[cp, :, pl.ds(pl.multiple_of(plane * n_x, 8), n_x), :],
            send_sem=g_ssem.at[d], recv_sem=g_rsem.at[cp, plane],
            device_id={"xline": d, "inline": origin}, device_id_type=MESH,
        )

    def own_slab():
        return pltpu.make_async_copy(
            g_send.at[xl], grad_out.at[cp, :, pl.ds(pl.multiple_of(plane * n_x, 8), n_x), :], g_local.at[0]
        )

    def slab_arrival(a, p):
        return pltpu.make_async_remote_copy(
            src_ref=g_send.at[0],
            dst_ref=grad_out.at[a, :, pl.ds(pl.multiple_of(p * n_x, 8), n_x), :],
            send_sem=g_ssem.at[0], recv_sem=g_rsem.at[a, p],
            device_id={"xline": mate}, device_id_type=MESH,
        )

    def fused_gradient():
        group = 128 // dz
        lane = div(lax.broadcasted_iota(jnp.int32, (n_x, 128), 1), dz)
        for chunk in range(depth // 128):
            for ig in range(n_i // group):
                planes = [image[ig * group + j, :, pl.ds(chunk * 128, 128)] for j in range(group)]
                for dd in range(group):
                    out = None
                    for j in range(group):
                        shift = (j - dd) * dz % 128
                        moved = pltpu.roll(planes[j], shift, axis=1) if shift else planes[j]
                        out = moved if out is None else jnp.where(lane == j, moved, out)
                    g_send[chunk * group + dd, ig] = out

        @pl.loop(1, n_xline + 1)
        def _(r):
            d = lax.rem(xl + r, n_xline)

            @pl.when(jnp.logical_or(d != xl, origin != core))
            def _():
                slab_copy(d).start()

        home_start(1)

        @pl.when(origin == core)
        def _():
            own_slab().start()

        @pl.loop(0, n_xline)
        def _(r):
            a, p = lax.rem(r, 2), r // 2
            mine = jnp.logical_and(origin == core, jnp.logical_and(a == cp, p == plane))

            @pl.when(jnp.logical_not(mine))
            def _():
                slab_arrival(a, p).wait_recv()

        @pl.when(origin == core)
        def _():
            own_slab().wait()

        @pl.loop(1, n_xline + 1)
        def _(r):
            d = lax.rem(xl + r, n_xline)

            @pl.when(jnp.logical_or(d != xl, origin != core))
            def _():
                slab_copy(d).wait_send()

    for idx in range(5):
        field[idx, pl.ds(0, 4)] = jnp.zeros((4,) + field.shape[2:], jnp.float32)
        field[idx, pl.ds(n_i + 4, 4)] = jnp.zeros((4,) + field.shape[2:], jnp.float32)
        field[idx, inner_i, pl.ds(0, 8)] = jnp.zeros((n_i, 8, depth), jnp.float32)
        field[idx, inner_i, pl.ds(8 + n_x, 8)] = jnp.zeros((n_i, 8, depth), jnp.float32)
    for way in (LEFT, RIGHT, UP, DOWN):
        @pl.when(jnp.logical_not(has[way]))
        def _():
            halo = x_in if way < UP else i_in
            halo[:, way % 2] = jnp.zeros(halo.shape[:1] + halo.shape[2:], jnp.float32)
    image[...] = jnp.zeros(image.shape, jnp.float32)

    for copy in small:
        copy.wait()
    n_counts = rec_counts.shape[1]
    spread = (
        div(lax.broadcasted_iota(jnp.int32, (n_counts, slots), 1), CAP)
        == lax.broadcasted_iota(jnp.int32, (n_counts, slots), 0)
    ).astype(jnp.float32).astype(jnp.bfloat16)
    counts = jnp.broadcast_to(rec_counts[...].astype(jnp.float32), (8, n_counts)).astype(jnp.bfloat16)
    live = dot(counts, spread)
    place = mod(lax.broadcasted_iota(jnp.int32, (8, slots), 1), CAP).astype(jnp.float32)
    list_out[...] = jnp.where(place < live, jnp.broadcast_to(rec_cells[...], (8, slots)), -1)

    pl.semaphore_wait(barrier, greeted)

    for a in range(2):
        @pl.when(leaves(a))
        def _():
            list_copy(a).start()

    for n in (RHO, NOW):
        tile_start(n)
    for n in (SPEED, BEFORE):
        tile_start(n)

    obs_in[me] = observed[...]

    @pl.when(stays)
    def _():
        list_in[y] = list_out[...]

    offset = lax.broadcasted_iota(jnp.int32, (depth, depth), 0) - lax.broadcasted_iota(jnp.int32, (depth, depth), 1)
    second = jnp.zeros((depth, depth), jnp.float32)
    first = jnp.zeros((depth, depth), jnp.float32)
    for k in range(1, 5):
        second = jnp.where((offset == k) | (offset == -k), SECOND_COEFFS[k] / SECOND_COEFFS[1], second)
        first = jnp.where(offset == k, FIRST_COEFFS[k - 1] / FIRST_COEFFS[0], first)
        first = jnp.where(offset == -k, -FIRST_COEFFS[k - 1] / FIRST_COEFFS[0], first)
    z_mat[:, pl.ds(0, depth)] = second.astype(jnp.bfloat16)
    z_mat[:, pl.ds(depth, depth)] = first.astype(jnp.bfloat16)

    full_x = tile_x * n_xline
    cells = src_cell[...]
    src_i = div(cells, full_x * depth) - q * n_i
    src_x = mod(div(cells, depth), full_x) - plane * n_x
    inside = (src_i >= 0) & (src_i < n_i) & (src_x >= 0) & (src_x < n_x)
    src_row = jnp.where(inside, src_i * n_x + src_x, -1)
    n_src = cells.shape[1]
    src_rows = (lax.broadcasted_iota(jnp.int32, (rows, n_src), 0) == src_row).astype(jnp.float32)
    src_cols = (lax.broadcasted_iota(jnp.int32, (depth, n_src), 0) == mod(cells, depth)).astype(jnp.float32).astype(jnp.bfloat16)

    def flat(idx):
        return field[idx, inner_i, inner_x, :].reshape(rows, depth)

    def along_depth(idx):
        high, low = split_bf16(flat(idx))
        both = dot(high, z_mat[...]) + dot(low, z_mat[...])
        return both[:, :depth], both[:, depth:]

    def across(idx, i):
        lap = slope_i = slope_x = None
        for k in range(1, 5):
            plus_i = field[idx, i + 4 + k, inner_x, :]
            minus_i = field[idx, i + 4 - k, inner_x, :]
            plus_x = field[idx, i + 4, pl.ds(8 + k, n_x), :]
            minus_x = field[idx, i + 4, pl.ds(8 - k, n_x), :]
            terms = (
                SECOND_COEFFS[k] * ((plus_i + minus_i) + (plus_x + minus_x)),
                FIRST_COEFFS[k - 1] * (plus_i - minus_i),
                FIRST_COEFFS[k - 1] * (plus_x - minus_x),
            )
            if lap is None:
                lap, slope_i, slope_x = terms
            else:
                lap, slope_i, slope_x = lap + terms[0], slope_i + terms[1], slope_x + terms[2]
        return lap, slope_i, slope_x

    tile_finish(RHO)
    for part in halves:
        stage(DENSITY, part)
        send(DENSITY, part)
    tile_finish(NOW)
    for part in halves:
        stage(0, part)
        send(0, part)

    slopes[2] = (FIRST_COEFFS[0] * FIRST_COEFFS[0] * along_depth(DENSITY)[1]).reshape(n_i, n_x, depth)

    def bare(idx):
        lap, slope = along_depth(idx)
        return (SECOND_COEFFS[1] * lap - slopes[2].reshape(rows, depth) * slope).reshape(n_i, n_x, depth)

    def inject_sources(t):
        high, low = split_bf16(src_rows * wavelet[pl.ds(t, 1), :])
        return dot_nt(high, src_cols) + dot_nt(low, src_cols)

    base[...] = bare(0)
    accel[0] = inject_sources(0).reshape(n_i, n_x, depth)

    finish(DENSITY, 0)
    finish(DENSITY, 1)
    field[DENSITY, pl.ds(0, 4), inner_x, :] = i_in[DENSITY, 0]
    field[DENSITY, pl.ds(n_i + 4, 4), inner_x, :] = i_in[DENSITY, 1]
    field[DENSITY, inner_i, pl.ds(4, 4), :] = x_in[DENSITY, 0]
    field[DENSITY, inner_i, pl.ds(8 + n_x, 4), :] = x_in[DENSITY, 1]

    def lateral(idx, i):
        lap, slope_i, slope_x = across(idx, i)
        center = field[idx, i + 4, inner_x, :]
        return center, (
            3.0 * SECOND_COEFFS[0] * center + lap - slopes[0, i] * slope_i - slopes[1, i] * slope_x
        )

    @pl.loop(0, n_i)
    def _(i):
        _, slope_i, slope_x = across(DENSITY, i)
        slopes[0, i] = slope_i
        slopes[1, i] = slope_x

    @pl.loop(0, n_i)
    def _(i):
        base[i] += lateral(0, i)[1]

    tile_finish(SPEED)
    column = lax.broadcasted_iota(jnp.int32, (n_x, depth), 0)

    @pl.loop(0, n_i)
    def _(i):
        square = vel[i] * vel[i]
        speed_sq[i] = square
        accel[0, i] += square * base[i]
        for k in range(1, 5):
            weight = jnp.where(
                column < k, SECOND_COEFFS[k] + FIRST_COEFFS[k - 1] * slopes[1, i],
                jnp.where(column >= n_x - k, SECOND_COEFFS[k] - FIRST_COEFFS[k - 1] * slopes[1, i], 0.0),
            )
            wx[k - 1, i] = square * weight

    tile_finish(BEFORE)

    @pl.loop(0, n_i)
    def _(i):
        field[1, i + 4, inner_x, :] = (
            2.0 * field[0, i + 4, inner_x, :] - field[1, i + 4, inner_x, :] + accel[0, i]
        )

    def make_maps():
        for from_y in range(2):
            @pl.when(arrives(from_y))
            def _():
                list_arrival(from_y).wait_recv()
        for a in range(2):
            @pl.when(leaves(a))
            def _():
                list_copy(a).wait_send()
        for from_y in range(2):
            spot = list_in[from_y][:1]
            cell_i = div(spot, tile_x * depth) - cp * n_i
            cell_x = mod(div(spot, depth), tile_x) + from_y * tile_x
            row = jnp.where((spot >= 0) & (cell_i >= 0) & (cell_i < n_i), cell_i * n_x + cell_x, -1)
            columns = pl.ds(from_y * slots, slots)
            row_map[:, columns] = (lax.broadcasted_iota(jnp.int32, (rows, slots), 0) == row).astype(jnp.float32)
            zmap_t[:, columns] = (
                lax.broadcasted_iota(jnp.int32, (depth, slots), 0) == mod(spot, depth)
            ).astype(jnp.float32).astype(jnp.bfloat16)

    def make_traces():
        @pl.loop(1, n_group)
        def _(r):
            peer = lax.rem(me + r, n_group)
            obs_copy(peer, peer).wait_recv()
            obs_copy(peer, me).wait_send()

        lane = div(lax.broadcasted_iota(jnp.int32, (8, slots), 1), CAP)
        for from_y in range(2):
            owner = (2 * plane + from_y) * 2 + origin

            def place_one(s, total):
                moved = pltpu.roll(obs_in[s], lax.rem(s - owner + n_group, n_group) * CAP, axis=1)
                return jnp.where(lane == s, moved, total)

            traces[:, pl.ds(from_y * slots, slots)] = lax.fori_loop(
                0, n_group, place_one, jnp.zeros((8, slots), jnp.float32)
            )

    def prepare(idx, term):
        base[...] = term.reshape(n_i, n_x, depth) + speed_sq[...] * bare(idx)

    def interior(now, other, i):
        center, sideways = lateral(now, i)
        change = base[i] + speed_sq[i] * sideways
        field[other, i + 4, inner_x, :] = 2.0 * center - field[other, i + 4, inner_x, :] + change
        return center, change

    def correction(now, i):
        pair = jnp.concatenate([x_in[now, 1, i], x_in[now, 0, i]], axis=0)
        total = None
        for k in range(1, 5):
            pieces = [pltpu.roll(pair, k, axis=0)]
            if n_x > 16:
                pieces.append(jnp.zeros((n_x - 16, depth), jnp.float32))
            pieces.append(pltpu.roll(pair, 8 - k, axis=0))
            term = wx[k - 1, i] * jnp.concatenate(pieces, axis=0)
            total = term if total is None else total + term
        return total

    def correct(now, other, part, t):
        up = part == 0
        sign = jnp.where(up, 1.0, -1.0)
        for r in range(middle):
            i = jnp.where(up, r, n_i - 1 - r)
            change = correction(now, i)
            lap = None
            for h in range(4 - r):
                k = r + 1 + h
                halo = i_in[now, part, jnp.where(up, 3 - h, h)]
                terms = SECOND_COEFFS[k] * halo, FIRST_COEFFS[k - 1] * halo
                lap, slope = terms if lap is None else (lap + terms[0], slope + terms[1])
            if lap is not None:
                change = change + speed_sq[i] * (lap + (sign * slopes[0, i]) * slope)
            fresh = field[other, i + 4, inner_x, :] + change
            field[other, i + 4, inner_x, :] = fresh
            x_out[other, 0, i] = fresh[:4]
            x_out[other, 1, i] = fresh[n_x - 4:]
            if t is not None:
                accel[t, i] += change

    def sample(idx, t):
        high, low = split_bf16(flat(idx))
        picked = dot(high, zmap_t[...]) + dot(low, zmap_t[...])
        predicted = jnp.sum(picked * row_map[...], axis=0, keepdims=True)
        residual_ref[t] = predicted

    def adjoint_start(part):
        @pl.loop(part * middle, (part + 1) * middle)
        def _(i):
            center, sideways = lateral(2, i)
            field[3, i + 4, inner_x, :] = (
                2.0 * center - field[3, i + 4, inner_x, :] + speed_sq[i] * (adj_base[i] + sideways)
            )

    def task_now():
        tile_start(ADJ_NOW)
        make_maps()

    def task_before():
        tile_start(ADJ_BEFORE)

    def task_traces():
        @pl.loop(1, n_group)
        def _(r):
            obs_copy(lax.rem(me + r, n_group), me).start()

    def task_halos():
        tile_finish(ADJ_NOW)
        for part in halves:
            stage(2, part)
            send(2, part)
        adj_base[...] = bare(2)

    def task_upper():
        tile_finish(ADJ_BEFORE)
        adjoint_start(0)

    def task_lower():
        adjoint_start(1)

    tasks = [task_now, task_before, task_traces, task_halos, task_upper, task_lower, make_traces]
    times = [1 + n * (steps - 2) // (len(tasks) - 1) for n in range(len(tasks))]

    @pl.loop(0, steps)
    def _(t):
        now = lax.rem(t, 2)
        other = 1 - now

        @pl.when(t > 0)
        def _():
            prepare(now, inject_sources(t))

            @pl.loop(0, n_i)
            def _(i):
                _, change = interior(now, other, i)
                accel[t, i] = change

        for at, task in zip(times, tasks):
            pl.when(t == at)(task)

        @pl.when(t >= 1)
        def _():
            sample(now, t - 1)

        for part in halves:
            finish(now, part)
            correct(now, other, part, t)

            @pl.when(t < steps - 1)
            def _():
                send(other, part)

    sample(steps % 2, steps - 1)

    @pl.loop(0, steps)
    def _(j):
        now = 2 + lax.rem(j, 2)
        other = 5 - now
        t = steps - 1 - j
        high, low = split_bf16(row_map[...] * (residual_ref[t] - traces[pl.ds(t, 1), :]))
        injected = dot_nt(high, zmap_t[...]) + dot_nt(low, zmap_t[...])

        @pl.when(j == 0)
        def _():
            field[3, inner_i, inner_x, :] += injected.reshape(n_i, n_x, depth)

        @pl.when(j > 0)
        def _():
            prepare(now, injected)

            @pl.loop(0, n_i)
            def _(i):
                center, _ = interior(now, other, i)
                image[i] += center * accel[t + 1, i]

        @pl.when(j == steps - 1)
        def _():
            home_start(0)

        for part in halves:
            finish(now, part)
            correct(now, other, part, None)

            @pl.when(j < steps - 1)
            def _():
                send(other, part)

    @pl.loop(0, n_i)
    def _(i):
        total = image[i] + field[final_idx[1], i + 4, inner_x, :] * accel[0, i]
        image[i] = total * (2.0 / steps) / vel[i]

    if fused:
        fused_gradient()
    else:
        grad_out[...] = image[...]
        home_start(1)
    home_finish(0)
    home_finish(1)


def finish_kernel(shape, slabs, last, previous):
    dz, tile_i, full_x = shape
    _, n_groups, _, lanes = slabs.shape
    group = lanes // dz

    def kernel(slabs_in, last_in, previous_in, gradient, last_out, previous_out, sem):
        copies = [
            pltpu.make_async_copy(last_in, last_out, sem.at[0]),
            pltpu.make_async_copy(previous_in, previous_out, sem.at[1]),
        ]
        for copy in copies:
            copy.start()
        far = (
            lax.broadcasted_iota(jnp.int32, (full_x, full_x), 0) - lax.broadcasted_iota(jnp.int32, (full_x, full_x), 1)
        ).astype(jnp.float32)
        weights = jnp.exp(-jnp.abs(far) / SMOOTH)
        weights = weights / jnp.sum(weights, axis=0, keepdims=True)
        for a in range(2):
            for ig in range(n_groups):
                lines = dot_tn_exact(slabs_in[a, ig], weights)
                for j in range(group):
                    gradient[:, (a * n_groups + ig) * group + j, :] = lines[j * dz:(j + 1) * dz]
        for copy in copies:
            copy.wait()

    vmem = pl.BlockSpec(memory_space=pltpu.VMEM)
    anywhere = pl.BlockSpec(memory_space=pl.ANY)
    return pl.pallas_call(
        kernel,
        out_shape=[jax.ShapeDtypeStruct(dims, jnp.float32) for dims in (shape, last.shape, previous.shape)],
        in_specs=[vmem] * 3,
        out_specs=[vmem, anywhere, anywhere],
        scratch_shapes=[pltpu.SemaphoreType.DMA((2,))],
    )(slabs, last, previous)


def per_device(
    fwd_now, fwd_before, adj_now, adj_before, velocity, log_density,
    observed, rec_cells, rec_counts, src_cell, wavelet,
):
    tile_i, tile_x, depth = fwd_now.shape
    steps = wavelet.shape[0]
    n_xline = lax.axis_size("xline")
    full_x = tile_x * n_xline
    n_i, n_x = tile_i // 2, tile_x * 2
    rows = n_i * n_x
    slots = rec_cells.shape[1]
    n_group = 2 * n_xline
    dz = depth // n_xline
    fused = dz >= 8 and 128 % dz == 0 and depth % 128 == 0 and n_i % (128 // dz) == 0
    group = 128 // dz if fused else 1

    block = (n_i, n_x, depth)
    vmem = pl.BlockSpec(memory_space=pltpu.VMEM)
    anywhere = pl.BlockSpec(memory_space=pl.ANY)
    dma = pltpu.SemaphoreType.DMA
    kernel = functools.partial(wave_kernel, (tile_i, tile_x, n_i, n_x, depth, steps, n_xline, fused))
    grad_shape = (2, n_i // group, full_x, 128) if fused else block
    slab_shape = (n_xline, n_i // group, n_x, 128) if fused else (8, 128)
    small_shapes = [observed, rec_cells, rec_counts, src_cell[None, :], wavelet]
    raw, last, previous = pl.pallas_call(
        kernel,
        out_shape=[
            jax.ShapeDtypeStruct(grad_shape, jnp.float32),
            jax.ShapeDtypeStruct(fwd_now.shape, jnp.float32),
            jax.ShapeDtypeStruct(fwd_now.shape, jnp.float32),
        ],
        in_specs=[anywhere] * 11,
        out_specs=[anywhere if fused else vmem, anywhere, anywhere],
        scratch_shapes=[
            pltpu.VMEM((5, n_i + 8, n_x + 16, depth), jnp.float32),
            pltpu.VMEM(block, jnp.float32),
            pltpu.VMEM((5, 2, n_i, 4, depth), jnp.float32),
            pltpu.VMEM((5, 2, n_i, 4, depth), jnp.float32),
            pltpu.VMEM((5, 2, 4, n_x, depth), jnp.float32),
            pltpu.VMEM((steps,) + block, jnp.float32),
            pltpu.VMEM(block, jnp.float32),
            pltpu.VMEM(block, jnp.float32),
            pltpu.VMEM((3,) + block, jnp.float32),
            pltpu.VMEM(block, jnp.float32),
            pltpu.VMEM((4,) + block, jnp.float32),
            pltpu.VMEM((rows, 2 * slots), jnp.float32),
            pltpu.VMEM((depth, 2 * slots), jnp.bfloat16),
            pltpu.VMEM((depth, 2 * depth), jnp.bfloat16),
            pltpu.VMEM((steps, 1, 2 * slots), jnp.float32),
            pltpu.VMEM((steps, 2 * slots), jnp.float32),
            pltpu.VMEM((8, slots), jnp.int32),
            pltpu.VMEM((2, 8, slots), jnp.int32),
            pltpu.VMEM((n_group,) + observed.shape, jnp.float32),
            pltpu.VMEM(slab_shape, jnp.float32),
            *[pltpu.VMEM(value.shape, value.dtype) for value in small_shapes],
            pltpu.VMEM(block, jnp.float32),
            dma((5, 6)), dma((5, 6)),
            dma((6, 2)), dma((6, 2)), dma((6,)),
            dma((2,)), dma((2,)),
            dma((n_group,)), dma((n_group,)),
            dma((2, 2)), dma((2, 2)), dma((2,)),
            dma((n_xline,)), dma((2, n_xline // 2)), dma((1,)), dma((5,)),
        ],
        compiler_params=pltpu.CompilerParams(
            collective_id=0, has_side_effects=True, vmem_limit_bytes=56 * 1024 * 1024
        ),
    )(
        log_density, fwd_now, velocity, fwd_before, adj_now, adj_before,
        *small_shapes,
    )
    if fused:
        return finish_kernel((dz, tile_i, full_x), raw, last, previous)

    places = []
    for xl in range(n_xline):
        for core in range(2):
            y, plane = xl % 2, xl // 2
            cp = (core + plane % 2) % 2
            places.append((xl * 2 + core, (2 * plane + cp) * 2 + y))
    raw = lax.ppermute(raw, ("xline", "inline"), places)
    columns = lax.all_to_all(
        raw.reshape(n_i, n_x, n_xline, dz).transpose(2, 0, 1, 3),
        "xline", split_axis=0, concat_axis=0, tiled=True,
    ).reshape(n_xline // 2, 2, n_i, n_x, dz)
    positions = jnp.arange(full_x).astype(jnp.float32)
    weights = jnp.exp(-jnp.abs(positions[:, None] - positions[None, :]) / SMOOTH)
    weights = weights / jnp.sum(weights, axis=1, keepdims=True)
    gradient = jnp.einsum(
        "phixz,ypx->zhiy", columns, weights.reshape(full_x, n_xline // 2, n_x),
        precision=lax.Precision.HIGHEST,
    ).reshape(dz, tile_i, full_x)
    return gradient, last, previous


def solution(mesh):
    return jax.shard_map(
        per_device,
        mesh=mesh,
        in_specs=(
            P(("shots", "inline"), "xline", None),
            P(("shots", "inline"), "xline", None),
            P(("shots", "inline"), "xline", None),
            P(("shots", "inline"), "xline", None),
            P("inline", "xline", None),
            P("inline", "xline", None),
            P("shots", ("xline", "inline")),
            P(("xline", "inline"), None),
            P(("xline", "inline"), None),
            P("shots"),
            P("shots", None),
        ),
        out_specs=(
            P(("shots", "xline"), "inline", None),
            P(("shots", "inline"), "xline", None),
            P(("shots", "inline"), "xline", None),
        ),
        check_vma=False,
    )
```

```python
import functools

import jax
import jax.numpy as jnp
from jax import lax
from jax.experimental import pallas as pl
from jax.experimental.pallas import tpu as pltpu
from jax.sharding import PartitionSpec as P

CAP = 8
SMOOTH = 16
MESH = pl.DeviceIdType.MESH

SECOND_COEFFS = (-205.0 / 72.0, 8.0 / 5.0, -1.0 / 5.0, 8.0 / 315.0, -1.0 / 560.0)
FIRST_COEFFS = (4.0 / 5.0, -1.0 / 5.0, 4.0 / 105.0, -1.0 / 280.0)
LEFT, RIGHT, UP, DOWN = 0, 1, 2, 3
DENSITY = 4
RHO, NOW, SPEED, BEFORE, ADJ_NOW, ADJ_BEFORE = range(6)


def split_bf16(value):
    high = value.astype(jnp.bfloat16)
    low = (value - high.astype(jnp.float32)).astype(jnp.bfloat16)
    return high, low


def dot(a, b):
    return jnp.dot(a, b, preferred_element_type=jnp.float32)


def dot_nt(a, b):
    return lax.dot_general(a, b, (((1,), (1,)), ((), ())), preferred_element_type=jnp.float32)


def dot_tn_exact(a, b):
    dims = (((0,), (0,)), ((), ()))
    ah, al = split_bf16(a)
    bh, bl = split_bf16(b)
    one = lax.dot_general(ah, bh, dims, preferred_element_type=jnp.float32)
    two = lax.dot_general(al, bh, dims, preferred_element_type=jnp.float32)
    three = lax.dot_general(ah, bl, dims, preferred_element_type=jnp.float32)
    return one + (two + three)


def div(value, n):
    return lax.shift_right_arithmetic(value, jnp.full_like(value, n.bit_length() - 1))


def mod(value, n):
    return value & (n - 1)


def wave_kernel(
    sizes,
    log_density, fwd_now, velocity, fwd_before, adj_now, adj_before,
    given_observed, given_cells, given_counts, given_src, given_wavelet,
    grad_out, last_out, previous_out,
    field, vel, x_in, x_out, i_in, accel, base, image, slopes, speed_sq, wx,
    row_map, zmap_t, z_mat, residual_ref, traces, list_out, list_in, obs_in, g_send,
    held_observed, held_cells, held_counts, held_src, held_wavelet, row_mat, wide, deep,
    x_send, x_recv, i_send, i_recv, rt_send, rt_recv, rt_local, list_send, list_recv, obs_send, obs_recv,
    ret_send, ret_recv, ret_local, g_ssem, g_rsem, g_local, small_sem,
):
    tile_i, tile_x, n_i, n_x, depth, steps, n_xline, fused = sizes
    rows = n_i * n_x
    small_in = (given_observed, given_cells, given_counts, given_src, given_wavelet)
    small_held = (held_observed, held_cells, held_counts, held_src, held_wavelet)
    slots = held_cells.shape[1]
    n_group = 2 * n_xline
    xl = lax.axis_index("xline")
    core = lax.axis_index("inline")
    me = xl * 2 + core
    y = lax.rem(xl, 2)
    plane = xl // 2
    z_odd = lax.rem(plane, 2)
    mate = xl + 1 - 2 * y
    cp = lax.rem(core + z_odd, 2)
    origin = y
    q = 2 * y + cp
    stays = y == core
    has = (xl >= 2, xl < n_xline - 2, q > 0, q < 3)
    other_core = 1 - core
    target = (
        {"xline": xl - 2, "inline": other_core},
        {"xline": xl + 2, "inline": other_core},
        {"xline": jnp.where(q == 2, mate, xl), "inline": other_core},
        {"xline": jnp.where(q == 1, mate, xl), "inline": other_core},
    )
    inner_i = pl.ds(4, n_i)
    inner_x = pl.ds(8, n_x)
    middle = n_i // 2

    barrier = pltpu.get_barrier_semaphore()

    def greet(device):
        pl.semaphore_signal(barrier, inc=1, device_id=device, device_id_type=MESH)

    near = n_xline // 2 <= 4
    if near:
        greet({"inline": other_core})
        greet({"xline": mate})
        greet({"xline": mate, "inline": other_core})
        for way in (LEFT, RIGHT):
            @pl.when(has[way])
            def _():
                greet(target[way])
        greeted = 3 + has[LEFT].astype(jnp.int32) + has[RIGHT].astype(jnp.int32)
    else:
        @pl.loop(1, n_group)
        def _(r):
            peer = lax.rem(me + r, n_group)
            greet({"xline": peer // 2, "inline": lax.rem(peer, 2)})
        greeted = n_group - 1

    small = [
        pltpu.make_async_copy(given, held, small_sem.at[n])
        for n, (given, held) in enumerate(zip(small_in, small_held))
    ]
    for copy in small:
        copy.start()
    observed, rec_cells, rec_counts, src_cell, wavelet = small_held

    layers = depth // 128
    half_x = n_x // 2

    def beside(idx, way, part, d):
        part_rows = pl.ds(part * middle, middle)
        return pltpu.make_async_remote_copy(
            src_ref=x_out.at[idx, way, d, part_rows], dst_ref=x_in.at[idx, 1 - way, d, part_rows],
            send_sem=x_send.at[idx, way, part, d], recv_sem=x_recv.at[idx, way, part, d],
            device_id=target[way], device_id_type=MESH,
        )

    def above(idx, part, c, d, arriving):
        up = part == 0
        return pltpu.make_async_remote_copy(
            src_ref=field.at[
                idx, pl.ds(4 + part * (n_i - 4), 4), pl.ds(8 + c * half_x, half_x), pl.ds(d * 128, 128)
            ],
            dst_ref=i_in.at[idx, part if arriving else 1 - part, d, c],
            send_sem=i_send.at[idx, part, c, d],
            recv_sem=i_recv.at[idx, 1 - part if arriving else part, c, d],
            device_id={
                "xline": jnp.where(up, target[UP]["xline"], target[DOWN]["xline"]), "inline": other_core
            },
            device_id_type=MESH,
        )

    def has_row(part):
        return jnp.where(part == 0, q, 3 - q) > 0

    def send(idx, part, d, c):
        @pl.when(has[c])
        def _():
            beside(idx, c, part, d).start()

        @pl.when(has_row(part))
        def _():
            above(idx, part, c, d, False).start()

    def finish(idx, part, d, c):
        @pl.when(has[c])
        def _():
            beside(idx, c, part, d).wait_send()
            beside(idx, 1 - c, part, d).wait_recv()

        @pl.when(has_row(part))
        def _():
            above(idx, part, c, d, False).wait_send()
            above(idx, part, c, d, True).wait_recv()

    def send_all(idx):
        for part, d, c in pieces:
            rows_at = pl.ds(part * middle, middle)
            x_out[idx, c, d, rows_at] = field[
                idx, pl.ds(4 + part * middle, middle), pl.ds(8 + c * (n_x - 4), 4), pl.ds(d * 128, 128)
            ]
            send(idx, part, d, c)

    halves = (1 - y, y)
    pieces = [(part, d, c) for part in halves for d in range(layers) for c in range(2)]

    sources = (log_density, fwd_now, velocity, fwd_before, adj_now, adj_before)
    places = (DENSITY, 0, None, 1, 2, 3)

    def landing(n, from_y):
        columns = pl.multiple_of(from_y * tile_x, tile_x)
        if n == SPEED:
            return vel.at[:, pl.ds(columns, tile_x), :]
        return field.at[places[n], inner_i, pl.ds(pl.multiple_of(8 + columns, 8), tile_x), :]

    def tile_copy(n, a):
        return pltpu.make_async_remote_copy(
            src_ref=sources[n].at[pl.ds(a * n_i, n_i)], dst_ref=landing(n, y),
            send_sem=rt_send.at[n, a], recv_sem=rt_recv.at[n, y],
            device_id={"xline": 2 * plane + core, "inline": lax.rem(a + z_odd, 2)},
            device_id_type=MESH,
        )

    def tile_arrival(n, from_y):
        return pltpu.make_async_remote_copy(
            src_ref=sources[n].at[pl.ds(0, n_i)], dst_ref=landing(n, from_y),
            send_sem=rt_send.at[n, 0], recv_sem=rt_recv.at[n, from_y],
            device_id={"xline": mate}, device_id_type=MESH,
        )

    def own_copy(n):
        return pltpu.make_async_copy(
            sources[n].at[pl.ds(cp * n_i, n_i)], landing(n, y), rt_local.at[n]
        )

    def leaves(a):
        return jnp.logical_not(jnp.logical_and(stays, cp == a))

    def arrives(from_y):
        return jnp.logical_not(jnp.logical_and(stays, y == from_y))

    def tile_start(n):
        for a in range(2):
            @pl.when(leaves(a))
            def _():
                tile_copy(n, a).start()

        @pl.when(stays)
        def _():
            own_copy(n).start()

    def tile_finish(n):
        for from_y in range(2):
            @pl.when(arrives(from_y))
            def _():
                tile_arrival(n, from_y).wait_recv()
        for a in range(2):
            @pl.when(leaves(a))
            def _():
                tile_copy(n, a).wait_send()

        @pl.when(stays)
        def _():
            own_copy(n).wait()

    def list_copy(a):
        return pltpu.make_async_remote_copy(
            src_ref=list_out, dst_ref=list_in.at[y],
            send_sem=list_send.at[a], recv_sem=list_recv.at[y],
            device_id={"xline": 2 * plane + core, "inline": lax.rem(a + z_odd, 2)},
            device_id_type=MESH,
        )

    def list_arrival(from_y):
        return pltpu.make_async_remote_copy(
            src_ref=list_out, dst_ref=list_in.at[from_y],
            send_sem=list_send.at[0], recv_sem=list_recv.at[from_y],
            device_id={"xline": mate}, device_id_type=MESH,
        )

    def obs_copy(peer, slot):
        return pltpu.make_async_remote_copy(
            src_ref=observed, dst_ref=obs_in.at[slot],
            send_sem=obs_send.at[peer], recv_sem=obs_recv.at[slot],
            device_id={"xline": peer // 2, "inline": lax.rem(peer, 2)}, device_id_type=MESH,
        )

    finals = (previous_out, last_out)
    final_idx = (2 + (steps - 1) % 2, 2 + steps % 2)

    def home_copy(n, to_y):
        return pltpu.make_async_remote_copy(
            src_ref=field.at[final_idx[n], inner_i, pl.ds(8 + to_y * tile_x, tile_x), :],
            dst_ref=finals[n].at[pl.ds(cp * n_i, n_i)],
            send_sem=ret_send.at[n, to_y], recv_sem=ret_recv.at[n, cp],
            device_id={"xline": 2 * plane + to_y, "inline": origin}, device_id_type=MESH,
        )

    def home_arrival(n, a):
        return pltpu.make_async_remote_copy(
            src_ref=field.at[final_idx[n], inner_i, pl.ds(8, tile_x), :],
            dst_ref=finals[n].at[pl.ds(a * n_i, n_i)],
            send_sem=ret_send.at[n, 0], recv_sem=ret_recv.at[n, a],
            device_id={"xline": mate}, device_id_type=MESH,
        )

    def home_own(n):
        columns = pl.multiple_of(8 + y * tile_x, 8)
        return pltpu.make_async_copy(
            field.at[final_idx[n], inner_i, pl.ds(columns, tile_x), :],
            finals[n].at[pl.ds(cp * n_i, n_i)], ret_local.at[n],
        )

    def home_start(n):
        for to_y in range(2):
            @pl.when(arrives(to_y))
            def _():
                home_copy(n, to_y).start()

        @pl.when(stays)
        def _():
            home_own(n).start()

    def home_finish(n):
        for to_y in range(2):
            @pl.when(arrives(to_y))
            def _():
                home_copy(n, to_y).wait_send()
        for a in range(2):
            @pl.when(leaves(a))
            def _():
                home_arrival(n, a).wait_recv()

        @pl.when(stays)
        def _():
            home_own(n).wait()

    dz = depth // n_xline
    planes_n = n_xline // 2

    def slab_copy(d):
        return pltpu.make_async_remote_copy(
            src_ref=g_send.at[d],
            dst_ref=grad_out.at[cp, :, pl.ds(pl.multiple_of(plane * n_x, 8), n_x), :],
            send_sem=g_ssem.at[d], recv_sem=g_rsem.at[cp, plane],
            device_id={"xline": d, "inline": origin}, device_id_type=MESH,
        )

    def own_slab():
        return pltpu.make_async_copy(
            g_send.at[xl], grad_out.at[cp, :, pl.ds(pl.multiple_of(plane * n_x, 8), n_x), :], g_local.at[0]
        )

    def slab_arrival(a, p):
        return pltpu.make_async_remote_copy(
            src_ref=g_send.at[0],
            dst_ref=grad_out.at[a, :, pl.ds(pl.multiple_of(p * n_x, 8), n_x), :],
            send_sem=g_ssem.at[0], recv_sem=g_rsem.at[a, p],
            device_id={"xline": mate}, device_id_type=MESH,
        )

    def fused_gradient():
        group = 128 // dz
        lane = div(lax.broadcasted_iota(jnp.int32, (n_x, 128), 1), dz)
        for chunk in range(depth // 128):
            for ig in range(n_i // group):
                planes = [image[ig * group + j, :, pl.ds(chunk * 128, 128)] for j in range(group)]
                for dd in range(group):
                    out = None
                    for j in range(group):
                        shift = (j - dd) * dz % 128
                        moved = pltpu.roll(planes[j], shift, axis=1) if shift else planes[j]
                        out = moved if out is None else jnp.where(lane == j, moved, out)
                    g_send[chunk * group + dd, ig] = out

        @pl.loop(1, n_xline + 1)
        def _(r):
            d = lax.rem(xl + r, n_xline)

            @pl.when(jnp.logical_or(d != xl, origin != core))
            def _():
                slab_copy(d).start()

        home_start(1)

        @pl.when(origin == core)
        def _():
            own_slab().start()

        @pl.loop(0, n_xline)
        def _(r):
            a, p = lax.rem(r, 2), r // 2
            mine = jnp.logical_and(origin == core, jnp.logical_and(a == cp, p == plane))

            @pl.when(jnp.logical_not(mine))
            def _():
                slab_arrival(a, p).wait_recv()

        @pl.when(origin == core)
        def _():
            own_slab().wait()

        @pl.loop(1, n_xline + 1)
        def _(r):
            d = lax.rem(xl + r, n_xline)

            @pl.when(jnp.logical_or(d != xl, origin != core))
            def _():
                slab_copy(d).wait_send()

    for idx in range(5):
        field[idx, pl.ds(0, 4)] = jnp.zeros((4,) + field.shape[2:], jnp.float32)
        field[idx, pl.ds(n_i + 4, 4)] = jnp.zeros((4,) + field.shape[2:], jnp.float32)
        field[idx, inner_i, pl.ds(0, 8)] = jnp.zeros((n_i, 8, depth), jnp.float32)
        field[idx, inner_i, pl.ds(8 + n_x, 8)] = jnp.zeros((n_i, 8, depth), jnp.float32)
    for way in (LEFT, RIGHT, UP, DOWN):
        @pl.when(jnp.logical_not(has[way]))
        def _():
            halo = x_in if way < UP else i_in
            halo[:, way % 2] = jnp.zeros(halo.shape[:1] + halo.shape[2:], jnp.float32)
    image[...] = jnp.zeros(image.shape, jnp.float32)

    for copy in small:
        copy.wait()
    n_counts = rec_counts.shape[1]
    spread = (
        div(lax.broadcasted_iota(jnp.int32, (n_counts, slots), 1), CAP)
        == lax.broadcasted_iota(jnp.int32, (n_counts, slots), 0)
    ).astype(jnp.float32).astype(jnp.bfloat16)
    counts = jnp.broadcast_to(rec_counts[...].astype(jnp.float32), (8, n_counts)).astype(jnp.bfloat16)
    live = dot(counts, spread)
    place = mod(lax.broadcasted_iota(jnp.int32, (8, slots), 1), CAP).astype(jnp.float32)
    list_out[...] = jnp.where(place < live, jnp.broadcast_to(rec_cells[...], (8, slots)), -1)

    pl.semaphore_wait(barrier, greeted)

    for a in range(2):
        @pl.when(leaves(a))
        def _():
            list_copy(a).start()

    for n in (RHO, NOW):
        tile_start(n)
    for n in (SPEED, BEFORE):
        tile_start(n)

    obs_in[me] = observed[...]

    @pl.when(stays)
    def _():
        list_in[y] = list_out[...]

    offset = lax.broadcasted_iota(jnp.int32, (depth, depth), 0) - lax.broadcasted_iota(jnp.int32, (depth, depth), 1)
    second = jnp.zeros((depth, depth), jnp.float32)
    first = jnp.zeros((depth, depth), jnp.float32)
    for k in range(1, 5):
        second = jnp.where((offset == k) | (offset == -k), SECOND_COEFFS[k] / SECOND_COEFFS[1], second)
        first = jnp.where(offset == k, FIRST_COEFFS[k - 1] / FIRST_COEFFS[0], first)
        first = jnp.where(offset == -k, -FIRST_COEFFS[k - 1] / FIRST_COEFFS[0], first)
    z_mat[:, pl.ds(0, depth)] = second.astype(jnp.bfloat16)
    z_mat[:, pl.ds(depth, depth)] = first.astype(jnp.bfloat16)

    at = lax.broadcasted_iota(jnp.int32, (rows, rows), 0)
    to = lax.broadcasted_iota(jnp.int32, (rows, rows), 1)
    step_i = div(to, n_x) - div(at, n_x)
    step_x = mod(to, n_x) - mod(at, n_x)
    lateral_lap = jnp.zeros((rows, rows), jnp.float32)
    for n, (along, still) in enumerate(((step_i, step_x), (step_x, step_i))):
        along = jnp.where(still == 0, along, 0)
        first = jnp.zeros((rows, rows), jnp.float32)
        for k in range(1, 5):
            lateral_lap = jnp.where((along == k) | (along == -k), SECOND_COEFFS[k] / SECOND_COEFFS[1], lateral_lap)
            first = jnp.where(along == k, FIRST_COEFFS[k - 1] / FIRST_COEFFS[0], first)
            first = jnp.where(along == -k, -FIRST_COEFFS[k - 1] / FIRST_COEFFS[0], first)
        row_mat[pl.ds((n + 1) * rows, rows), :] = first.astype(jnp.bfloat16)
    row_mat[pl.ds(0, rows), :] = lateral_lap.astype(jnp.bfloat16)

    full_x = tile_x * n_xline
    cells = src_cell[...]
    src_i = div(cells, full_x * depth) - q * n_i
    src_x = mod(div(cells, depth), full_x) - plane * n_x
    inside = (src_i >= 0) & (src_i < n_i) & (src_x >= 0) & (src_x < n_x)
    src_row = jnp.where(inside, src_i * n_x + src_x, -1)
    n_src = cells.shape[1]
    src_rows = (lax.broadcasted_iota(jnp.int32, (rows, n_src), 0) == src_row).astype(jnp.float32)
    src_cols = (lax.broadcasted_iota(jnp.int32, (depth, n_src), 0) == mod(cells, depth)).astype(jnp.float32).astype(jnp.bfloat16)

    def flat(idx):
        return field[idx, inner_i, inner_x, :].reshape(rows, depth)

    def differences(idx):
        high, low = split_bf16(flat(idx))
        wide[...] = dot(row_mat[...], high) + dot(row_mat[...], low)
        deep[...] = dot(high, z_mat[...]) + dot(low, z_mat[...])

    def operator(idx, i):
        def line(n):
            return pl.ds(pl.multiple_of(n * rows + i * n_x, n_x), n_x)

        center = field[idx, i + 4, inner_x, :]
        return center, (
            3.0 * SECOND_COEFFS[0] * center
            + SECOND_COEFFS[1] * (wide[line(0), :] + deep[line(0), pl.ds(0, depth)])
            - slopes[0, i] * wide[line(1), :] - slopes[1, i] * wide[line(2), :]
            - slopes[2, i] * deep[line(0), pl.ds(depth, depth)]
        )

    def across(idx, i):
        lap = slope_i = slope_x = None
        for k in range(1, 5):
            plus_i = field[idx, i + 4 + k, inner_x, :]
            minus_i = field[idx, i + 4 - k, inner_x, :]
            plus_x = field[idx, i + 4, pl.ds(8 + k, n_x), :]
            minus_x = field[idx, i + 4, pl.ds(8 - k, n_x), :]
            terms = (
                SECOND_COEFFS[k] * ((plus_i + minus_i) + (plus_x + minus_x)),
                FIRST_COEFFS[k - 1] * (plus_i - minus_i),
                FIRST_COEFFS[k - 1] * (plus_x - minus_x),
            )
            if lap is None:
                lap, slope_i, slope_x = terms
            else:
                lap, slope_i, slope_x = lap + terms[0], slope_i + terms[1], slope_x + terms[2]
        return lap, slope_i, slope_x

    tile_finish(RHO)
    send_all(DENSITY)
    tile_finish(NOW)
    send_all(0)

    high, low = split_bf16(flat(DENSITY))
    deep[...] = dot(high, z_mat[...]) + dot(low, z_mat[...])
    slopes[2] = ((FIRST_COEFFS[0] * FIRST_COEFFS[0]) * deep[:, pl.ds(depth, depth)]).reshape(n_i, n_x, depth)
    differences(0)

    def inject_sources(t):
        high, low = split_bf16(src_rows * wavelet[pl.ds(t, 1), :])
        return dot_nt(high, src_cols) + dot_nt(low, src_cols)

    accel[0] = inject_sources(0).reshape(n_i, n_x, depth)

    for part, d, c in pieces:
        finish(DENSITY, part, d, c)
    for d in range(layers):
        lanes = pl.ds(d * 128, 128)
        for side in range(2):
            for c in range(2):
                field[DENSITY, pl.ds(side * (n_i + 4), 4), pl.ds(8 + c * half_x, half_x), lanes] = i_in[DENSITY, side, d, c]
            field[DENSITY, inner_i, pl.ds(4 + side * (n_x + 4), 4), lanes] = x_in[DENSITY, side, d]

    @pl.loop(0, n_i)
    def _(i):
        _, slope_i, slope_x = across(DENSITY, i)
        slopes[0, i] = FIRST_COEFFS[0] * slope_i
        slopes[1, i] = FIRST_COEFFS[0] * slope_x

    tile_finish(SPEED)
    column = lax.broadcasted_iota(jnp.int32, (n_x, depth), 0)

    @pl.loop(0, n_i)
    def _(i):
        square = vel[i] * vel[i]
        speed_sq[i] = square
        accel[0, i] += square * operator(0, i)[1]
        for k in range(1, 5):
            weight = jnp.where(
                column < k, SECOND_COEFFS[k] + (FIRST_COEFFS[k - 1] / FIRST_COEFFS[0]) * slopes[1, i],
                jnp.where(
                    column >= n_x - k, SECOND_COEFFS[k] - (FIRST_COEFFS[k - 1] / FIRST_COEFFS[0]) * slopes[1, i], 0.0
                ),
            )
            wx[k - 1, i] = square * weight

    tile_finish(BEFORE)

    @pl.loop(0, n_i)
    def _(i):
        field[1, i + 4, inner_x, :] = (
            2.0 * field[0, i + 4, inner_x, :] - field[1, i + 4, inner_x, :] + accel[0, i]
        )

    def make_maps():
        for from_y in range(2):
            @pl.when(arrives(from_y))
            def _():
                list_arrival(from_y).wait_recv()
        for a in range(2):
            @pl.when(leaves(a))
            def _():
                list_copy(a).wait_send()
        for from_y in range(2):
            spot = list_in[from_y][:1]
            cell_i = div(spot, tile_x * depth) - cp * n_i
            cell_x = mod(div(spot, depth), tile_x) + from_y * tile_x
            row = jnp.where((spot >= 0) & (cell_i >= 0) & (cell_i < n_i), cell_i * n_x + cell_x, -1)
            columns = pl.ds(from_y * slots, slots)
            row_map[:, columns] = (lax.broadcasted_iota(jnp.int32, (rows, slots), 0) == row).astype(jnp.float32)
            zmap_t[:, columns] = (
                lax.broadcasted_iota(jnp.int32, (depth, slots), 0) == mod(spot, depth)
            ).astype(jnp.float32).astype(jnp.bfloat16)

    def make_traces():
        @pl.loop(1, n_group)
        def _(r):
            peer = lax.rem(me + r, n_group)
            obs_copy(peer, peer).wait_recv()
            obs_copy(peer, me).wait_send()

        lane = div(lax.broadcasted_iota(jnp.int32, (8, slots), 1), CAP)
        for from_y in range(2):
            owner = (2 * plane + from_y) * 2 + origin

            def place_one(s, total):
                moved = pltpu.roll(obs_in[s], lax.rem(s - owner + n_group, n_group) * CAP, axis=1)
                return jnp.where(lane == s, moved, total)

            traces[:, pl.ds(from_y * slots, slots)] = lax.fori_loop(
                0, n_group, place_one, jnp.zeros((8, slots), jnp.float32)
            )

    def prepare(idx, term):
        base[...] = term.reshape(n_i, n_x, depth)
        differences(idx)

    def interior(now, other, i):
        center, value = operator(now, i)
        change = base[i] + speed_sq[i] * value
        field[other, i + 4, inner_x, :] = 2.0 * center - field[other, i + 4, inner_x, :] + change
        return center, change

    def correct(now, other, part, d, c, t):
        up = part == 0
        sign = jnp.where(up, 1.0, -1.0)
        columns, lanes = pl.ds(c * half_x, half_x), pl.ds(d * 128, 128)
        for r in range(middle):
            i = jnp.where(up, r, n_i - 1 - r)
            halo = x_in[now, c, d, i]
            pair = jnp.concatenate([halo] * (half_x // 4), axis=0)
            change = wx[3, i, columns, lanes] * pair
            for k in range(1, 4):
                change += wx[k - 1, i, columns, lanes] * pltpu.roll(pair, half_x - k if c else k, axis=0)
            lap = None
            for h in range(4 - r):
                k = r + 1 + h
                halo = i_in[now, part, d, c, jnp.where(up, 3 - h, h)]
                terms = SECOND_COEFFS[k] * halo, (FIRST_COEFFS[k - 1] / FIRST_COEFFS[0]) * halo
                lap, slope = terms if lap is None else (lap + terms[0], slope + terms[1])
            if lap is not None:
                change += speed_sq[i, columns, lanes] * (lap + (sign * slopes[0, i, columns, lanes]) * slope)
            spot = (other, i + 4, pl.ds(8 + c * half_x, half_x), lanes)
            fresh = field[spot] + change
            field[spot] = fresh
            x_out[other, c, d, i] = fresh[half_x - 4:] if c else fresh[:4]
            if t is not None:
                accel[t, i, columns, lanes] += change

    def sample(idx, t):
        high, low = split_bf16(flat(idx))
        picked = dot(high, zmap_t[...]) + dot(low, zmap_t[...])
        predicted = jnp.sum(picked * row_map[...], axis=0, keepdims=True)
        residual_ref[t] = predicted

    def task_now():
        tile_start(ADJ_NOW)
        make_maps()

    def task_before():
        tile_start(ADJ_BEFORE)

    def task_traces():
        @pl.loop(1, n_group)
        def _(r):
            obs_copy(lax.rem(me + r, n_group), me).start()

    def task_halos():
        tile_finish(ADJ_NOW)
        send_all(2)

    def task_adjoint():
        tile_finish(ADJ_BEFORE)
        differences(2)

        @pl.loop(0, n_i, unroll=2)
        def _(i):
            center, value = operator(2, i)
            field[3, i + 4, inner_x, :] = (
                2.0 * center - field[3, i + 4, inner_x, :] + speed_sq[i] * value
            )

    tasks = [task_now, task_before, task_traces, task_halos, task_adjoint, make_traces]
    times = [1 + n * (steps - 2) // len(tasks) for n in range(len(tasks))]

    @pl.loop(0, steps)
    def _(t):
        now = lax.rem(t, 2)
        other = 1 - now

        @pl.when(t > 0)
        def _():
            prepare(now, inject_sources(t))

            @pl.loop(0, n_i, unroll=2)
            def _(i):
                _, change = interior(now, other, i)
                accel[t, i] = change

        for at, task in zip(times, tasks):
            pl.when(t == at)(task)

        @pl.when(t >= 1)
        def _():
            sample(now, t - 1)

        for part, d, c in pieces:
            finish(now, part, d, c)
            correct(now, other, part, d, c, t)

            @pl.when(t < steps - 1)
            def _():
                send(other, part, d, c)

    sample(steps % 2, steps - 1)

    @pl.loop(0, steps)
    def _(j):
        now = 2 + lax.rem(j, 2)
        other = 5 - now
        t = steps - 1 - j
        high, low = split_bf16(row_map[...] * (residual_ref[t] - traces[pl.ds(t, 1), :]))
        injected = dot_nt(high, zmap_t[...]) + dot_nt(low, zmap_t[...])

        @pl.when(j == 0)
        def _():
            field[3, inner_i, inner_x, :] += injected.reshape(n_i, n_x, depth)

        @pl.when(j > 0)
        def _():
            prepare(now, injected)

            @pl.loop(0, n_i, unroll=2)
            def _(i):
                center, _ = interior(now, other, i)
                image[i] += center * accel[t + 1, i]

        @pl.when(j == steps - 1)
        def _():
            home_start(0)

        for part, d, c in pieces:
            finish(now, part, d, c)
            correct(now, other, part, d, c, None)

            @pl.when(j < steps - 1)
            def _():
                send(other, part, d, c)

    @pl.loop(0, n_i)
    def _(i):
        total = image[i] + field[final_idx[1], i + 4, inner_x, :] * accel[0, i]
        image[i] = total * (2.0 / steps) / vel[i]

    if fused:
        fused_gradient()
    else:
        grad_out[...] = image[...]
        home_start(1)
    home_finish(0)
    home_finish(1)


def finish_kernel(shape, slabs, last, previous):
    dz, tile_i, full_x = shape
    _, n_groups, _, lanes = slabs.shape
    group = lanes // dz

    def kernel(slabs_in, last_in, previous_in, gradient, last_out, previous_out, sem):
        copies = [
            pltpu.make_async_copy(last_in, last_out, sem.at[0]),
            pltpu.make_async_copy(previous_in, previous_out, sem.at[1]),
        ]
        for copy in copies:
            copy.start()
        far = (
            lax.broadcasted_iota(jnp.int32, (full_x, full_x), 0) - lax.broadcasted_iota(jnp.int32, (full_x, full_x), 1)
        ).astype(jnp.float32)
        weights = jnp.exp(-jnp.abs(far) / SMOOTH)
        weights = weights / jnp.sum(weights, axis=0, keepdims=True)
        for a in range(2):
            for ig in range(n_groups):
                lines = dot_tn_exact(slabs_in[a, ig], weights)
                for j in range(group):
                    gradient[:, (a * n_groups + ig) * group + j, :] = lines[j * dz:(j + 1) * dz]
        for copy in copies:
            copy.wait()

    vmem = pl.BlockSpec(memory_space=pltpu.VMEM)
    anywhere = pl.BlockSpec(memory_space=pl.ANY)
    return pl.pallas_call(
        kernel,
        out_shape=[jax.ShapeDtypeStruct(dims, jnp.float32) for dims in (shape, last.shape, previous.shape)],
        in_specs=[vmem] * 3,
        out_specs=[vmem, anywhere, anywhere],
        scratch_shapes=[pltpu.SemaphoreType.DMA((2,))],
    )(slabs, last, previous)


def per_device(
    fwd_now, fwd_before, adj_now, adj_before, velocity, log_density,
    observed, rec_cells, rec_counts, src_cell, wavelet,
):
    tile_i, tile_x, depth = fwd_now.shape
    steps = wavelet.shape[0]
    n_xline = lax.axis_size("xline")
    full_x = tile_x * n_xline
    n_i, n_x = tile_i // 2, tile_x * 2
    rows = n_i * n_x
    slots = rec_cells.shape[1]
    n_group = 2 * n_xline
    dz = depth // n_xline
    fused = dz >= 8 and 128 % dz == 0 and depth % 128 == 0 and n_i % (128 // dz) == 0
    group = 128 // dz if fused else 1
    layers = depth // 128

    block = (n_i, n_x, depth)
    vmem = pl.BlockSpec(memory_space=pltpu.VMEM)
    anywhere = pl.BlockSpec(memory_space=pl.ANY)
    dma = pltpu.SemaphoreType.DMA
    kernel = functools.partial(wave_kernel, (tile_i, tile_x, n_i, n_x, depth, steps, n_xline, fused))
    grad_shape = (2, n_i // group, full_x, 128) if fused else block
    slab_shape = (n_xline, n_i // group, n_x, 128) if fused else (8, 128)
    small_shapes = [observed, rec_cells, rec_counts, src_cell[None, :], wavelet]
    raw, last, previous = pl.pallas_call(
        kernel,
        out_shape=[
            jax.ShapeDtypeStruct(grad_shape, jnp.float32),
            jax.ShapeDtypeStruct(fwd_now.shape, jnp.float32),
            jax.ShapeDtypeStruct(fwd_now.shape, jnp.float32),
        ],
        in_specs=[anywhere] * 11,
        out_specs=[anywhere if fused else vmem, anywhere, anywhere],
        scratch_shapes=[
            pltpu.VMEM((5, n_i + 8, n_x + 16, depth), jnp.float32),
            pltpu.VMEM(block, jnp.float32),
            pltpu.VMEM((5, 2, layers, n_i, 4, 128), jnp.float32),
            pltpu.VMEM((5, 2, layers, n_i, 4, 128), jnp.float32),
            pltpu.VMEM((5, 2, layers, 2, 4, tile_x, 128), jnp.float32),
            pltpu.VMEM((steps,) + block, jnp.float32),
            pltpu.VMEM(block, jnp.float32),
            pltpu.VMEM(block, jnp.float32),
            pltpu.VMEM((3,) + block, jnp.float32),
            pltpu.VMEM(block, jnp.float32),
            pltpu.VMEM((4,) + block, jnp.float32),
            pltpu.VMEM((rows, 2 * slots), jnp.float32),
            pltpu.VMEM((depth, 2 * slots), jnp.bfloat16),
            pltpu.VMEM((depth, 2 * depth), jnp.bfloat16),
            pltpu.VMEM((steps, 1, 2 * slots), jnp.float32),
            pltpu.VMEM((steps, 2 * slots), jnp.float32),
            pltpu.VMEM((8, slots), jnp.int32),
            pltpu.VMEM((2, 8, slots), jnp.int32),
            pltpu.VMEM((n_group,) + observed.shape, jnp.float32),
            pltpu.VMEM(slab_shape, jnp.float32),
            *[pltpu.VMEM(value.shape, value.dtype) for value in small_shapes],
            pltpu.VMEM((3 * rows, rows), jnp.bfloat16),
            pltpu.VMEM((3 * rows, depth), jnp.float32),
            pltpu.VMEM((rows, 2 * depth), jnp.float32),
            *[dma((5, 2, 2, layers)) for _ in range(4)],
            dma((6, 2)), dma((6, 2)), dma((6,)),
            dma((2,)), dma((2,)),
            dma((n_group,)), dma((n_group,)),
            dma((2, 2)), dma((2, 2)), dma((2,)),
            dma((n_xline,)), dma((2, n_xline // 2)), dma((1,)), dma((5,)),
        ],
        compiler_params=pltpu.CompilerParams(
            collective_id=0, has_side_effects=True, vmem_limit_bytes=56 * 1024 * 1024
        ),
    )(
        log_density, fwd_now, velocity, fwd_before, adj_now, adj_before,
        *small_shapes,
    )
    if fused:
        return finish_kernel((dz, tile_i, full_x), raw, last, previous)

    places = []
    for xl in range(n_xline):
        for core in range(2):
            y, plane = xl % 2, xl // 2
            cp = (core + plane % 2) % 2
            places.append((xl * 2 + core, (2 * plane + cp) * 2 + y))
    raw = lax.ppermute(raw, ("xline", "inline"), places)
    columns = lax.all_to_all(
        raw.reshape(n_i, n_x, n_xline, dz).transpose(2, 0, 1, 3),
        "xline", split_axis=0, concat_axis=0, tiled=True,
    ).reshape(n_xline // 2, 2, n_i, n_x, dz)
    positions = jnp.arange(full_x).astype(jnp.float32)
    weights = jnp.exp(-jnp.abs(positions[:, None] - positions[None, :]) / SMOOTH)
    weights = weights / jnp.sum(weights, axis=1, keepdims=True)
    gradient = jnp.einsum(
        "phixz,ypx->zhiy", columns, weights.reshape(full_x, n_xline // 2, n_x),
        precision=lax.Precision.HIGHEST,
    ).reshape(dz, tile_i, full_x)
    return gradient, last, previous


def solution(mesh):
    return jax.shard_map(
        per_device,
        mesh=mesh,
        in_specs=(
            P(("shots", "inline"), "xline", None),
            P(("shots", "inline"), "xline", None),
            P(("shots", "inline"), "xline", None),
            P(("shots", "inline"), "xline", None),
            P("inline", "xline", None),
            P("inline", "xline", None),
            P("shots", ("xline", "inline")),
            P(("xline", "inline"), None),
            P(("xline", "inline"), None),
            P("shots"),
            P("shots", None),
        ),
        out_specs=(
            P(("shots", "xline"), "inline", None),
            P(("shots", "inline"), "xline", None),
            P(("shots", "inline"), "xline", None),
        ),
        check_vma=False,
    )
```

```python
import functools

import jax
import jax.numpy as jnp
from jax import lax
from jax.experimental import pallas as pl
from jax.experimental.pallas import tpu as pltpu
from jax.sharding import PartitionSpec as P

CAP = 8
SMOOTH = 16
MESH = pl.DeviceIdType.MESH

SECOND_COEFFS = (-205.0 / 72.0, 8.0 / 5.0, -1.0 / 5.0, 8.0 / 315.0, -1.0 / 560.0)
FIRST_COEFFS = (4.0 / 5.0, -1.0 / 5.0, 4.0 / 105.0, -1.0 / 280.0)
LEFT, RIGHT, UP, DOWN = 0, 1, 2, 3
DENSITY = 4
RHO, NOW, SPEED, BEFORE, ADJ_NOW, ADJ_BEFORE = range(6)


def split_bf16(value):
    high = value.astype(jnp.bfloat16)
    low = (value - high.astype(jnp.float32)).astype(jnp.bfloat16)
    return high, low


def dot(a, b):
    return jnp.dot(a, b, preferred_element_type=jnp.float32)


def dot_nt(a, b):
    return lax.dot_general(a, b, (((1,), (1,)), ((), ())), preferred_element_type=jnp.float32)


def dot_tn_exact(a, b):
    dims = (((0,), (0,)), ((), ()))
    ah, al = split_bf16(a)
    bh, bl = split_bf16(b)
    one = lax.dot_general(ah, bh, dims, preferred_element_type=jnp.float32)
    two = lax.dot_general(al, bh, dims, preferred_element_type=jnp.float32)
    three = lax.dot_general(ah, bl, dims, preferred_element_type=jnp.float32)
    return one + (two + three)


def div(value, n):
    return lax.shift_right_arithmetic(value, jnp.full_like(value, n.bit_length() - 1))


def mod(value, n):
    return value & (n - 1)


def wave_kernel(
    sizes,
    log_density, fwd_now, velocity, fwd_before, adj_now, adj_before,
    given_observed, given_cells, given_counts, given_src, given_wavelet,
    grad_out, last_out, previous_out,
    field, vel, x_in, x_out, i_in, accel, base, image, slopes, speed_sq, wx,
    row_map, zmap_t, z_mat, residual_ref, traces, list_out, list_in, obs_in, g_send,
    held_observed, held_cells, held_counts, held_src, held_wavelet, row_mat, wide, deep,
    x_send, x_recv, i_send, i_recv, rt_send, rt_recv, rt_local, list_send, list_recv, obs_send, obs_recv,
    ret_send, ret_recv, ret_local, g_ssem, g_rsem, g_local, small_sem, pass_send, pass_recv,
):
    tile_i, tile_x, n_i, n_x, depth, steps, n_xline, fused = sizes
    rows = n_i * n_x
    small_in = (given_observed, given_cells, given_counts, given_src, given_wavelet)
    small_held = (held_observed, held_cells, held_counts, held_src, held_wavelet)
    slots = held_cells.shape[1]
    n_group = 2 * n_xline
    xl = lax.axis_index("xline")
    core = lax.axis_index("inline")
    me = xl * 2 + core
    y = lax.rem(xl, 2)
    plane = xl // 2
    z_odd = lax.rem(plane, 2)
    mate = xl + 1 - 2 * y
    cp = lax.rem(core + z_odd, 2)
    origin = y
    q = 2 * y + cp
    stays = y == core
    has = (xl >= 2, xl < n_xline - 2, q > 0, q < 3)
    other_core = 1 - core
    shot = lax.axis_index("shots")
    shares = (RHO, SPEED) if lax.axis_size("shots") == 2 else ()
    target = (
        {"xline": xl - 2, "inline": other_core},
        {"xline": xl + 2, "inline": other_core},
        {"xline": jnp.where(q == 2, mate, xl), "inline": other_core},
        {"xline": jnp.where(q == 1, mate, xl), "inline": other_core},
    )
    inner_i = pl.ds(4, n_i)
    inner_x = pl.ds(8, n_x)
    middle = n_i // 2

    barrier = pltpu.get_barrier_semaphore()

    def greet(device):
        pl.semaphore_signal(barrier, inc=1, device_id=device, device_id_type=MESH)

    near = n_xline // 2 <= 4
    if near:
        greet({"inline": other_core})
        greet({"xline": mate})
        greet({"xline": mate, "inline": other_core})
        for way in (LEFT, RIGHT):
            @pl.when(has[way])
            def _():
                greet(target[way])
        greeted = 3 + has[LEFT].astype(jnp.int32) + has[RIGHT].astype(jnp.int32)
    else:
        @pl.loop(1, n_group)
        def _(r):
            peer = lax.rem(me + r, n_group)
            greet({"xline": peer // 2, "inline": lax.rem(peer, 2)})
        greeted = n_group - 1
    if shares:
        greet({"shots": 1 - shot})
        greeted = greeted + 1

    small = [
        pltpu.make_async_copy(given, held, small_sem.at[n])
        for n, (given, held) in enumerate(zip(small_in, small_held))
    ]
    for copy in small:
        copy.start()
    observed, rec_cells, rec_counts, src_cell, wavelet = small_held

    layers = depth // 128
    half_x = n_x // 2

    def beside(idx, way, part, d):
        part_rows = pl.ds(part * middle, middle)
        return pltpu.make_async_remote_copy(
            src_ref=x_out.at[idx, way, d, part_rows], dst_ref=x_in.at[idx, 1 - way, d, part_rows],
            send_sem=x_send.at[idx, way, part, d], recv_sem=x_recv.at[idx, way, part, d],
            device_id=target[way], device_id_type=MESH,
        )

    def above(idx, part, c, d, arriving):
        up = part == 0
        return pltpu.make_async_remote_copy(
            src_ref=field.at[
                idx, pl.ds(4 + part * (n_i - 4), 4), pl.ds(8 + c * half_x, half_x), pl.ds(d * 128, 128)
            ],
            dst_ref=i_in.at[idx, part if arriving else 1 - part, d, c],
            send_sem=i_send.at[idx, part, c, d],
            recv_sem=i_recv.at[idx, 1 - part if arriving else part, c, d],
            device_id={
                "xline": jnp.where(up, target[UP]["xline"], target[DOWN]["xline"]), "inline": other_core
            },
            device_id_type=MESH,
        )

    def has_row(part):
        return jnp.where(part == 0, q, 3 - q) > 0

    def send(idx, part, d, c):
        @pl.when(has[c])
        def _():
            beside(idx, c, part, d).start()

        @pl.when(has_row(part))
        def _():
            above(idx, part, c, d, False).start()

    def finish(idx, part, d, c):
        @pl.when(has[c])
        def _():
            beside(idx, c, part, d).wait_send()
            beside(idx, 1 - c, part, d).wait_recv()

        @pl.when(has_row(part))
        def _():
            above(idx, part, c, d, False).wait_send()
            above(idx, part, c, d, True).wait_recv()

    def send_all(idx):
        for part, d, c in pieces:
            rows_at = pl.ds(part * middle, middle)
            x_out[idx, c, d, rows_at] = field[
                idx, pl.ds(4 + part * middle, middle), pl.ds(8 + c * (n_x - 4), 4), pl.ds(d * 128, 128)
            ]
            send(idx, part, d, c)

    halves = (1 - y, y)
    pieces = [(part, d, c) for part in halves for d in range(layers) for c in range(2)]

    sources = (log_density, fwd_now, velocity, fwd_before, adj_now, adj_before)
    places = (DENSITY, 0, None, 1, 2, 3)

    def landing(n, from_y):
        columns = pl.multiple_of(from_y * tile_x, tile_x)
        if n == SPEED:
            return vel.at[:, pl.ds(columns, tile_x), :]
        return field.at[places[n], inner_i, pl.ds(pl.multiple_of(8 + columns, 8), tile_x), :]

    def tile_copy(n, a):
        return pltpu.make_async_remote_copy(
            src_ref=sources[n].at[pl.ds(a * n_i, n_i)], dst_ref=landing(n, y),
            send_sem=rt_send.at[n, a], recv_sem=rt_recv.at[n, y],
            device_id={"xline": 2 * plane + core, "inline": lax.rem(a + z_odd, 2)},
            device_id_type=MESH,
        )

    def tile_arrival(n, from_y):
        return pltpu.make_async_remote_copy(
            src_ref=sources[n].at[pl.ds(0, n_i)], dst_ref=landing(n, from_y),
            send_sem=rt_send.at[n, 0], recv_sem=rt_recv.at[n, from_y],
            device_id={"xline": mate}, device_id_type=MESH,
        )

    def own_copy(n):
        return pltpu.make_async_copy(
            sources[n].at[pl.ds(cp * n_i, n_i)], landing(n, y), rt_local.at[n]
        )

    def leaves(a):
        return jnp.logical_not(jnp.logical_and(stays, cp == a))

    def arrives(from_y):
        return jnp.logical_not(jnp.logical_and(stays, y == from_y))

    def tile_start(n):
        for a in range(2):
            @pl.when(jnp.logical_and(stays, cp != a) if n in shares else leaves(a))
            def _():
                tile_copy(n, a).start()

        if n in shares:
            for a in range(2):
                @pl.when(jnp.logical_not(stays))
                def _():
                    half_copy(n, a).start()

        @pl.when(stays)
        def _():
            own_copy(n).start()

    def tile_finish(n):
        for from_y in range(2):
            @pl.when(jnp.logical_and(arrives(from_y), y == from_y) if n in shares else arrives(from_y))
            def _():
                tile_arrival(n, from_y).wait_recv()
        for a in range(2):
            @pl.when(jnp.logical_and(stays, cp != a) if n in shares else leaves(a))
            def _():
                tile_copy(n, a).wait_send()

        @pl.when(stays)
        def _():
            own_copy(n).wait()

        if n in shares:
            for a in range(2):
                @pl.when(jnp.logical_not(stays))
                def _():
                    half_copy(n, a).wait_send()
            pass_on(n).wait_send()
            passed_on(n).wait_recv()

    def half_landing(n, from_y, which):
        columns = pl.multiple_of(from_y * tile_x, tile_x)
        if n == SPEED:
            return vel.at[pl.ds(which * middle, middle), pl.ds(columns, tile_x), :]
        return field.at[
            places[n], pl.ds(4 + which * middle, middle), pl.ds(pl.multiple_of(8 + columns, 8), tile_x), :
        ]

    def half_copy(n, a):
        return pltpu.make_async_remote_copy(
            src_ref=sources[n].at[pl.ds(a * n_i + shot * middle, middle)], dst_ref=half_landing(n, y, shot),
            send_sem=rt_send.at[n, a], recv_sem=rt_recv.at[n, y],
            device_id={"xline": mate, "inline": lax.rem(a + z_odd, 2)}, device_id_type=MESH,
        )

    def half_arrival(n):
        return pltpu.make_async_remote_copy(
            src_ref=sources[n].at[pl.ds(0, middle)], dst_ref=half_landing(n, 1 - y, shot),
            send_sem=rt_send.at[n, 0], recv_sem=rt_recv.at[n, 1 - y],
            device_id={"xline": mate}, device_id_type=MESH,
        )

    def pass_on(n):
        return pltpu.make_async_remote_copy(
            src_ref=half_landing(n, 1 - y, shot), dst_ref=half_landing(n, 1 - y, shot),
            send_sem=pass_send.at[n], recv_sem=pass_recv.at[n],
            device_id={"shots": 1 - shot}, device_id_type=MESH,
        )

    def passed_on(n):
        return pltpu.make_async_remote_copy(
            src_ref=half_landing(n, 1 - y, shot), dst_ref=half_landing(n, 1 - y, 1 - shot),
            send_sem=pass_send.at[n], recv_sem=pass_recv.at[n],
            device_id={"shots": 1 - shot}, device_id_type=MESH,
        )

    def list_copy(a):
        return pltpu.make_async_remote_copy(
            src_ref=list_out, dst_ref=list_in.at[y],
            send_sem=list_send.at[a], recv_sem=list_recv.at[y],
            device_id={"xline": 2 * plane + core, "inline": lax.rem(a + z_odd, 2)},
            device_id_type=MESH,
        )

    def list_arrival(from_y):
        return pltpu.make_async_remote_copy(
            src_ref=list_out, dst_ref=list_in.at[from_y],
            send_sem=list_send.at[0], recv_sem=list_recv.at[from_y],
            device_id={"xline": mate}, device_id_type=MESH,
        )

    def obs_copy(peer, slot):
        return pltpu.make_async_remote_copy(
            src_ref=observed, dst_ref=obs_in.at[slot],
            send_sem=obs_send.at[peer], recv_sem=obs_recv.at[slot],
            device_id={"xline": peer // 2, "inline": lax.rem(peer, 2)}, device_id_type=MESH,
        )

    finals = (previous_out, last_out)
    final_idx = (2 + (steps - 1) % 2, 2 + steps % 2)

    def home_copy(n, to_y):
        return pltpu.make_async_remote_copy(
            src_ref=field.at[final_idx[n], inner_i, pl.ds(8 + to_y * tile_x, tile_x), :],
            dst_ref=finals[n].at[pl.ds(cp * n_i, n_i)],
            send_sem=ret_send.at[n, to_y], recv_sem=ret_recv.at[n, cp],
            device_id={"xline": 2 * plane + to_y, "inline": origin}, device_id_type=MESH,
        )

    def home_arrival(n, a):
        return pltpu.make_async_remote_copy(
            src_ref=field.at[final_idx[n], inner_i, pl.ds(8, tile_x), :],
            dst_ref=finals[n].at[pl.ds(a * n_i, n_i)],
            send_sem=ret_send.at[n, 0], recv_sem=ret_recv.at[n, a],
            device_id={"xline": mate}, device_id_type=MESH,
        )

    def home_own(n):
        columns = pl.multiple_of(8 + y * tile_x, 8)
        return pltpu.make_async_copy(
            field.at[final_idx[n], inner_i, pl.ds(columns, tile_x), :],
            finals[n].at[pl.ds(cp * n_i, n_i)], ret_local.at[n],
        )

    def home_start(n):
        for to_y in range(2):
            @pl.when(arrives(to_y))
            def _():
                home_copy(n, to_y).start()

        @pl.when(stays)
        def _():
            home_own(n).start()

    def home_finish(n):
        for to_y in range(2):
            @pl.when(arrives(to_y))
            def _():
                home_copy(n, to_y).wait_send()
        for a in range(2):
            @pl.when(leaves(a))
            def _():
                home_arrival(n, a).wait_recv()

        @pl.when(stays)
        def _():
            home_own(n).wait()

    dz = depth // n_xline
    planes_n = n_xline // 2

    def slab_copy(d):
        return pltpu.make_async_remote_copy(
            src_ref=g_send.at[d],
            dst_ref=grad_out.at[cp, :, pl.ds(pl.multiple_of(plane * n_x, 8), n_x), :],
            send_sem=g_ssem.at[d], recv_sem=g_rsem.at[cp, plane],
            device_id={"xline": d, "inline": origin}, device_id_type=MESH,
        )

    def own_slab():
        return pltpu.make_async_copy(
            g_send.at[xl], grad_out.at[cp, :, pl.ds(pl.multiple_of(plane * n_x, 8), n_x), :], g_local.at[0]
        )

    def slab_arrival(a, p):
        return pltpu.make_async_remote_copy(
            src_ref=g_send.at[0],
            dst_ref=grad_out.at[a, :, pl.ds(pl.multiple_of(p * n_x, 8), n_x), :],
            send_sem=g_ssem.at[0], recv_sem=g_rsem.at[a, p],
            device_id={"xline": mate}, device_id_type=MESH,
        )

    def fused_gradient():
        group = 128 // dz
        lane = div(lax.broadcasted_iota(jnp.int32, (n_x, 128), 1), dz)
        for chunk in range(depth // 128):
            for ig in range(n_i // group):
                planes = [image[ig * group + j, :, pl.ds(chunk * 128, 128)] for j in range(group)]
                for dd in range(group):
                    out = None
                    for j in range(group):
                        shift = (j - dd) * dz % 128
                        moved = pltpu.roll(planes[j], shift, axis=1) if shift else planes[j]
                        out = moved if out is None else jnp.where(lane == j, moved, out)
                    g_send[chunk * group + dd, ig] = out

        @pl.loop(1, n_xline + 1)
        def _(r):
            d = lax.rem(xl + r, n_xline)

            @pl.when(jnp.logical_or(d != xl, origin != core))
            def _():
                slab_copy(d).start()

        home_start(1)

        @pl.when(origin == core)
        def _():
            own_slab().start()

        @pl.loop(0, n_xline)
        def _(r):
            a, p = lax.rem(r, 2), r // 2
            mine = jnp.logical_and(origin == core, jnp.logical_and(a == cp, p == plane))

            @pl.when(jnp.logical_not(mine))
            def _():
                slab_arrival(a, p).wait_recv()

        @pl.when(origin == core)
        def _():
            own_slab().wait()

        @pl.loop(1, n_xline + 1)
        def _(r):
            d = lax.rem(xl + r, n_xline)

            @pl.when(jnp.logical_or(d != xl, origin != core))
            def _():
                slab_copy(d).wait_send()

    for idx in range(5):
        field[idx, pl.ds(0, 4)] = jnp.zeros((4,) + field.shape[2:], jnp.float32)
        field[idx, pl.ds(n_i + 4, 4)] = jnp.zeros((4,) + field.shape[2:], jnp.float32)
        field[idx, inner_i, pl.ds(0, 8)] = jnp.zeros((n_i, 8, depth), jnp.float32)
        field[idx, inner_i, pl.ds(8 + n_x, 8)] = jnp.zeros((n_i, 8, depth), jnp.float32)
    for way in (LEFT, RIGHT, UP, DOWN):
        @pl.when(jnp.logical_not(has[way]))
        def _():
            halo = x_in if way < UP else i_in
            halo[:, way % 2] = jnp.zeros(halo.shape[:1] + halo.shape[2:], jnp.float32)
    image[...] = jnp.zeros(image.shape, jnp.float32)

    for copy in small:
        copy.wait()
    n_counts = rec_counts.shape[1]
    spread = (
        div(lax.broadcasted_iota(jnp.int32, (n_counts, slots), 1), CAP)
        == lax.broadcasted_iota(jnp.int32, (n_counts, slots), 0)
    ).astype(jnp.float32).astype(jnp.bfloat16)
    counts = jnp.broadcast_to(rec_counts[...].astype(jnp.float32), (8, n_counts)).astype(jnp.bfloat16)
    live = dot(counts, spread)
    place = mod(lax.broadcasted_iota(jnp.int32, (8, slots), 1), CAP).astype(jnp.float32)
    list_out[...] = jnp.where(place < live, jnp.broadcast_to(rec_cells[...], (8, slots)), -1)

    pl.semaphore_wait(barrier, greeted)

    for a in range(2):
        @pl.when(leaves(a))
        def _():
            list_copy(a).start()

    for n in (RHO, SPEED, NOW):
        tile_start(n)
    tile_start(BEFORE)

    obs_in[me] = observed[...]

    @pl.when(stays)
    def _():
        list_in[y] = list_out[...]

    offset = lax.broadcasted_iota(jnp.int32, (depth, depth), 0) - lax.broadcasted_iota(jnp.int32, (depth, depth), 1)
    second = jnp.zeros((depth, depth), jnp.float32)
    first = jnp.zeros((depth, depth), jnp.float32)
    for k in range(1, 5):
        second = jnp.where((offset == k) | (offset == -k), SECOND_COEFFS[k] / SECOND_COEFFS[1], second)
        first = jnp.where(offset == k, FIRST_COEFFS[k - 1] / FIRST_COEFFS[0], first)
        first = jnp.where(offset == -k, -FIRST_COEFFS[k - 1] / FIRST_COEFFS[0], first)
    z_mat[:, pl.ds(0, depth)] = second.astype(jnp.bfloat16)
    z_mat[:, pl.ds(depth, depth)] = first.astype(jnp.bfloat16)

    at = lax.broadcasted_iota(jnp.int32, (rows, rows), 0)
    to = lax.broadcasted_iota(jnp.int32, (rows, rows), 1)
    step_i = div(to, n_x) - div(at, n_x)
    step_x = mod(to, n_x) - mod(at, n_x)
    lateral_lap = jnp.zeros((rows, rows), jnp.float32)
    for n, (along, still) in enumerate(((step_i, step_x), (step_x, step_i))):
        along = jnp.where(still == 0, along, 0)
        first = jnp.zeros((rows, rows), jnp.float32)
        for k in range(1, 5):
            lateral_lap = jnp.where((along == k) | (along == -k), SECOND_COEFFS[k] / SECOND_COEFFS[1], lateral_lap)
            first = jnp.where(along == k, FIRST_COEFFS[k - 1] / FIRST_COEFFS[0], first)
            first = jnp.where(along == -k, -FIRST_COEFFS[k - 1] / FIRST_COEFFS[0], first)
        row_mat[pl.ds((n + 1) * rows, rows), :] = first.astype(jnp.bfloat16)
    row_mat[pl.ds(0, rows), :] = lateral_lap.astype(jnp.bfloat16)

    full_x = tile_x * n_xline
    cells = src_cell[...]
    src_i = div(cells, full_x * depth) - q * n_i
    src_x = mod(div(cells, depth), full_x) - plane * n_x
    inside = (src_i >= 0) & (src_i < n_i) & (src_x >= 0) & (src_x < n_x)
    src_row = jnp.where(inside, src_i * n_x + src_x, -1)
    n_src = cells.shape[1]
    src_rows = (lax.broadcasted_iota(jnp.int32, (rows, n_src), 0) == src_row).astype(jnp.float32)
    src_cols = (lax.broadcasted_iota(jnp.int32, (depth, n_src), 0) == mod(cells, depth)).astype(jnp.float32).astype(jnp.bfloat16)

    def flat(idx):
        return field[idx, inner_i, inner_x, :].reshape(rows, depth)

    def differences(idx):
        high, low = split_bf16(flat(idx))
        wide[...] = dot(row_mat[...], high) + dot(row_mat[...], low)
        deep[...] = dot(high, z_mat[...]) + dot(low, z_mat[...])

    def operator(idx, i):
        def line(n):
            return pl.ds(pl.multiple_of(n * rows + i * n_x, n_x), n_x)

        center = field[idx, i + 4, inner_x, :]
        return center, (
            3.0 * SECOND_COEFFS[0] * center
            + SECOND_COEFFS[1] * (wide[line(0), :] + deep[line(0), pl.ds(0, depth)])
            - slopes[0, i] * wide[line(1), :] - slopes[1, i] * wide[line(2), :]
            - slopes[2, i] * deep[line(0), pl.ds(depth, depth)]
        )

    def across(idx, i):
        lap = slope_i = slope_x = None
        for k in range(1, 5):
            plus_i = field[idx, i + 4 + k, inner_x, :]
            minus_i = field[idx, i + 4 - k, inner_x, :]
            plus_x = field[idx, i + 4, pl.ds(8 + k, n_x), :]
            minus_x = field[idx, i + 4, pl.ds(8 - k, n_x), :]
            terms = (
                SECOND_COEFFS[k] * ((plus_i + minus_i) + (plus_x + minus_x)),
                FIRST_COEFFS[k - 1] * (plus_i - minus_i),
                FIRST_COEFFS[k - 1] * (plus_x - minus_x),
            )
            if lap is None:
                lap, slope_i, slope_x = terms
            else:
                lap, slope_i, slope_x = lap + terms[0], slope_i + terms[1], slope_x + terms[2]
        return lap, slope_i, slope_x

    for n in shares:
        half_arrival(n).wait_recv()
        pass_on(n).start()
    tile_finish(RHO)
    send_all(DENSITY)
    tile_finish(NOW)
    send_all(0)

    high, low = split_bf16(flat(DENSITY))
    deep[...] = dot(high, z_mat[...]) + dot(low, z_mat[...])
    slopes[2] = ((FIRST_COEFFS[0] * FIRST_COEFFS[0]) * deep[:, pl.ds(depth, depth)]).reshape(n_i, n_x, depth)
    differences(0)

    def inject_sources(t):
        high, low = split_bf16(src_rows * wavelet[pl.ds(t, 1), :])
        return dot_nt(high, src_cols) + dot_nt(low, src_cols)

    accel[0] = inject_sources(0).reshape(n_i, n_x, depth)

    for part, d, c in pieces:
        finish(DENSITY, part, d, c)
    for d in range(layers):
        lanes = pl.ds(d * 128, 128)
        for side in range(2):
            for c in range(2):
                field[DENSITY, pl.ds(side * (n_i + 4), 4), pl.ds(8 + c * half_x, half_x), lanes] = i_in[DENSITY, side, d, c]
            field[DENSITY, inner_i, pl.ds(4 + side * (n_x + 4), 4), lanes] = x_in[DENSITY, side, d]

    @pl.loop(0, n_i)
    def _(i):
        _, slope_i, slope_x = across(DENSITY, i)
        slopes[0, i] = FIRST_COEFFS[0] * slope_i
        slopes[1, i] = FIRST_COEFFS[0] * slope_x

    tile_finish(SPEED)
    column = lax.broadcasted_iota(jnp.int32, (n_x, depth), 0)

    @pl.loop(0, n_i)
    def _(i):
        square = vel[i] * vel[i]
        speed_sq[i] = square
        accel[0, i] += square * operator(0, i)[1]
        for k in range(1, 5):
            weight = jnp.where(
                column < k, SECOND_COEFFS[k] + (FIRST_COEFFS[k - 1] / FIRST_COEFFS[0]) * slopes[1, i],
                jnp.where(
                    column >= n_x - k, SECOND_COEFFS[k] - (FIRST_COEFFS[k - 1] / FIRST_COEFFS[0]) * slopes[1, i], 0.0
                ),
            )
            wx[k - 1, i] = square * weight

    tile_finish(BEFORE)

    @pl.loop(0, n_i)
    def _(i):
        field[1, i + 4, inner_x, :] = (
            2.0 * field[0, i + 4, inner_x, :] - field[1, i + 4, inner_x, :] + accel[0, i]
        )

    def make_maps():
        for from_y in range(2):
            @pl.when(arrives(from_y))
            def _():
                list_arrival(from_y).wait_recv()
        for a in range(2):
            @pl.when(leaves(a))
            def _():
                list_copy(a).wait_send()
        for from_y in range(2):
            spot = list_in[from_y][:1]
            cell_i = div(spot, tile_x * depth) - cp * n_i
            cell_x = mod(div(spot, depth), tile_x) + from_y * tile_x
            row = jnp.where((spot >= 0) & (cell_i >= 0) & (cell_i < n_i), cell_i * n_x + cell_x, -1)
            columns = pl.ds(from_y * slots, slots)
            row_map[:, columns] = (lax.broadcasted_iota(jnp.int32, (rows, slots), 0) == row).astype(jnp.float32)
            zmap_t[:, columns] = (
                lax.broadcasted_iota(jnp.int32, (depth, slots), 0) == mod(spot, depth)
            ).astype(jnp.float32).astype(jnp.bfloat16)

    def make_traces():
        @pl.loop(1, n_group)
        def _(r):
            peer = lax.rem(me + r, n_group)
            obs_copy(peer, peer).wait_recv()
            obs_copy(peer, me).wait_send()

        lane = div(lax.broadcasted_iota(jnp.int32, (8, slots), 1), CAP)
        for from_y in range(2):
            owner = (2 * plane + from_y) * 2 + origin

            def place_one(s, total):
                moved = pltpu.roll(obs_in[s], lax.rem(s - owner + n_group, n_group) * CAP, axis=1)
                return jnp.where(lane == s, moved, total)

            traces[:, pl.ds(from_y * slots, slots)] = lax.fori_loop(
                0, n_group, place_one, jnp.zeros((8, slots), jnp.float32)
            )

    def prepare(idx, term):
        base[...] = term.reshape(n_i, n_x, depth)
        differences(idx)

    def interior(now, other, i):
        center, value = operator(now, i)
        change = base[i] + speed_sq[i] * value
        field[other, i + 4, inner_x, :] = 2.0 * center - field[other, i + 4, inner_x, :] + change
        return center, change

    def correct(now, other, part, d, c, t):
        up = part == 0
        sign = jnp.where(up, 1.0, -1.0)
        columns, lanes = pl.ds(c * half_x, half_x), pl.ds(d * 128, 128)
        for r in range(middle):
            i = jnp.where(up, r, n_i - 1 - r)
            halo = x_in[now, c, d, i]
            pair = jnp.concatenate([halo] * (half_x // 4), axis=0)
            change = wx[3, i, columns, lanes] * pair
            for k in range(1, 4):
                change += wx[k - 1, i, columns, lanes] * pltpu.roll(pair, half_x - k if c else k, axis=0)
            lap = None
            for h in range(4 - r):
                k = r + 1 + h
                halo = i_in[now, part, d, c, jnp.where(up, 3 - h, h)]
                terms = SECOND_COEFFS[k] * halo, (FIRST_COEFFS[k - 1] / FIRST_COEFFS[0]) * halo
                lap, slope = terms if lap is None else (lap + terms[0], slope + terms[1])
            if lap is not None:
                change += speed_sq[i, columns, lanes] * (lap + (sign * slopes[0, i, columns, lanes]) * slope)
            spot = (other, i + 4, pl.ds(8 + c * half_x, half_x), lanes)
            fresh = field[spot] + change
            field[spot] = fresh
            x_out[other, c, d, i] = fresh[half_x - 4:] if c else fresh[:4]
            if t is not None:
                accel[t, i, columns, lanes] += change

    def sample(idx, t):
        high, low = split_bf16(flat(idx))
        picked = dot(high, zmap_t[...]) + dot(low, zmap_t[...])
        predicted = jnp.sum(picked * row_map[...], axis=0, keepdims=True)
        residual_ref[t] = predicted

    def task_now():
        tile_start(ADJ_NOW)
        make_maps()

    def task_before():
        tile_start(ADJ_BEFORE)

    def task_traces():
        @pl.loop(1, n_group)
        def _(r):
            obs_copy(lax.rem(me + r, n_group), me).start()

    def task_halos():
        tile_finish(ADJ_NOW)
        send_all(2)

    def task_adjoint():
        tile_finish(ADJ_BEFORE)
        differences(2)

        @pl.loop(0, n_i, unroll=2)
        def _(i):
            center, value = operator(2, i)
            field[3, i + 4, inner_x, :] = (
                2.0 * center - field[3, i + 4, inner_x, :] + speed_sq[i] * value
            )

    tasks = [task_now, task_before, task_traces, task_halos, task_adjoint, make_traces]
    times = [1 + n * (steps - 2) // len(tasks) for n in range(len(tasks))]

    @pl.loop(0, steps)
    def _(t):
        now = lax.rem(t, 2)
        other = 1 - now

        @pl.when(t > 0)
        def _():
            prepare(now, inject_sources(t))

            @pl.loop(0, n_i, unroll=2)
            def _(i):
                _, change = interior(now, other, i)
                accel[t, i] = change

        for at, task in zip(times, tasks):
            pl.when(t == at)(task)

        @pl.when(t >= 1)
        def _():
            sample(now, t - 1)

        for part, d, c in pieces:
            finish(now, part, d, c)
            correct(now, other, part, d, c, t)

            @pl.when(t < steps - 1)
            def _():
                send(other, part, d, c)

    sample(steps % 2, steps - 1)

    @pl.loop(0, steps)
    def _(j):
        now = 2 + lax.rem(j, 2)
        other = 5 - now
        t = steps - 1 - j
        high, low = split_bf16(row_map[...] * (residual_ref[t] - traces[pl.ds(t, 1), :]))
        injected = dot_nt(high, zmap_t[...]) + dot_nt(low, zmap_t[...])

        @pl.when(j == 0)
        def _():
            field[3, inner_i, inner_x, :] += injected.reshape(n_i, n_x, depth)

        @pl.when(j > 0)
        def _():
            prepare(now, injected)

            @pl.loop(0, n_i, unroll=2)
            def _(i):
                center, _ = interior(now, other, i)
                image[i] += center * accel[t + 1, i]

        @pl.when(j == steps - 1)
        def _():
            home_start(0)

        for part, d, c in pieces:
            finish(now, part, d, c)
            correct(now, other, part, d, c, None)

            @pl.when(j < steps - 1)
            def _():
                send(other, part, d, c)

    @pl.loop(0, n_i)
    def _(i):
        total = image[i] + field[final_idx[1], i + 4, inner_x, :] * accel[0, i]
        image[i] = total * (2.0 / steps) / vel[i]

    if fused:
        fused_gradient()
    else:
        grad_out[...] = image[...]
        home_start(1)
    home_finish(0)
    home_finish(1)


def finish_kernel(shape, slabs, last, previous):
    dz, tile_i, full_x = shape
    _, n_groups, _, lanes = slabs.shape
    group = lanes // dz

    def kernel(slabs_in, last_in, previous_in, gradient, last_out, previous_out, sem):
        copies = [
            pltpu.make_async_copy(last_in, last_out, sem.at[0]),
            pltpu.make_async_copy(previous_in, previous_out, sem.at[1]),
        ]
        for copy in copies:
            copy.start()
        far = (
            lax.broadcasted_iota(jnp.int32, (full_x, full_x), 0) - lax.broadcasted_iota(jnp.int32, (full_x, full_x), 1)
        ).astype(jnp.float32)
        weights = jnp.exp(-jnp.abs(far) / SMOOTH)
        weights = weights / jnp.sum(weights, axis=0, keepdims=True)
        for a in range(2):
            for ig in range(n_groups):
                lines = dot_tn_exact(slabs_in[a, ig], weights)
                for j in range(group):
                    gradient[:, (a * n_groups + ig) * group + j, :] = lines[j * dz:(j + 1) * dz]
        for copy in copies:
            copy.wait()

    vmem = pl.BlockSpec(memory_space=pltpu.VMEM)
    anywhere = pl.BlockSpec(memory_space=pl.ANY)
    return pl.pallas_call(
        kernel,
        out_shape=[jax.ShapeDtypeStruct(dims, jnp.float32) for dims in (shape, last.shape, previous.shape)],
        in_specs=[vmem] * 3,
        out_specs=[vmem, anywhere, anywhere],
        scratch_shapes=[pltpu.SemaphoreType.DMA((2,))],
    )(slabs, last, previous)


def per_device(
    fwd_now, fwd_before, adj_now, adj_before, velocity, log_density,
    observed, rec_cells, rec_counts, src_cell, wavelet,
):
    tile_i, tile_x, depth = fwd_now.shape
    steps = wavelet.shape[0]
    n_xline = lax.axis_size("xline")
    full_x = tile_x * n_xline
    n_i, n_x = tile_i // 2, tile_x * 2
    rows = n_i * n_x
    slots = rec_cells.shape[1]
    n_group = 2 * n_xline
    dz = depth // n_xline
    fused = dz >= 8 and 128 % dz == 0 and depth % 128 == 0 and n_i % (128 // dz) == 0
    group = 128 // dz if fused else 1
    layers = depth // 128

    block = (n_i, n_x, depth)
    vmem = pl.BlockSpec(memory_space=pltpu.VMEM)
    anywhere = pl.BlockSpec(memory_space=pl.ANY)
    dma = pltpu.SemaphoreType.DMA
    kernel = functools.partial(wave_kernel, (tile_i, tile_x, n_i, n_x, depth, steps, n_xline, fused))
    grad_shape = (2, n_i // group, full_x, 128) if fused else block
    slab_shape = (n_xline, n_i // group, n_x, 128) if fused else (8, 128)
    small_shapes = [observed, rec_cells, rec_counts, src_cell[None, :], wavelet]
    raw, last, previous = pl.pallas_call(
        kernel,
        out_shape=[
            jax.ShapeDtypeStruct(grad_shape, jnp.float32),
            jax.ShapeDtypeStruct(fwd_now.shape, jnp.float32),
            jax.ShapeDtypeStruct(fwd_now.shape, jnp.float32),
        ],
        in_specs=[anywhere] * 11,
        out_specs=[anywhere if fused else vmem, anywhere, anywhere],
        scratch_shapes=[
            pltpu.VMEM((5, n_i + 8, n_x + 16, depth), jnp.float32),
            pltpu.VMEM(block, jnp.float32),
            pltpu.VMEM((5, 2, layers, n_i, 4, 128), jnp.float32),
            pltpu.VMEM((5, 2, layers, n_i, 4, 128), jnp.float32),
            pltpu.VMEM((5, 2, layers, 2, 4, tile_x, 128), jnp.float32),
            pltpu.VMEM((steps,) + block, jnp.float32),
            pltpu.VMEM(block, jnp.float32),
            pltpu.VMEM(block, jnp.float32),
            pltpu.VMEM((3,) + block, jnp.float32),
            pltpu.VMEM(block, jnp.float32),
            pltpu.VMEM((4,) + block, jnp.float32),
            pltpu.VMEM((rows, 2 * slots), jnp.float32),
            pltpu.VMEM((depth, 2 * slots), jnp.bfloat16),
            pltpu.VMEM((depth, 2 * depth), jnp.bfloat16),
            pltpu.VMEM((steps, 1, 2 * slots), jnp.float32),
            pltpu.VMEM((steps, 2 * slots), jnp.float32),
            pltpu.VMEM((8, slots), jnp.int32),
            pltpu.VMEM((2, 8, slots), jnp.int32),
            pltpu.VMEM((n_group,) + observed.shape, jnp.float32),
            pltpu.VMEM(slab_shape, jnp.float32),
            *[pltpu.VMEM(value.shape, value.dtype) for value in small_shapes],
            pltpu.VMEM((3 * rows, rows), jnp.bfloat16),
            pltpu.VMEM((3 * rows, depth), jnp.float32),
            pltpu.VMEM((rows, 2 * depth), jnp.float32),
            *[dma((5, 2, 2, layers)) for _ in range(4)],
            dma((6, 2)), dma((6, 2)), dma((6,)),
            dma((2,)), dma((2,)),
            dma((n_group,)), dma((n_group,)),
            dma((2, 2)), dma((2, 2)), dma((2,)),
            dma((n_xline,)), dma((2, n_xline // 2)), dma((1,)), dma((5,)),
            dma((6,)), dma((6,)),
        ],
        compiler_params=pltpu.CompilerParams(
            collective_id=0, has_side_effects=True, vmem_limit_bytes=56 * 1024 * 1024
        ),
    )(
        log_density, fwd_now, velocity, fwd_before, adj_now, adj_before,
        *small_shapes,
    )
    if fused:
        return finish_kernel((dz, tile_i, full_x), raw, last, previous)

    places = []
    for xl in range(n_xline):
        for core in range(2):
            y, plane = xl % 2, xl // 2
            cp = (core + plane % 2) % 2
            places.append((xl * 2 + core, (2 * plane + cp) * 2 + y))
    raw = lax.ppermute(raw, ("xline", "inline"), places)
    columns = lax.all_to_all(
        raw.reshape(n_i, n_x, n_xline, dz).transpose(2, 0, 1, 3),
        "xline", split_axis=0, concat_axis=0, tiled=True,
    ).reshape(n_xline // 2, 2, n_i, n_x, dz)
    positions = jnp.arange(full_x).astype(jnp.float32)
    weights = jnp.exp(-jnp.abs(positions[:, None] - positions[None, :]) / SMOOTH)
    weights = weights / jnp.sum(weights, axis=1, keepdims=True)
    gradient = jnp.einsum(
        "phixz,ypx->zhiy", columns, weights.reshape(full_x, n_xline // 2, n_x),
        precision=lax.Precision.HIGHEST,
    ).reshape(dz, tile_i, full_x)
    return gradient, last, previous


def solution(mesh):
    return jax.shard_map(
        per_device,
        mesh=mesh,
        in_specs=(
            P(("shots", "inline"), "xline", None),
            P(("shots", "inline"), "xline", None),
            P(("shots", "inline"), "xline", None),
            P(("shots", "inline"), "xline", None),
            P("inline", "xline", None),
            P("inline", "xline", None),
            P("shots", ("xline", "inline")),
            P(("xline", "inline"), None),
            P(("xline", "inline"), None),
            P("shots"),
            P("shots", None),
        ),
        out_specs=(
            P(("shots", "xline"), "inline", None),
            P(("shots", "inline"), "xline", None),
            P(("shots", "inline"), "xline", None),
        ),
        check_vma=False,
    )
```

```python
import functools

import jax
import jax.numpy as jnp
from jax import lax
from jax.experimental import pallas as pl
from jax.experimental.pallas import tpu as pltpu
from jax.sharding import PartitionSpec as P

CAP = 8
SMOOTH = 16
MESH = pl.DeviceIdType.MESH

SECOND_COEFFS = (-205.0 / 72.0, 8.0 / 5.0, -1.0 / 5.0, 8.0 / 315.0, -1.0 / 560.0)
FIRST_COEFFS = (4.0 / 5.0, -1.0 / 5.0, 4.0 / 105.0, -1.0 / 280.0)
LEFT, RIGHT, UP, DOWN = 0, 1, 2, 3
DENSITY = 4
RHO, NOW, SPEED, BEFORE, ADJ_NOW, ADJ_BEFORE = range(6)


def split_bf16(value):
    high = value.astype(jnp.bfloat16)
    low = (value - high.astype(jnp.float32)).astype(jnp.bfloat16)
    return high, low


def dot(a, b):
    return jnp.dot(a, b, preferred_element_type=jnp.float32)


def dot_nt(a, b):
    return lax.dot_general(a, b, (((1,), (1,)), ((), ())), preferred_element_type=jnp.float32)


def dot_tn_exact(a, b):
    dims = (((0,), (0,)), ((), ()))
    ah, al = split_bf16(a)
    bh, bl = split_bf16(b)
    one = lax.dot_general(ah, bh, dims, preferred_element_type=jnp.float32)
    two = lax.dot_general(al, bh, dims, preferred_element_type=jnp.float32)
    three = lax.dot_general(ah, bl, dims, preferred_element_type=jnp.float32)
    return one + (two + three)


def div(value, n):
    return lax.shift_right_arithmetic(value, jnp.full_like(value, n.bit_length() - 1))


def mod(value, n):
    return value & (n - 1)


def wave_kernel(
    sizes,
    log_density, fwd_now, velocity, fwd_before, adj_now, adj_before,
    given_observed, given_cells, given_counts, given_src, given_wavelet,
    grad_out, last_out, previous_out,
    field, vel, x_in, x_out, i_in, i_out, accel, base, image, slopes, speed_sq, wx,
    row_map, zmap_t, z_mat, residual_ref, traces, list_out, list_in, obs_in, g_send,
    held_observed, held_cells, held_counts, held_src, held_wavelet, row_mat, wide, deep,
    x_send, x_recv, i_send, i_recv, rt_send, rt_recv, rt_local, list_send, list_recv, obs_send, obs_recv,
    ret_send, ret_recv, ret_local, g_ssem, g_rsem, g_local, small_sem, pass_send, pass_recv,
):
    tile_i, tile_x, n_i, n_x, depth, steps, n_xline, fused = sizes
    rows = n_i * n_x
    small_in = (given_observed, given_cells, given_counts, given_src, given_wavelet)
    small_held = (held_observed, held_cells, held_counts, held_src, held_wavelet)
    slots = held_cells.shape[1]
    n_group = 2 * n_xline
    xl = lax.axis_index("xline")
    core = lax.axis_index("inline")
    me = xl * 2 + core
    y = lax.rem(xl, 2)
    plane = xl // 2
    z_odd = lax.rem(plane, 2)
    mate = xl + 1 - 2 * y
    cp = lax.rem(core + z_odd, 2)
    origin = y
    q = 2 * y + cp
    stays = y == core
    has = (xl >= 2, xl < n_xline - 2, q > 0, q < 3)
    other_core = 1 - core
    shot = lax.axis_index("shots")
    shares = (RHO, SPEED) if lax.axis_size("shots") == 2 else ()
    target = (
        {"xline": xl - 2, "inline": other_core},
        {"xline": xl + 2, "inline": other_core},
        {"xline": jnp.where(q == 2, mate, xl), "inline": other_core},
        {"xline": jnp.where(q == 1, mate, xl), "inline": other_core},
    )
    inner_i = pl.ds(4, n_i)
    inner_x = pl.ds(8, n_x)
    middle = n_i // 2

    barrier = pltpu.get_barrier_semaphore()

    def greet(device):
        pl.semaphore_signal(barrier, inc=1, device_id=device, device_id_type=MESH)

    near = n_xline // 2 <= 4
    if near:
        greet({"inline": other_core})
        greet({"xline": mate})
        greet({"xline": mate, "inline": other_core})
        for way in (LEFT, RIGHT):
            @pl.when(has[way])
            def _():
                greet(target[way])
        greeted = 3 + has[LEFT].astype(jnp.int32) + has[RIGHT].astype(jnp.int32)
    else:
        @pl.loop(1, n_group)
        def _(r):
            peer = lax.rem(me + r, n_group)
            greet({"xline": peer // 2, "inline": lax.rem(peer, 2)})
        greeted = n_group - 1
    if shares:
        greet({"shots": 1 - shot})
        greeted = greeted + 1

    small = [
        pltpu.make_async_copy(given, held, small_sem.at[n])
        for n, (given, held) in enumerate(zip(small_in, small_held))
    ]
    for copy in small:
        copy.start()
    observed, rec_cells, rec_counts, src_cell, wavelet = small_held

    layers = depth // 128
    half_x = n_x // 2

    def beside(idx, way, part, d):
        part_rows = pl.ds(part * middle, middle)
        return pltpu.make_async_remote_copy(
            src_ref=x_out.at[idx, way, d, part_rows], dst_ref=x_in.at[idx, 1 - way, d, part_rows],
            send_sem=x_send.at[idx, way], recv_sem=x_recv.at[idx, way, part, d],
            device_id=target[way], device_id_type=MESH,
        )

    def above(idx, part, c, d, arriving):
        up = part == 0
        return pltpu.make_async_remote_copy(
            src_ref=i_out.at[idx, part, d, c],
            dst_ref=i_in.at[idx, part if arriving else 1 - part, d, c],
            send_sem=i_send.at[idx, part],
            recv_sem=i_recv.at[idx, 1 - part if arriving else part, c, d],
            device_id={
                "xline": jnp.where(up, target[UP]["xline"], target[DOWN]["xline"]), "inline": other_core
            },
            device_id_type=MESH,
        )

    def has_row(part):
        return jnp.where(part == 0, q, 3 - q) > 0

    def send(idx, part, d, c):
        @pl.when(has[c])
        def _():
            beside(idx, c, part, d).start()

        @pl.when(has_row(part))
        def _():
            above(idx, part, c, d, False).start()

    def finish(idx, part, d, c):
        @pl.when(has[c])
        def _():
            beside(idx, 1 - c, part, d).wait_recv()

        @pl.when(has_row(part))
        def _():
            above(idx, part, c, d, True).wait_recv()

    def sent(idx):
        for n in range(2):
            @pl.when(has[n])
            def _():
                pltpu.make_async_remote_copy(
                    src_ref=x_out.at[idx, n], dst_ref=x_in.at[idx, 1 - n],
                    send_sem=x_send.at[idx, n], recv_sem=x_recv.at[idx, n, 0, 0],
                    device_id=target[n], device_id_type=MESH,
                ).wait_send()

            @pl.when(has[UP + n])
            def _():
                pltpu.make_async_remote_copy(
                    src_ref=i_out.at[idx, n], dst_ref=i_in.at[idx, 1 - n],
                    send_sem=i_send.at[idx, n], recv_sem=i_recv.at[idx, n, 0, 0],
                    device_id=target[UP + n], device_id_type=MESH,
                ).wait_send()

    def send_all(idx):
        for part, d, c in pieces:
            rows_at = pl.ds(part * middle, middle)
            x_out[idx, c, d, rows_at] = field[
                idx, pl.ds(4 + part * middle, middle), pl.ds(8 + c * (n_x - 4), 4), pl.ds(d * 128, 128)
            ]
            i_out[idx, part, d, c] = field[
                idx, pl.ds(4 + part * (n_i - 4), 4), pl.ds(8 + c * half_x, half_x), pl.ds(d * 128, 128)
            ]
            send(idx, part, d, c)

    halves = (1 - y, y)
    pieces = [(part, d, c) for part in halves for d in range(layers) for c in range(2)]

    sources = (log_density, fwd_now, velocity, fwd_before, adj_now, adj_before)
    places = (DENSITY, 0, None, 1, 2, 3)

    def landing(n, from_y):
        columns = pl.multiple_of(from_y * tile_x, tile_x)
        if n == SPEED:
            return vel.at[:, pl.ds(columns, tile_x), :]
        return field.at[places[n], inner_i, pl.ds(pl.multiple_of(8 + columns, 8), tile_x), :]

    def tile_copy(n, a):
        return pltpu.make_async_remote_copy(
            src_ref=sources[n].at[pl.ds(a * n_i, n_i)], dst_ref=landing(n, y),
            send_sem=rt_send.at[n, a], recv_sem=rt_recv.at[n, y],
            device_id={"xline": 2 * plane + core, "inline": lax.rem(a + z_odd, 2)},
            device_id_type=MESH,
        )

    def tile_arrival(n, from_y):
        return pltpu.make_async_remote_copy(
            src_ref=sources[n].at[pl.ds(0, n_i)], dst_ref=landing(n, from_y),
            send_sem=rt_send.at[n, 0], recv_sem=rt_recv.at[n, from_y],
            device_id={"xline": mate}, device_id_type=MESH,
        )

    def own_copy(n):
        return pltpu.make_async_copy(
            sources[n].at[pl.ds(cp * n_i, n_i)], landing(n, y), rt_local.at[n]
        )

    def leaves(a):
        return jnp.logical_not(jnp.logical_and(stays, cp == a))

    def arrives(from_y):
        return jnp.logical_not(jnp.logical_and(stays, y == from_y))

    def tile_start(n):
        for a in range(2):
            @pl.when(jnp.logical_and(stays, cp != a) if n in shares else leaves(a))
            def _():
                tile_copy(n, a).start()

        if n in shares:
            for a in range(2):
                @pl.when(jnp.logical_not(stays))
                def _():
                    half_copy(n, a).start()

        @pl.when(stays)
        def _():
            own_copy(n).start()

    def tile_finish(n):
        for from_y in range(2):
            @pl.when(jnp.logical_and(arrives(from_y), y == from_y) if n in shares else arrives(from_y))
            def _():
                tile_arrival(n, from_y).wait_recv()
        for a in range(2):
            @pl.when(jnp.logical_and(stays, cp != a) if n in shares else leaves(a))
            def _():
                tile_copy(n, a).wait_send()

        @pl.when(stays)
        def _():
            own_copy(n).wait()

        if n in shares:
            for a in range(2):
                @pl.when(jnp.logical_not(stays))
                def _():
                    half_copy(n, a).wait_send()
            pass_on(n).wait_send()
            passed_on(n).wait_recv()

    def quarter_start(n, which):
        for a in range(2):
            @pl.when(leaves(a))
            def _():
                pltpu.make_async_remote_copy(
                    src_ref=sources[n].at[pl.ds(a * n_i + which * middle, middle)], dst_ref=half_landing(n, y, which),
                    send_sem=rt_send.at[n, a], recv_sem=rt_recv.at[n, y],
                    device_id={"xline": 2 * plane + core, "inline": lax.rem(a + z_odd, 2)},
                    device_id_type=MESH,
                ).start()

        if which == 0:
            @pl.when(stays)
            def _():
                own_copy(n).start()

    def half_landing(n, from_y, which):
        columns = pl.multiple_of(from_y * tile_x, tile_x)
        if n == SPEED:
            return vel.at[pl.ds(which * middle, middle), pl.ds(columns, tile_x), :]
        return field.at[
            places[n], pl.ds(4 + which * middle, middle), pl.ds(pl.multiple_of(8 + columns, 8), tile_x), :
        ]

    def half_copy(n, a):
        return pltpu.make_async_remote_copy(
            src_ref=sources[n].at[pl.ds(a * n_i + shot * middle, middle)], dst_ref=half_landing(n, y, shot),
            send_sem=rt_send.at[n, a], recv_sem=rt_recv.at[n, y],
            device_id={"xline": mate, "inline": lax.rem(a + z_odd, 2)}, device_id_type=MESH,
        )

    def half_arrival(n):
        return pltpu.make_async_remote_copy(
            src_ref=sources[n].at[pl.ds(0, middle)], dst_ref=half_landing(n, 1 - y, shot),
            send_sem=rt_send.at[n, 0], recv_sem=rt_recv.at[n, 1 - y],
            device_id={"xline": mate}, device_id_type=MESH,
        )

    def pass_on(n):
        return pltpu.make_async_remote_copy(
            src_ref=half_landing(n, 1 - y, shot), dst_ref=half_landing(n, 1 - y, shot),
            send_sem=pass_send.at[n], recv_sem=pass_recv.at[n],
            device_id={"shots": 1 - shot}, device_id_type=MESH,
        )

    def passed_on(n):
        return pltpu.make_async_remote_copy(
            src_ref=half_landing(n, 1 - y, shot), dst_ref=half_landing(n, 1 - y, 1 - shot),
            send_sem=pass_send.at[n], recv_sem=pass_recv.at[n],
            device_id={"shots": 1 - shot}, device_id_type=MESH,
        )

    def list_copy(a):
        return pltpu.make_async_remote_copy(
            src_ref=list_out, dst_ref=list_in.at[y],
            send_sem=list_send.at[a], recv_sem=list_recv.at[y],
            device_id={"xline": 2 * plane + core, "inline": lax.rem(a + z_odd, 2)},
            device_id_type=MESH,
        )

    def list_arrival(from_y):
        return pltpu.make_async_remote_copy(
            src_ref=list_out, dst_ref=list_in.at[from_y],
            send_sem=list_send.at[0], recv_sem=list_recv.at[from_y],
            device_id={"xline": mate}, device_id_type=MESH,
        )

    def obs_copy(peer, slot):
        return pltpu.make_async_remote_copy(
            src_ref=observed, dst_ref=obs_in.at[slot],
            send_sem=obs_send.at[peer], recv_sem=obs_recv.at[slot],
            device_id={"xline": peer // 2, "inline": lax.rem(peer, 2)}, device_id_type=MESH,
        )

    finals = (previous_out, last_out)
    final_idx = (2 + (steps - 1) % 2, 2 + steps % 2)

    def home_copy(n, to_y):
        return pltpu.make_async_remote_copy(
            src_ref=field.at[final_idx[n], inner_i, pl.ds(8 + to_y * tile_x, tile_x), :],
            dst_ref=finals[n].at[pl.ds(cp * n_i, n_i)],
            send_sem=ret_send.at[n, to_y], recv_sem=ret_recv.at[n, cp],
            device_id={"xline": 2 * plane + to_y, "inline": origin}, device_id_type=MESH,
        )

    def home_arrival(n, a):
        return pltpu.make_async_remote_copy(
            src_ref=field.at[final_idx[n], inner_i, pl.ds(8, tile_x), :],
            dst_ref=finals[n].at[pl.ds(a * n_i, n_i)],
            send_sem=ret_send.at[n, 0], recv_sem=ret_recv.at[n, a],
            device_id={"xline": mate}, device_id_type=MESH,
        )

    def home_own(n):
        columns = pl.multiple_of(8 + y * tile_x, 8)
        return pltpu.make_async_copy(
            field.at[final_idx[n], inner_i, pl.ds(columns, tile_x), :],
            finals[n].at[pl.ds(cp * n_i, n_i)], ret_local.at[n],
        )

    def home_start(n):
        for to_y in range(2):
            @pl.when(arrives(to_y))
            def _():
                home_copy(n, to_y).start()

        @pl.when(stays)
        def _():
            home_own(n).start()

    def home_finish(n):
        for to_y in range(2):
            @pl.when(arrives(to_y))
            def _():
                home_copy(n, to_y).wait_send()
        for a in range(2):
            @pl.when(leaves(a))
            def _():
                home_arrival(n, a).wait_recv()

        @pl.when(stays)
        def _():
            home_own(n).wait()

    dz = depth // n_xline
    planes_n = n_xline // 2

    def slab_copy(d):
        return pltpu.make_async_remote_copy(
            src_ref=g_send.at[d],
            dst_ref=grad_out.at[cp, :, pl.ds(pl.multiple_of(plane * n_x, 8), n_x), :],
            send_sem=g_ssem.at[d], recv_sem=g_rsem.at[cp, plane],
            device_id={"xline": d, "inline": origin}, device_id_type=MESH,
        )

    def own_slab():
        return pltpu.make_async_copy(
            g_send.at[xl], grad_out.at[cp, :, pl.ds(pl.multiple_of(plane * n_x, 8), n_x), :], g_local.at[0]
        )

    def slab_arrival(a, p):
        return pltpu.make_async_remote_copy(
            src_ref=g_send.at[0],
            dst_ref=grad_out.at[a, :, pl.ds(pl.multiple_of(p * n_x, 8), n_x), :],
            send_sem=g_ssem.at[0], recv_sem=g_rsem.at[a, p],
            device_id={"xline": mate}, device_id_type=MESH,
        )

    def fused_gradient():
        group = 128 // dz
        lane = div(lax.broadcasted_iota(jnp.int32, (n_x, 128), 1), dz)
        for chunk in range(depth // 128):
            for ig in range(n_i // group):
                planes = [image[ig * group + j, :, pl.ds(chunk * 128, 128)] for j in range(group)]
                for dd in range(group):
                    out = None
                    for j in range(group):
                        shift = (j - dd) * dz % 128
                        moved = pltpu.roll(planes[j], shift, axis=1) if shift else planes[j]
                        out = moved if out is None else jnp.where(lane == j, moved, out)
                    g_send[chunk * group + dd, ig] = out

        @pl.loop(1, n_xline + 1)
        def _(r):
            d = lax.rem(xl + r, n_xline)

            @pl.when(jnp.logical_or(d != xl, origin != core))
            def _():
                slab_copy(d).start()

        home_start(1)

        @pl.when(origin == core)
        def _():
            own_slab().start()

        @pl.loop(0, n_xline)
        def _(r):
            a, p = lax.rem(r, 2), r // 2
            mine = jnp.logical_and(origin == core, jnp.logical_and(a == cp, p == plane))

            @pl.when(jnp.logical_not(mine))
            def _():
                slab_arrival(a, p).wait_recv()

        @pl.when(origin == core)
        def _():
            own_slab().wait()

        @pl.loop(1, n_xline + 1)
        def _(r):
            d = lax.rem(xl + r, n_xline)

            @pl.when(jnp.logical_or(d != xl, origin != core))
            def _():
                slab_copy(d).wait_send()

    for way in (LEFT, RIGHT, UP, DOWN):
        @pl.when(jnp.logical_not(has[way]))
        def _():
            halo = x_in if way < UP else i_in
            halo[:, way % 2] = jnp.zeros(halo.shape[:1] + halo.shape[2:], jnp.float32)
    image[...] = jnp.zeros(image.shape, jnp.float32)

    for copy in small:
        copy.wait()
    n_counts = rec_counts.shape[1]
    spread = (
        div(lax.broadcasted_iota(jnp.int32, (n_counts, slots), 1), CAP)
        == lax.broadcasted_iota(jnp.int32, (n_counts, slots), 0)
    ).astype(jnp.float32).astype(jnp.bfloat16)
    counts = jnp.broadcast_to(rec_counts[...].astype(jnp.float32), (8, n_counts)).astype(jnp.bfloat16)
    live = dot(counts, spread)
    place = mod(lax.broadcasted_iota(jnp.int32, (8, slots), 1), CAP).astype(jnp.float32)
    list_out[...] = jnp.where(place < live, jnp.broadcast_to(rec_cells[...], (8, slots)), -1)

    pl.semaphore_wait(barrier, greeted)

    for a in range(2):
        @pl.when(leaves(a))
        def _():
            list_copy(a).start()

    for n in (RHO, SPEED, NOW):
        tile_start(n)
    tile_start(BEFORE)

    obs_in[me] = observed[...]

    @pl.when(stays)
    def _():
        list_in[y] = list_out[...]

    offset = lax.broadcasted_iota(jnp.int32, (depth, depth), 0) - lax.broadcasted_iota(jnp.int32, (depth, depth), 1)
    second = jnp.zeros((depth, depth), jnp.float32)
    first = jnp.zeros((depth, depth), jnp.float32)
    for k in range(1, 5):
        second = jnp.where((offset == k) | (offset == -k), SECOND_COEFFS[k] / SECOND_COEFFS[1], second)
        first = jnp.where(offset == k, FIRST_COEFFS[k - 1] / FIRST_COEFFS[0], first)
        first = jnp.where(offset == -k, -FIRST_COEFFS[k - 1] / FIRST_COEFFS[0], first)
    z_mat[:, pl.ds(0, depth)] = second.astype(jnp.bfloat16)
    z_mat[:, pl.ds(depth, depth)] = first.astype(jnp.bfloat16)

    at = lax.broadcasted_iota(jnp.int32, (rows, rows), 0)
    to = lax.broadcasted_iota(jnp.int32, (rows, rows), 1)
    step_i = div(to, n_x) - div(at, n_x)
    step_x = mod(to, n_x) - mod(at, n_x)
    lateral_lap = jnp.zeros((rows, rows), jnp.float32)
    for n, (along, still) in enumerate(((step_i, step_x), (step_x, step_i))):
        along = jnp.where(still == 0, along, 0)
        first = jnp.zeros((rows, rows), jnp.float32)
        for k in range(1, 5):
            lateral_lap = jnp.where((along == k) | (along == -k), SECOND_COEFFS[k] / SECOND_COEFFS[1], lateral_lap)
            first = jnp.where(along == k, FIRST_COEFFS[k - 1] / FIRST_COEFFS[0], first)
            first = jnp.where(along == -k, -FIRST_COEFFS[k - 1] / FIRST_COEFFS[0], first)
        row_mat[pl.ds((n + 1) * rows, rows), :] = first.astype(jnp.bfloat16)
    row_mat[pl.ds(0, rows), :] = lateral_lap.astype(jnp.bfloat16)

    full_x = tile_x * n_xline
    cells = src_cell[...]
    src_i = div(cells, full_x * depth) - q * n_i
    src_x = mod(div(cells, depth), full_x) - plane * n_x
    inside = (src_i >= 0) & (src_i < n_i) & (src_x >= 0) & (src_x < n_x)
    src_row = jnp.where(inside, src_i * n_x + src_x, -1)
    n_src = cells.shape[1]
    src_rows = (lax.broadcasted_iota(jnp.int32, (rows, n_src), 0) == src_row).astype(jnp.float32)
    src_cols = (lax.broadcasted_iota(jnp.int32, (depth, n_src), 0) == mod(cells, depth)).astype(jnp.float32).astype(jnp.bfloat16)

    def flat(idx):
        return field[idx, inner_i, inner_x, :].reshape(rows, depth)

    def differences(idx):
        high, low = split_bf16(flat(idx))
        wide[...] = dot(row_mat[...], high) + dot(row_mat[...], low)
        deep[...] = dot(high, z_mat[...]) + dot(low, z_mat[...])

    def operator(idx, i):
        def line(n):
            return pl.ds(pl.multiple_of(n * rows + i * n_x, n_x), n_x)

        center = field[idx, i + 4, inner_x, :]
        return center, (
            3.0 * SECOND_COEFFS[0] * center
            + SECOND_COEFFS[1] * (wide[line(0), :] + deep[line(0), pl.ds(0, depth)])
            - slopes[0, i] * wide[line(1), :] - slopes[1, i] * wide[line(2), :]
            - slopes[2, i] * deep[line(0), pl.ds(depth, depth)]
        )

    def across(idx, i):
        lap = slope_i = slope_x = None
        for k in range(1, 5):
            plus_i = field[idx, i + 4 + k, inner_x, :]
            minus_i = field[idx, i + 4 - k, inner_x, :]
            plus_x = field[idx, i + 4, pl.ds(8 + k, n_x), :]
            minus_x = field[idx, i + 4, pl.ds(8 - k, n_x), :]
            terms = (
                SECOND_COEFFS[k] * ((plus_i + minus_i) + (plus_x + minus_x)),
                FIRST_COEFFS[k - 1] * (plus_i - minus_i),
                FIRST_COEFFS[k - 1] * (plus_x - minus_x),
            )
            if lap is None:
                lap, slope_i, slope_x = terms
            else:
                lap, slope_i, slope_x = lap + terms[0], slope_i + terms[1], slope_x + terms[2]
        return lap, slope_i, slope_x

    for n in shares:
        half_arrival(n).wait_recv()
        pass_on(n).start()
    tile_finish(RHO)
    send_all(DENSITY)
    tile_finish(NOW)
    send_all(0)

    high, low = split_bf16(flat(DENSITY))
    deep[...] = dot(high, z_mat[...]) + dot(low, z_mat[...])
    slopes[2] = ((FIRST_COEFFS[0] * FIRST_COEFFS[0]) * deep[:, pl.ds(depth, depth)]).reshape(n_i, n_x, depth)
    differences(0)

    def inject_sources(t):
        high, low = split_bf16(src_rows * wavelet[pl.ds(t, 1), :])
        return dot_nt(high, src_cols) + dot_nt(low, src_cols)

    accel[0] = inject_sources(0).reshape(n_i, n_x, depth)

    for part, d, c in pieces:
        finish(DENSITY, part, d, c)
    sent(DENSITY)
    for d in range(layers):
        lanes = pl.ds(d * 128, 128)
        for side in range(2):
            for c in range(2):
                field[DENSITY, pl.ds(side * (n_i + 4), 4), pl.ds(8 + c * half_x, half_x), lanes] = i_in[DENSITY, side, d, c]
            field[DENSITY, inner_i, pl.ds(4 + side * (n_x + 4), 4), lanes] = x_in[DENSITY, side, d]

    @pl.loop(0, n_i)
    def _(i):
        _, slope_i, slope_x = across(DENSITY, i)
        slopes[0, i] = FIRST_COEFFS[0] * slope_i
        slopes[1, i] = FIRST_COEFFS[0] * slope_x

    tile_finish(SPEED)
    column = lax.broadcasted_iota(jnp.int32, (n_x, depth), 0)

    @pl.loop(0, n_i)
    def _(i):
        square = vel[i] * vel[i]
        speed_sq[i] = square
        accel[0, i] += square * operator(0, i)[1]
        for k in range(1, 5):
            weight = jnp.where(
                column < k, SECOND_COEFFS[k] + (FIRST_COEFFS[k - 1] / FIRST_COEFFS[0]) * slopes[1, i],
                jnp.where(
                    column >= n_x - k, SECOND_COEFFS[k] - (FIRST_COEFFS[k - 1] / FIRST_COEFFS[0]) * slopes[1, i], 0.0
                ),
            )
            wx[k - 1, i] = square * weight

    tile_finish(BEFORE)

    @pl.loop(0, n_i)
    def _(i):
        field[1, i + 4, inner_x, :] = (
            2.0 * field[0, i + 4, inner_x, :] - field[1, i + 4, inner_x, :] + accel[0, i]
        )

    def make_maps():
        for from_y in range(2):
            @pl.when(arrives(from_y))
            def _():
                list_arrival(from_y).wait_recv()
        for a in range(2):
            @pl.when(leaves(a))
            def _():
                list_copy(a).wait_send()
        for from_y in range(2):
            spot = list_in[from_y][:1]
            cell_i = div(spot, tile_x * depth) - cp * n_i
            cell_x = mod(div(spot, depth), tile_x) + from_y * tile_x
            row = jnp.where((spot >= 0) & (cell_i >= 0) & (cell_i < n_i), cell_i * n_x + cell_x, -1)
            columns = pl.ds(from_y * slots, slots)
            row_map[:, columns] = (lax.broadcasted_iota(jnp.int32, (rows, slots), 0) == row).astype(jnp.float32)
            zmap_t[:, columns] = (
                lax.broadcasted_iota(jnp.int32, (depth, slots), 0) == mod(spot, depth)
            ).astype(jnp.float32).astype(jnp.bfloat16)

    def make_traces():
        @pl.loop(1, n_group)
        def _(r):
            peer = lax.rem(me + r, n_group)
            obs_copy(peer, peer).wait_recv()
            obs_copy(peer, me).wait_send()

        lane = div(lax.broadcasted_iota(jnp.int32, (8, slots), 1), CAP)
        for from_y in range(2):
            owner = (2 * plane + from_y) * 2 + origin

            def place_one(s, total):
                moved = pltpu.roll(obs_in[s], lax.rem(s - owner + n_group, n_group) * CAP, axis=1)
                return jnp.where(lane == s, moved, total)

            traces[:, pl.ds(from_y * slots, slots)] = lax.fori_loop(
                0, n_group, place_one, jnp.zeros((8, slots), jnp.float32)
            )

    def prepare(idx, term):
        base[...] = term.reshape(n_i, n_x, depth)
        differences(idx)

    def interior(now, other, i):
        center, value = operator(now, i)
        change = base[i] + speed_sq[i] * value
        field[other, i + 4, inner_x, :] = 2.0 * center - field[other, i + 4, inner_x, :] + change
        return center, change

    def correct(now, other, part, d, c, t):
        up = part == 0
        sign = jnp.where(up, 1.0, -1.0)
        columns, lanes = pl.ds(c * half_x, half_x), pl.ds(d * 128, 128)
        for r in range(middle):
            i = jnp.where(up, r, n_i - 1 - r)
            halo = x_in[now, c, d, i]
            pair = jnp.concatenate([halo] * (half_x // 4), axis=0)
            change = wx[3, i, columns, lanes] * pair
            for k in range(1, 4):
                change += wx[k - 1, i, columns, lanes] * pltpu.roll(pair, half_x - k if c else k, axis=0)
            lap = None
            for h in range(4 - r):
                k = r + 1 + h
                halo = i_in[now, part, d, c, jnp.where(up, 3 - h, h)]
                terms = SECOND_COEFFS[k] * halo, (FIRST_COEFFS[k - 1] / FIRST_COEFFS[0]) * halo
                lap, slope = terms if lap is None else (lap + terms[0], slope + terms[1])
            if lap is not None:
                change += speed_sq[i, columns, lanes] * (lap + (sign * slopes[0, i, columns, lanes]) * slope)
            spot = (other, i + 4, pl.ds(8 + c * half_x, half_x), lanes)
            fresh = field[spot] + change
            field[spot] = fresh
            x_out[other, c, d, i] = fresh[half_x - 4:] if c else fresh[:4]
            if r < 4:
                i_out[other, part, d, c, jnp.where(up, r, 3 - r)] = fresh
            if t is not None:
                accel[t, i, columns, lanes] += change

    def sample(idx, t):
        high, low = split_bf16(flat(idx))
        picked = dot(high, zmap_t[...]) + dot(low, zmap_t[...])
        predicted = jnp.sum(picked * row_map[...], axis=0, keepdims=True)
        residual_ref[t] = predicted

    def task_first():
        quarter_start(ADJ_NOW, 0)
        make_maps()

    def task_second():
        quarter_start(ADJ_NOW, 1)

    def task_third():
        quarter_start(ADJ_BEFORE, 0)

        @pl.loop(1, n_group)
        def _(r):
            obs_copy(lax.rem(me + r, n_group), me).start()

    def task_halos():
        quarter_start(ADJ_BEFORE, 1)
        tile_finish(ADJ_NOW)
        send_all(2)

    def task_adjoint():
        tile_finish(ADJ_BEFORE)
        differences(2)
        vel[...] = (2.0 / steps) / vel[...]

        @pl.loop(0, n_i, unroll=2)
        def _(i):
            center, value = operator(2, i)
            field[3, i + 4, inner_x, :] = (
                2.0 * center - field[3, i + 4, inner_x, :] + speed_sq[i] * value
            )

    tasks = [task_first, task_second, task_third, task_halos, task_adjoint, make_traces]
    times = [1 + n * (steps - 2) // len(tasks) for n in range(len(tasks))]

    @pl.loop(0, steps)
    def _(t):
        now = lax.rem(t, 2)
        other = 1 - now

        @pl.when(t > 0)
        def _():
            prepare(now, inject_sources(t))

            @pl.loop(0, n_i, unroll=2)
            def _(i):
                _, change = interior(now, other, i)
                accel[t, i] = change

        for at, task in zip(times, tasks):
            pl.when(t == at)(task)

        @pl.when(t >= 1)
        def _():
            sample(now, t - 1)
            sent(other)

        for part, d, c in pieces:
            finish(now, part, d, c)
            correct(now, other, part, d, c, t)

            @pl.when(t < steps - 1)
            def _():
                send(other, part, d, c)

    sent((steps - 1) % 2)
    sample(steps % 2, steps - 1)

    @pl.loop(0, steps)
    def _(j):
        now = 2 + lax.rem(j, 2)
        other = 5 - now
        t = steps - 1 - j
        high, low = split_bf16(row_map[...] * (residual_ref[t] - traces[pl.ds(t, 1), :]))
        injected = dot_nt(high, zmap_t[...]) + dot_nt(low, zmap_t[...])

        @pl.when(j == 0)
        def _():
            field[3, inner_i, inner_x, :] += injected.reshape(n_i, n_x, depth)

        @pl.when(j > 0)
        def _():
            prepare(now, injected)

            @pl.loop(0, n_i, unroll=2)
            def _(i):
                center, _ = interior(now, other, i)
                image[i] += center * accel[t + 1, i]

            sent(other)

        @pl.when(j == steps - 1)
        def _():
            home_start(0)

        for part, d, c in pieces:
            finish(now, part, d, c)
            correct(now, other, part, d, c, None)

            @pl.when(j < steps - 1)
            def _():
                send(other, part, d, c)

    sent(2 + (steps - 1) % 2)

    @pl.loop(0, n_i, unroll=4)
    def _(i):
        image[i] = (image[i] + field[final_idx[1], i + 4, inner_x, :] * accel[0, i]) * vel[i]

    if fused:
        fused_gradient()
    else:
        grad_out[...] = image[...]
        home_start(1)
    home_finish(0)
    home_finish(1)


def finish_kernel(shape, slabs, last, previous):
    dz, tile_i, full_x = shape
    _, n_groups, _, lanes = slabs.shape
    group = lanes // dz

    def kernel(
        slabs_in, last_in, previous_in, gradient, last_out, previous_out,
        slabs_held, last_held, previous_held, lines_held, in_sem, out_sem,
    ):
        loads = [
            pltpu.make_async_copy(slabs_in, slabs_held, in_sem.at[0]),
            pltpu.make_async_copy(last_in, last_held, in_sem.at[1]),
            pltpu.make_async_copy(previous_in, previous_held, in_sem.at[2]),
        ]
        for load in loads:
            load.start()
        far = (
            lax.broadcasted_iota(jnp.int32, (full_x, full_x), 0) - lax.broadcasted_iota(jnp.int32, (full_x, full_x), 1)
        ).astype(jnp.float32)
        weights = jnp.exp(-jnp.abs(far) / SMOOTH)
        weights = weights / jnp.sum(weights, axis=0, keepdims=True)
        stores = [
            pltpu.make_async_copy(last_held, last_out, out_sem.at[0]),
            pltpu.make_async_copy(previous_held, previous_out, out_sem.at[1]),
        ]
        for load, store in zip(loads[1:], stores):
            load.wait()
            store.start()
        loads[0].wait()
        for a in range(2):
            for ig in range(n_groups):
                lines = dot_tn_exact(slabs_held[a, ig], weights)
                for j in range(group):
                    lines_held[:, (a * n_groups + ig) * group + j, :] = lines[j * dz:(j + 1) * dz]
            span = pl.ds(a * (tile_i // 2), tile_i // 2)
            store = pltpu.make_async_copy(lines_held.at[:, span, :], gradient.at[:, span, :], out_sem.at[2 + a])
            store.start()
            stores.append(store)
        for store in stores:
            store.wait()

    anywhere = pl.BlockSpec(memory_space=pl.ANY)
    return pl.pallas_call(
        kernel,
        out_shape=[jax.ShapeDtypeStruct(dims, jnp.float32) for dims in (shape, last.shape, previous.shape)],
        in_specs=[anywhere] * 3,
        out_specs=[anywhere] * 3,
        scratch_shapes=[
            *[pltpu.VMEM(dims, jnp.float32) for dims in (slabs.shape, last.shape, previous.shape, shape)],
            pltpu.SemaphoreType.DMA((3,)),
            pltpu.SemaphoreType.DMA((4,)),
        ],
        compiler_params=pltpu.CompilerParams(vmem_limit_bytes=56 * 1024 * 1024),
    )(slabs, last, previous)


def per_device(
    fwd_now, fwd_before, adj_now, adj_before, velocity, log_density,
    observed, rec_cells, rec_counts, src_cell, wavelet,
):
    tile_i, tile_x, depth = fwd_now.shape
    steps = wavelet.shape[0]
    n_xline = lax.axis_size("xline")
    full_x = tile_x * n_xline
    n_i, n_x = tile_i // 2, tile_x * 2
    rows = n_i * n_x
    slots = rec_cells.shape[1]
    n_group = 2 * n_xline
    dz = depth // n_xline
    fused = dz >= 8 and 128 % dz == 0 and depth % 128 == 0 and n_i % (128 // dz) == 0
    group = 128 // dz if fused else 1
    layers = depth // 128

    block = (n_i, n_x, depth)
    vmem = pl.BlockSpec(memory_space=pltpu.VMEM)
    anywhere = pl.BlockSpec(memory_space=pl.ANY)
    dma = pltpu.SemaphoreType.DMA
    kernel = functools.partial(wave_kernel, (tile_i, tile_x, n_i, n_x, depth, steps, n_xline, fused))
    grad_shape = (2, n_i // group, full_x, 128) if fused else block
    slab_shape = (n_xline, n_i // group, n_x, 128) if fused else (8, 128)
    small_shapes = [observed, rec_cells, rec_counts, src_cell[None, :], wavelet]
    raw, last, previous = pl.pallas_call(
        kernel,
        out_shape=[
            jax.ShapeDtypeStruct(grad_shape, jnp.float32),
            jax.ShapeDtypeStruct(fwd_now.shape, jnp.float32),
            jax.ShapeDtypeStruct(fwd_now.shape, jnp.float32),
        ],
        in_specs=[anywhere] * 11,
        out_specs=[anywhere if fused else vmem, anywhere, anywhere],
        scratch_shapes=[
            pltpu.VMEM((5, n_i + 8, n_x + 16, depth), jnp.float32),
            pltpu.VMEM(block, jnp.float32),
            pltpu.VMEM((5, 2, layers, n_i, 4, 128), jnp.float32),
            pltpu.VMEM((5, 2, layers, n_i, 4, 128), jnp.float32),
            pltpu.VMEM((5, 2, layers, 2, 4, tile_x, 128), jnp.float32),
            pltpu.VMEM((5, 2, layers, 2, 4, tile_x, 128), jnp.float32),
            pltpu.VMEM((steps,) + block, jnp.float32),
            pltpu.VMEM(block, jnp.float32),
            pltpu.VMEM(block, jnp.float32),
            pltpu.VMEM((3,) + block, jnp.float32),
            pltpu.VMEM(block, jnp.float32),
            pltpu.VMEM((4,) + block, jnp.float32),
            pltpu.VMEM((rows, 2 * slots), jnp.float32),
            pltpu.VMEM((depth, 2 * slots), jnp.bfloat16),
            pltpu.VMEM((depth, 2 * depth), jnp.bfloat16),
            pltpu.VMEM((steps, 1, 2 * slots), jnp.float32),
            pltpu.VMEM((steps, 2 * slots), jnp.float32),
            pltpu.VMEM((8, slots), jnp.int32),
            pltpu.VMEM((2, 8, slots), jnp.int32),
            pltpu.VMEM((n_group,) + observed.shape, jnp.float32),
            pltpu.VMEM(slab_shape, jnp.float32),
            *[pltpu.VMEM(value.shape, value.dtype) for value in small_shapes],
            pltpu.VMEM((3 * rows, rows), jnp.bfloat16),
            pltpu.VMEM((3 * rows, depth), jnp.float32),
            pltpu.VMEM((rows, 2 * depth), jnp.float32),
            dma((5, 2)), dma((5, 2, 2, layers)), dma((5, 2)), dma((5, 2, 2, layers)),
            dma((6, 2)), dma((6, 2)), dma((6,)),
            dma((2,)), dma((2,)),
            dma((n_group,)), dma((n_group,)),
            dma((2, 2)), dma((2, 2)), dma((2,)),
            dma((n_xline,)), dma((2, n_xline // 2)), dma((1,)), dma((5,)),
            dma((6,)), dma((6,)),
        ],
        compiler_params=pltpu.CompilerParams(
            collective_id=0, has_side_effects=True, vmem_limit_bytes=56 * 1024 * 1024
        ),
    )(
        log_density, fwd_now, velocity, fwd_before, adj_now, adj_before,
        *small_shapes,
    )
    if fused:
        return finish_kernel((dz, tile_i, full_x), raw, last, previous)

    places = []
    for xl in range(n_xline):
        for core in range(2):
            y, plane = xl % 2, xl // 2
            cp = (core + plane % 2) % 2
            places.append((xl * 2 + core, (2 * plane + cp) * 2 + y))
    raw = lax.ppermute(raw, ("xline", "inline"), places)
    columns = lax.all_to_all(
        raw.reshape(n_i, n_x, n_xline, dz).transpose(2, 0, 1, 3),
        "xline", split_axis=0, concat_axis=0, tiled=True,
    ).reshape(n_xline // 2, 2, n_i, n_x, dz)
    positions = jnp.arange(full_x).astype(jnp.float32)
    weights = jnp.exp(-jnp.abs(positions[:, None] - positions[None, :]) / SMOOTH)
    weights = weights / jnp.sum(weights, axis=1, keepdims=True)
    gradient = jnp.einsum(
        "phixz,ypx->zhiy", columns, weights.reshape(full_x, n_xline // 2, n_x),
        precision=lax.Precision.HIGHEST,
    ).reshape(dz, tile_i, full_x)
    return gradient, last, previous


def solution(mesh):
    return jax.shard_map(
        per_device,
        mesh=mesh,
        in_specs=(
            P(("shots", "inline"), "xline", None),
            P(("shots", "inline"), "xline", None),
            P(("shots", "inline"), "xline", None),
            P(("shots", "inline"), "xline", None),
            P("inline", "xline", None),
            P("inline", "xline", None),
            P("shots", ("xline", "inline")),
            P(("xline", "inline"), None),
            P(("xline", "inline"), None),
            P("shots"),
            P("shots", None),
        ),
        out_specs=(
            P(("shots", "xline"), "inline", None),
            P(("shots", "inline"), "xline", None),
            P(("shots", "inline"), "xline", None),
        ),
        check_vma=False,
    )
```

```python
import functools

import jax
import jax.numpy as jnp
from jax import lax
from jax.experimental import pallas as pl
from jax.experimental.pallas import tpu as pltpu
from jax.sharding import PartitionSpec as P

CAP = 8
SMOOTH = 16
MESH = pl.DeviceIdType.MESH

SECOND_COEFFS = (-205.0 / 72.0, 8.0 / 5.0, -1.0 / 5.0, 8.0 / 315.0, -1.0 / 560.0)
FIRST_COEFFS = (4.0 / 5.0, -1.0 / 5.0, 4.0 / 105.0, -1.0 / 280.0)
LEFT, RIGHT, UP, DOWN = 0, 1, 2, 3
DENSITY = 4
RHO, NOW, SPEED, BEFORE, ADJ_NOW, ADJ_BEFORE = range(6)


def split_bf16(value):
    high = value.astype(jnp.bfloat16)
    low = (value - high.astype(jnp.float32)).astype(jnp.bfloat16)
    return high, low


def dot(a, b):
    return jnp.dot(a, b, preferred_element_type=jnp.float32)


def dot_nt(a, b):
    return lax.dot_general(a, b, (((1,), (1,)), ((), ())), preferred_element_type=jnp.float32)


def dot_tn_exact(a, b):
    dims = (((0,), (0,)), ((), ()))
    ah, al = split_bf16(a)
    bh, bl = split_bf16(b)
    one = lax.dot_general(ah, bh, dims, preferred_element_type=jnp.float32)
    two = lax.dot_general(al, bh, dims, preferred_element_type=jnp.float32)
    three = lax.dot_general(ah, bl, dims, preferred_element_type=jnp.float32)
    return one + (two + three)


def div(value, n):
    return lax.shift_right_arithmetic(value, jnp.full_like(value, n.bit_length() - 1))


def mod(value, n):
    return value & (n - 1)


def wave_kernel(
    sizes,
    log_density, fwd_now, velocity, fwd_before, adj_now, adj_before,
    given_observed, given_cells, given_counts, given_src, given_wavelet,
    grad_out, last_out, previous_out,
    field, vel, x_in, x_out, i_in, i_out, accel, base, image, slopes, speed_sq, wx,
    row_map, zmap_t, z_mat, residual_ref, traces, list_out, list_in, obs_in, g_send,
    held_observed, held_cells, held_counts, held_src, held_wavelet, row_mat, wide, deep,
    x_send, x_recv, i_send, i_recv, rt_send, rt_recv, rt_local, list_send, list_recv, obs_send, obs_recv,
    ret_send, ret_recv, ret_local, g_ssem, g_rsem, g_local, small_sem, pass_send, pass_recv,
):
    tile_i, tile_x, n_i, n_x, depth, steps, n_xline, fused = sizes
    rows = n_i * n_x
    small_in = (given_observed, given_cells, given_counts, given_src, given_wavelet)
    small_held = (held_observed, held_cells, held_counts, held_src, held_wavelet)
    slots = held_cells.shape[1]
    n_group = 2 * n_xline
    xl = lax.axis_index("xline")
    core = lax.axis_index("inline")
    me = xl * 2 + core
    y = lax.rem(xl, 2)
    plane = xl // 2
    z_odd = lax.rem(plane, 2)
    mate = xl + 1 - 2 * y
    cp = lax.rem(core + z_odd, 2)
    origin = y
    q = 2 * y + cp
    stays = y == core
    has = (xl >= 2, xl < n_xline - 2, q > 0, q < 3)
    other_core = 1 - core
    shot = lax.axis_index("shots")
    shares = (RHO, SPEED) if lax.axis_size("shots") == 2 else ()
    target = (
        {"xline": xl - 2, "inline": other_core},
        {"xline": xl + 2, "inline": other_core},
        {"xline": jnp.where(q == 2, mate, xl), "inline": other_core},
        {"xline": jnp.where(q == 1, mate, xl), "inline": other_core},
    )
    inner_i = pl.ds(4, n_i)
    inner_x = pl.ds(8, n_x)
    middle = n_i // 2

    barrier = pltpu.get_barrier_semaphore()

    def greet(device):
        pl.semaphore_signal(barrier, inc=1, device_id=device, device_id_type=MESH)

    near = n_xline // 2 <= 4
    if near:
        greet({"inline": other_core})
        greet({"xline": mate})
        greet({"xline": mate, "inline": other_core})
        for way in (LEFT, RIGHT):
            @pl.when(has[way])
            def _():
                greet(target[way])
        greeted = 3 + has[LEFT].astype(jnp.int32) + has[RIGHT].astype(jnp.int32)
    else:
        @pl.loop(1, n_group)
        def _(r):
            peer = lax.rem(me + r, n_group)
            greet({"xline": peer // 2, "inline": lax.rem(peer, 2)})
        greeted = n_group - 1
    if shares:
        greet({"shots": 1 - shot})
        greeted = greeted + 1

    small = [
        pltpu.make_async_copy(given, held, small_sem.at[n])
        for n, (given, held) in enumerate(zip(small_in, small_held))
    ]
    for copy in small:
        copy.start()
    observed, rec_cells, rec_counts, src_cell, wavelet = small_held

    layers = depth // 128
    half_x = n_x // 2

    def beside(idx, way, part, d):
        part_rows = pl.ds(part * middle, middle)
        return pltpu.make_async_remote_copy(
            src_ref=x_out.at[idx, way, d, part_rows], dst_ref=x_in.at[idx, 1 - way, d, part_rows],
            send_sem=x_send.at[idx, way], recv_sem=x_recv.at[idx, way, part, d],
            device_id=target[way], device_id_type=MESH,
        )

    def above(idx, part, c, d, arriving):
        up = part == 0
        return pltpu.make_async_remote_copy(
            src_ref=i_out.at[idx, part, d, c],
            dst_ref=i_in.at[idx, part if arriving else 1 - part, d, c],
            send_sem=i_send.at[idx, part],
            recv_sem=i_recv.at[idx, 1 - part if arriving else part, c, d],
            device_id={
                "xline": jnp.where(up, target[UP]["xline"], target[DOWN]["xline"]), "inline": other_core
            },
            device_id_type=MESH,
        )

    def has_row(part):
        return jnp.where(part == 0, q, 3 - q) > 0

    def send(idx, part, d, c):
        @pl.when(has[c])
        def _():
            beside(idx, c, part, d).start()

        @pl.when(has_row(part))
        def _():
            above(idx, part, c, d, False).start()

    def finish(idx, part, d, c):
        @pl.when(has[c])
        def _():
            beside(idx, 1 - c, part, d).wait_recv()

        @pl.when(has_row(part))
        def _():
            above(idx, part, c, d, True).wait_recv()

    def sent(idx):
        for n in range(2):
            @pl.when(has[n])
            def _():
                pltpu.make_async_remote_copy(
                    src_ref=x_out.at[idx, n], dst_ref=x_in.at[idx, 1 - n],
                    send_sem=x_send.at[idx, n], recv_sem=x_recv.at[idx, n, 0, 0],
                    device_id=target[n], device_id_type=MESH,
                ).wait_send()

            @pl.when(has[UP + n])
            def _():
                pltpu.make_async_remote_copy(
                    src_ref=i_out.at[idx, n], dst_ref=i_in.at[idx, 1 - n],
                    send_sem=i_send.at[idx, n], recv_sem=i_recv.at[idx, n, 0, 0],
                    device_id=target[UP + n], device_id_type=MESH,
                ).wait_send()

    def send_all(idx):
        for part, d, c in pieces:
            rows_at = pl.ds(part * middle, middle)
            x_out[idx, c, d, rows_at] = field[
                idx, pl.ds(4 + part * middle, middle), pl.ds(8 + c * (n_x - 4), 4), pl.ds(d * 128, 128)
            ]
            i_out[idx, part, d, c] = field[
                idx, pl.ds(4 + part * (n_i - 4), 4), pl.ds(8 + c * half_x, half_x), pl.ds(d * 128, 128)
            ]
            send(idx, part, d, c)

    halves = (1 - y, y)
    pieces = [(part, d, c) for part in halves for d in range(layers) for c in range(2)]

    sources = (log_density, fwd_now, velocity, fwd_before, adj_now, adj_before)
    places = (DENSITY, 0, None, 1, 2, 3)

    def landing(n, from_y):
        columns = pl.multiple_of(from_y * tile_x, tile_x)
        if n == SPEED:
            return vel.at[:, pl.ds(columns, tile_x), :]
        return field.at[places[n], inner_i, pl.ds(pl.multiple_of(8 + columns, 8), tile_x), :]

    def tile_copy(n, a):
        return pltpu.make_async_remote_copy(
            src_ref=sources[n].at[pl.ds(a * n_i, n_i)], dst_ref=landing(n, y),
            send_sem=rt_send.at[n, a], recv_sem=rt_recv.at[n, y],
            device_id={"xline": 2 * plane + core, "inline": lax.rem(a + z_odd, 2)},
            device_id_type=MESH,
        )

    def tile_arrival(n, from_y):
        return pltpu.make_async_remote_copy(
            src_ref=sources[n].at[pl.ds(0, n_i)], dst_ref=landing(n, from_y),
            send_sem=rt_send.at[n, 0], recv_sem=rt_recv.at[n, from_y],
            device_id={"xline": mate}, device_id_type=MESH,
        )

    def own_copy(n):
        return pltpu.make_async_copy(
            sources[n].at[pl.ds(cp * n_i, n_i)], landing(n, y), rt_local.at[n]
        )

    def leaves(a):
        return jnp.logical_not(jnp.logical_and(stays, cp == a))

    def arrives(from_y):
        return jnp.logical_not(jnp.logical_and(stays, y == from_y))

    def tile_start(n):
        for a in range(2):
            @pl.when(jnp.logical_and(stays, cp != a) if n in shares else leaves(a))
            def _():
                tile_copy(n, a).start()

        if n in shares:
            for a in range(2):
                @pl.when(jnp.logical_not(stays))
                def _():
                    half_copy(n, a).start()

        @pl.when(stays)
        def _():
            own_copy(n).start()

    def tile_finish(n):
        for from_y in range(2):
            @pl.when(jnp.logical_and(arrives(from_y), y == from_y) if n in shares else arrives(from_y))
            def _():
                tile_arrival(n, from_y).wait_recv()
        for a in range(2):
            @pl.when(jnp.logical_and(stays, cp != a) if n in shares else leaves(a))
            def _():
                tile_copy(n, a).wait_send()

        @pl.when(stays)
        def _():
            own_copy(n).wait()

        if n in shares:
            for a in range(2):
                @pl.when(jnp.logical_not(stays))
                def _():
                    half_copy(n, a).wait_send()
            pass_on(n).wait_send()
            passed_on(n).wait_recv()

    def quarter_start(n, which):
        for a in range(2):
            @pl.when(leaves(a))
            def _():
                pltpu.make_async_remote_copy(
                    src_ref=sources[n].at[pl.ds(a * n_i + which * middle, middle)], dst_ref=half_landing(n, y, which),
                    send_sem=rt_send.at[n, a], recv_sem=rt_recv.at[n, y],
                    device_id={"xline": 2 * plane + core, "inline": lax.rem(a + z_odd, 2)},
                    device_id_type=MESH,
                ).start()

        if which == 0:
            @pl.when(stays)
            def _():
                own_copy(n).start()

    def half_landing(n, from_y, which):
        columns = pl.multiple_of(from_y * tile_x, tile_x)
        if n == SPEED:
            return vel.at[pl.ds(which * middle, middle), pl.ds(columns, tile_x), :]
        return field.at[
            places[n], pl.ds(4 + which * middle, middle), pl.ds(pl.multiple_of(8 + columns, 8), tile_x), :
        ]

    def half_copy(n, a):
        return pltpu.make_async_remote_copy(
            src_ref=sources[n].at[pl.ds(a * n_i + shot * middle, middle)], dst_ref=half_landing(n, y, shot),
            send_sem=rt_send.at[n, a], recv_sem=rt_recv.at[n, y],
            device_id={"xline": mate, "inline": lax.rem(a + z_odd, 2)}, device_id_type=MESH,
        )

    def half_arrival(n):
        return pltpu.make_async_remote_copy(
            src_ref=sources[n].at[pl.ds(0, middle)], dst_ref=half_landing(n, 1 - y, shot),
            send_sem=rt_send.at[n, 0], recv_sem=rt_recv.at[n, 1 - y],
            device_id={"xline": mate}, device_id_type=MESH,
        )

    def pass_on(n):
        return pltpu.make_async_remote_copy(
            src_ref=half_landing(n, 1 - y, shot), dst_ref=half_landing(n, 1 - y, shot),
            send_sem=pass_send.at[n], recv_sem=pass_recv.at[n],
            device_id={"shots": 1 - shot}, device_id_type=MESH,
        )

    def passed_on(n):
        return pltpu.make_async_remote_copy(
            src_ref=half_landing(n, 1 - y, shot), dst_ref=half_landing(n, 1 - y, 1 - shot),
            send_sem=pass_send.at[n], recv_sem=pass_recv.at[n],
            device_id={"shots": 1 - shot}, device_id_type=MESH,
        )

    def list_copy(a):
        return pltpu.make_async_remote_copy(
            src_ref=list_out, dst_ref=list_in.at[y],
            send_sem=list_send.at[a], recv_sem=list_recv.at[y],
            device_id={"xline": 2 * plane + core, "inline": lax.rem(a + z_odd, 2)},
            device_id_type=MESH,
        )

    def list_arrival(from_y):
        return pltpu.make_async_remote_copy(
            src_ref=list_out, dst_ref=list_in.at[from_y],
            send_sem=list_send.at[0], recv_sem=list_recv.at[from_y],
            device_id={"xline": mate}, device_id_type=MESH,
        )

    def obs_copy(peer, slot):
        return pltpu.make_async_remote_copy(
            src_ref=observed, dst_ref=obs_in.at[slot],
            send_sem=obs_send.at[peer], recv_sem=obs_recv.at[slot],
            device_id={"xline": peer // 2, "inline": lax.rem(peer, 2)}, device_id_type=MESH,
        )

    finals = (previous_out, last_out)
    final_idx = (2 + (steps - 1) % 2, 2 + steps % 2)

    def home_copy(n, to_y):
        return pltpu.make_async_remote_copy(
            src_ref=field.at[final_idx[n], inner_i, pl.ds(8 + to_y * tile_x, tile_x), :],
            dst_ref=finals[n].at[pl.ds(cp * n_i, n_i)],
            send_sem=ret_send.at[n, to_y], recv_sem=ret_recv.at[n, cp],
            device_id={"xline": 2 * plane + to_y, "inline": origin}, device_id_type=MESH,
        )

    def home_arrival(n, a):
        return pltpu.make_async_remote_copy(
            src_ref=field.at[final_idx[n], inner_i, pl.ds(8, tile_x), :],
            dst_ref=finals[n].at[pl.ds(a * n_i, n_i)],
            send_sem=ret_send.at[n, 0], recv_sem=ret_recv.at[n, a],
            device_id={"xline": mate}, device_id_type=MESH,
        )

    def home_own(n):
        columns = pl.multiple_of(8 + y * tile_x, 8)
        return pltpu.make_async_copy(
            field.at[final_idx[n], inner_i, pl.ds(columns, tile_x), :],
            finals[n].at[pl.ds(cp * n_i, n_i)], ret_local.at[n],
        )

    def home_start(n):
        for to_y in range(2):
            @pl.when(arrives(to_y))
            def _():
                home_copy(n, to_y).start()

        @pl.when(stays)
        def _():
            home_own(n).start()

    def home_finish(n):
        for to_y in range(2):
            @pl.when(arrives(to_y))
            def _():
                home_copy(n, to_y).wait_send()
        for a in range(2):
            @pl.when(leaves(a))
            def _():
                home_arrival(n, a).wait_recv()

        @pl.when(stays)
        def _():
            home_own(n).wait()

    dz = depth // n_xline
    planes_n = n_xline // 2

    def slab_copy(d):
        return pltpu.make_async_remote_copy(
            src_ref=g_send.at[d],
            dst_ref=grad_out.at[cp, :, pl.ds(pl.multiple_of(plane * n_x, 8), n_x), :],
            send_sem=g_ssem.at[d], recv_sem=g_rsem.at[cp, plane],
            device_id={"xline": d, "inline": origin}, device_id_type=MESH,
        )

    def own_slab():
        return pltpu.make_async_copy(
            g_send.at[xl], grad_out.at[cp, :, pl.ds(pl.multiple_of(plane * n_x, 8), n_x), :], g_local.at[0]
        )

    def slab_arrival(a, p):
        return pltpu.make_async_remote_copy(
            src_ref=g_send.at[0],
            dst_ref=grad_out.at[a, :, pl.ds(pl.multiple_of(p * n_x, 8), n_x), :],
            send_sem=g_ssem.at[0], recv_sem=g_rsem.at[a, p],
            device_id={"xline": mate}, device_id_type=MESH,
        )

    def fused_gradient():
        group = 128 // dz
        lane = div(lax.broadcasted_iota(jnp.int32, (n_x, 128), 1), dz)
        for chunk in range(depth // 128):
            for ig in range(n_i // group):
                planes = [image[ig * group + j, :, pl.ds(chunk * 128, 128)] for j in range(group)]
                for dd in range(group):
                    out = None
                    for j in range(group):
                        shift = (j - dd) * dz % 128
                        moved = pltpu.roll(planes[j], shift, axis=1) if shift else planes[j]
                        out = moved if out is None else jnp.where(lane == j, moved, out)
                    g_send[chunk * group + dd, ig] = out

        @pl.loop(1, n_xline + 1)
        def _(r):
            d = lax.rem(xl + r, n_xline)

            @pl.when(jnp.logical_or(d != xl, origin != core))
            def _():
                slab_copy(d).start()

        home_start(1)

        @pl.when(origin == core)
        def _():
            own_slab().start()

        @pl.loop(0, n_xline)
        def _(r):
            a, p = lax.rem(r, 2), r // 2
            mine = jnp.logical_and(origin == core, jnp.logical_and(a == cp, p == plane))

            @pl.when(jnp.logical_not(mine))
            def _():
                slab_arrival(a, p).wait_recv()

        @pl.when(origin == core)
        def _():
            own_slab().wait()

        @pl.loop(1, n_xline + 1)
        def _(r):
            d = lax.rem(xl + r, n_xline)

            @pl.when(jnp.logical_or(d != xl, origin != core))
            def _():
                slab_copy(d).wait_send()

    for way in (LEFT, RIGHT, UP, DOWN):
        @pl.when(jnp.logical_not(has[way]))
        def _():
            halo = x_in if way < UP else i_in
            halo[:, way % 2] = jnp.zeros(halo.shape[:1] + halo.shape[2:], jnp.float32)
    image[...] = jnp.zeros(image.shape, jnp.float32)

    for copy in small:
        copy.wait()
    n_counts = rec_counts.shape[1]
    spread = (
        div(lax.broadcasted_iota(jnp.int32, (n_counts, slots), 1), CAP)
        == lax.broadcasted_iota(jnp.int32, (n_counts, slots), 0)
    ).astype(jnp.float32).astype(jnp.bfloat16)
    counts = jnp.broadcast_to(rec_counts[...].astype(jnp.float32), (8, n_counts)).astype(jnp.bfloat16)
    live = dot(counts, spread)
    place = mod(lax.broadcasted_iota(jnp.int32, (8, slots), 1), CAP).astype(jnp.float32)
    list_out[...] = jnp.where(place < live, jnp.broadcast_to(rec_cells[...], (8, slots)), -1)

    pl.semaphore_wait(barrier, greeted)

    for a in range(2):
        @pl.when(leaves(a))
        def _():
            list_copy(a).start()

    for n in (RHO, SPEED, NOW):
        tile_start(n)
    tile_start(BEFORE)

    obs_in[me] = observed[...]

    @pl.when(stays)
    def _():
        list_in[y] = list_out[...]

    offset = lax.broadcasted_iota(jnp.int32, (depth, depth), 0) - lax.broadcasted_iota(jnp.int32, (depth, depth), 1)
    second = jnp.zeros((depth, depth), jnp.float32)
    first = jnp.zeros((depth, depth), jnp.float32)
    for k in range(1, 5):
        second = jnp.where((offset == k) | (offset == -k), SECOND_COEFFS[k] / SECOND_COEFFS[1], second)
        first = jnp.where(offset == k, FIRST_COEFFS[k - 1] / FIRST_COEFFS[0], first)
        first = jnp.where(offset == -k, -FIRST_COEFFS[k - 1] / FIRST_COEFFS[0], first)
    z_mat[:, pl.ds(0, depth)] = second.astype(jnp.bfloat16)
    z_mat[:, pl.ds(depth, depth)] = first.astype(jnp.bfloat16)

    at = lax.broadcasted_iota(jnp.int32, (rows, rows), 0)
    to = lax.broadcasted_iota(jnp.int32, (rows, rows), 1)
    step_i = div(to, n_x) - div(at, n_x)
    step_x = mod(to, n_x) - mod(at, n_x)
    lateral_lap = jnp.zeros((rows, rows), jnp.float32)
    for n, (along, still) in enumerate(((step_i, step_x), (step_x, step_i))):
        along = jnp.where(still == 0, along, 0)
        first = jnp.zeros((rows, rows), jnp.float32)
        for k in range(1, 5):
            lateral_lap = jnp.where((along == k) | (along == -k), SECOND_COEFFS[k] / SECOND_COEFFS[1], lateral_lap)
            first = jnp.where(along == k, FIRST_COEFFS[k - 1] / FIRST_COEFFS[0], first)
            first = jnp.where(along == -k, -FIRST_COEFFS[k - 1] / FIRST_COEFFS[0], first)
        row_mat[pl.ds((n + 1) * rows, rows), :] = first.astype(jnp.bfloat16)
    row_mat[pl.ds(0, rows), :] = lateral_lap.astype(jnp.bfloat16)

    full_x = tile_x * n_xline
    cells = src_cell[...]
    src_i = div(cells, full_x * depth) - q * n_i
    src_x = mod(div(cells, depth), full_x) - plane * n_x
    inside = (src_i >= 0) & (src_i < n_i) & (src_x >= 0) & (src_x < n_x)
    src_row = jnp.where(inside, src_i * n_x + src_x, -1)
    n_src = cells.shape[1]
    src_rows = (lax.broadcasted_iota(jnp.int32, (rows, n_src), 0) == src_row).astype(jnp.float32)
    src_cols = (lax.broadcasted_iota(jnp.int32, (depth, n_src), 0) == mod(cells, depth)).astype(jnp.float32).astype(jnp.bfloat16)

    def flat(idx):
        return field[idx, inner_i, inner_x, :].reshape(rows, depth)

    def differences(idx):
        high, low = split_bf16(flat(idx))
        wide[...] = dot(row_mat[...], high) + dot(row_mat[...], low)
        deep[...] = dot(high, z_mat[...]) + dot(low, z_mat[...])

    def operator(idx, i):
        def line(n):
            return pl.ds(pl.multiple_of(n * rows + i * n_x, n_x), n_x)

        center = field[idx, i + 4, inner_x, :]
        return center, (
            3.0 * SECOND_COEFFS[0] * center
            + SECOND_COEFFS[1] * (wide[line(0), :] + deep[line(0), pl.ds(0, depth)])
            - slopes[0, i] * wide[line(1), :] - slopes[1, i] * wide[line(2), :]
            - slopes[2, i] * deep[line(0), pl.ds(depth, depth)]
        )

    def across(idx, i):
        lap = slope_i = slope_x = None
        for k in range(1, 5):
            plus_i = field[idx, i + 4 + k, inner_x, :]
            minus_i = field[idx, i + 4 - k, inner_x, :]
            plus_x = field[idx, i + 4, pl.ds(8 + k, n_x), :]
            minus_x = field[idx, i + 4, pl.ds(8 - k, n_x), :]
            terms = (
                SECOND_COEFFS[k] * ((plus_i + minus_i) + (plus_x + minus_x)),
                FIRST_COEFFS[k - 1] * (plus_i - minus_i),
                FIRST_COEFFS[k - 1] * (plus_x - minus_x),
            )
            if lap is None:
                lap, slope_i, slope_x = terms
            else:
                lap, slope_i, slope_x = lap + terms[0], slope_i + terms[1], slope_x + terms[2]
        return lap, slope_i, slope_x

    for n in shares:
        half_arrival(n).wait_recv()
        pass_on(n).start()
    tile_finish(RHO)
    send_all(DENSITY)
    tile_finish(NOW)
    send_all(0)

    high, low = split_bf16(flat(DENSITY))
    deep[...] = dot(high, z_mat[...]) + dot(low, z_mat[...])
    slopes[2] = ((FIRST_COEFFS[0] * FIRST_COEFFS[0]) * deep[:, pl.ds(depth, depth)]).reshape(n_i, n_x, depth)
    differences(0)

    def inject_sources(t):
        high, low = split_bf16(src_rows * wavelet[pl.ds(t, 1), :])
        return dot_nt(high, src_cols) + dot_nt(low, src_cols)

    accel[0] = inject_sources(0).reshape(n_i, n_x, depth)

    for from_y in range(2):
        @pl.when(arrives(from_y))
        def _():
            list_arrival(from_y).wait_recv()
    for a in range(2):
        @pl.when(leaves(a))
        def _():
            list_copy(a).wait_send()
    for from_y in range(2):
        spot = list_in[from_y][:1]
        cell_i = div(spot, tile_x * depth) - cp * n_i
        cell_x = mod(div(spot, depth), tile_x) + from_y * tile_x
        row = jnp.where((spot >= 0) & (cell_i >= 0) & (cell_i < n_i), cell_i * n_x + cell_x, -1)
        columns = pl.ds(from_y * slots, slots)
        row_map[:, columns] = (lax.broadcasted_iota(jnp.int32, (rows, slots), 0) == row).astype(jnp.float32)
        zmap_t[:, columns] = (
            lax.broadcasted_iota(jnp.int32, (depth, slots), 0) == mod(spot, depth)
        ).astype(jnp.float32).astype(jnp.bfloat16)

    for part, d, c in pieces:
        finish(DENSITY, part, d, c)
    sent(DENSITY)
    for d in range(layers):
        lanes = pl.ds(d * 128, 128)
        for side in range(2):
            for c in range(2):
                field[DENSITY, pl.ds(side * (n_i + 4), 4), pl.ds(8 + c * half_x, half_x), lanes] = i_in[DENSITY, side, d, c]
            field[DENSITY, inner_i, pl.ds(4 + side * (n_x + 4), 4), lanes] = x_in[DENSITY, side, d]

    @pl.loop(0, n_i)
    def _(i):
        _, slope_i, slope_x = across(DENSITY, i)
        slopes[0, i] = FIRST_COEFFS[0] * slope_i
        slopes[1, i] = FIRST_COEFFS[0] * slope_x

    tile_finish(SPEED)
    column = lax.broadcasted_iota(jnp.int32, (n_x, depth), 0)

    @pl.loop(0, n_i)
    def _(i):
        square = vel[i] * vel[i]
        speed_sq[i] = square
        accel[0, i] += square * operator(0, i)[1]
        for k in range(1, 5):
            weight = jnp.where(
                column < k, SECOND_COEFFS[k] + (FIRST_COEFFS[k - 1] / FIRST_COEFFS[0]) * slopes[1, i],
                jnp.where(
                    column >= n_x - k, SECOND_COEFFS[k] - (FIRST_COEFFS[k - 1] / FIRST_COEFFS[0]) * slopes[1, i], 0.0
                ),
            )
            wx[k - 1, i] = square * weight

    tile_finish(BEFORE)

    @pl.loop(0, n_i)
    def _(i):
        field[1, i + 4, inner_x, :] = (
            2.0 * field[0, i + 4, inner_x, :] - field[1, i + 4, inner_x, :] + accel[0, i]
        )

    def start_traces(third):
        @pl.loop(1 + (n_group - 1) * third // 3, 1 + (n_group - 1) * (third + 1) // 3)
        def _(r):
            obs_copy(lax.rem(me + r, n_group), me).start()

    def make_traces(from_y):
        @pl.loop(1, n_group)
        def _(r):
            peer = lax.rem(me + r, n_group)
            if from_y == 0:
                obs_copy(peer, peer).wait_recv()
            else:
                obs_copy(peer, me).wait_send()

        lane = div(lax.broadcasted_iota(jnp.int32, (8, slots), 1), CAP)
        owner = (2 * plane + from_y) * 2 + origin

        def place_one(s, total):
            moved = pltpu.roll(obs_in[s], lax.rem(s - owner + n_group, n_group) * CAP, axis=1)
            return jnp.where(lane == s, moved, total)

        traces[:, pl.ds(from_y * slots, slots)] = lax.fori_loop(
            0, n_group, place_one, jnp.zeros((8, slots), jnp.float32)
        )

    def prepare(idx, term):
        base[...] = term.reshape(n_i, n_x, depth)
        differences(idx)

    def interior(now, other, i):
        center, value = operator(now, i)
        change = base[i] + speed_sq[i] * value
        field[other, i + 4, inner_x, :] = 2.0 * center - field[other, i + 4, inner_x, :] + change
        return center, change

    def correct(now, other, part, d, c, t):
        up = part == 0
        sign = jnp.where(up, 1.0, -1.0)
        columns, lanes = pl.ds(c * half_x, half_x), pl.ds(d * 128, 128)
        for r in range(middle):
            i = jnp.where(up, r, n_i - 1 - r)
            halo = x_in[now, c, d, i]
            pair = jnp.concatenate([halo] * (half_x // 4), axis=0)
            change = wx[3, i, columns, lanes] * pair
            for k in range(1, 4):
                change += wx[k - 1, i, columns, lanes] * pltpu.roll(pair, half_x - k if c else k, axis=0)
            lap = None
            for h in range(4 - r):
                k = r + 1 + h
                halo = i_in[now, part, d, c, jnp.where(up, 3 - h, h)]
                terms = SECOND_COEFFS[k] * halo, (FIRST_COEFFS[k - 1] / FIRST_COEFFS[0]) * halo
                lap, slope = terms if lap is None else (lap + terms[0], slope + terms[1])
            if lap is not None:
                change += speed_sq[i, columns, lanes] * (lap + (sign * slopes[0, i, columns, lanes]) * slope)
            spot = (other, i + 4, pl.ds(8 + c * half_x, half_x), lanes)
            fresh = field[spot] + change
            field[spot] = fresh
            x_out[other, c, d, i] = fresh[half_x - 4:] if c else fresh[:4]
            if r < 4:
                i_out[other, part, d, c, jnp.where(up, r, 3 - r)] = fresh
            if t is not None:
                accel[t, i, columns, lanes] += change

    def sample(idx, t):
        high, low = split_bf16(flat(idx))
        picked = dot(high, zmap_t[...]) + dot(low, zmap_t[...])
        predicted = jnp.sum(picked * row_map[...], axis=0, keepdims=True)
        residual_ref[t] = predicted

    def task_first():
        quarter_start(ADJ_NOW, 0)

    def task_second():
        quarter_start(ADJ_NOW, 1)

    def task_third():
        quarter_start(ADJ_BEFORE, 0)
        start_traces(0)

    def task_halos():
        quarter_start(ADJ_BEFORE, 1)
        start_traces(1)
        tile_finish(ADJ_NOW)
        send_all(2)

    def task_adjoint():
        tile_finish(ADJ_BEFORE)
        differences(2)
        vel[...] = (2.0 / steps) / vel[...]
        start_traces(2)

        @pl.loop(0, n_i, unroll=2)
        def _(i):
            center, value = operator(2, i)
            field[3, i + 4, inner_x, :] = (
                2.0 * center - field[3, i + 4, inner_x, :] + speed_sq[i] * value
            )

    tasks = [task_first, task_second, task_third, task_halos, task_adjoint]
    tasks += [functools.partial(make_traces, 0), functools.partial(make_traces, 1)]
    times = [1 + n * (steps - 1) // len(tasks) for n in range(len(tasks))]

    @pl.loop(0, steps)
    def _(t):
        now = lax.rem(t, 2)
        other = 1 - now

        @pl.when(t > 0)
        def _():
            prepare(now, inject_sources(t))

            @pl.loop(0, n_i, unroll=2)
            def _(i):
                _, change = interior(now, other, i)
                accel[t, i] = change

        for at, task in zip(times, tasks):
            pl.when(t == at)(task)

        @pl.when(t >= 1)
        def _():
            sample(now, t - 1)
            sent(other)

        for part, d, c in pieces:
            finish(now, part, d, c)
            correct(now, other, part, d, c, t)

            @pl.when(t < steps - 1)
            def _():
                send(other, part, d, c)

    sent((steps - 1) % 2)
    sample(steps % 2, steps - 1)

    @pl.loop(0, steps)
    def _(j):
        now = 2 + lax.rem(j, 2)
        other = 5 - now
        t = steps - 1 - j
        high, low = split_bf16(row_map[...] * (residual_ref[t] - traces[pl.ds(t, 1), :]))
        injected = dot_nt(high, zmap_t[...]) + dot_nt(low, zmap_t[...])

        @pl.when(j == 0)
        def _():
            field[3, inner_i, inner_x, :] += injected.reshape(n_i, n_x, depth)

        @pl.when(j > 0)
        def _():
            prepare(now, injected)

            @pl.loop(0, n_i, unroll=2)
            def _(i):
                center, _ = interior(now, other, i)
                image[i] += center * accel[t + 1, i]

            sent(other)

        @pl.when(j == steps - 1)
        def _():
            home_start(0)

        for part, d, c in pieces:
            finish(now, part, d, c)
            correct(now, other, part, d, c, None)

            @pl.when(j < steps - 1)
            def _():
                send(other, part, d, c)

    sent(2 + (steps - 1) % 2)

    @pl.loop(0, n_i, unroll=4)
    def _(i):
        image[i] = (image[i] + field[final_idx[1], i + 4, inner_x, :] * accel[0, i]) * vel[i]

    if fused:
        fused_gradient()
    else:
        grad_out[...] = image[...]
        home_start(1)
    home_finish(0)
    home_finish(1)


def finish_kernel(shape, slabs, last, previous):
    dz, tile_i, full_x = shape
    _, n_groups, _, lanes = slabs.shape
    group = lanes // dz

    def kernel(
        slabs_in, last_in, previous_in, gradient, last_out, previous_out,
        slabs_held, last_held, previous_held, lines_held, in_sem, out_sem,
    ):
        loads = [
            pltpu.make_async_copy(slabs_in, slabs_held, in_sem.at[0]),
            pltpu.make_async_copy(last_in, last_held, in_sem.at[1]),
            pltpu.make_async_copy(previous_in, previous_held, in_sem.at[2]),
        ]
        for load in loads:
            load.start()
        far = (
            lax.broadcasted_iota(jnp.int32, (full_x, full_x), 0) - lax.broadcasted_iota(jnp.int32, (full_x, full_x), 1)
        ).astype(jnp.float32)
        weights = jnp.exp(-jnp.abs(far) / SMOOTH)
        weights = weights / jnp.sum(weights, axis=0, keepdims=True)
        stores = [
            pltpu.make_async_copy(last_held, last_out, out_sem.at[0]),
            pltpu.make_async_copy(previous_held, previous_out, out_sem.at[1]),
        ]
        for load, store in zip(loads[1:], stores):
            load.wait()
            store.start()
        loads[0].wait()
        for a in range(2):
            for ig in range(n_groups):
                lines = dot_tn_exact(slabs_held[a, ig], weights)
                for j in range(group):
                    lines_held[:, (a * n_groups + ig) * group + j, :] = lines[j * dz:(j + 1) * dz]
            span = pl.ds(a * (tile_i // 2), tile_i // 2)
            store = pltpu.make_async_copy(lines_held.at[:, span, :], gradient.at[:, span, :], out_sem.at[2 + a])
            store.start()
            stores.append(store)
        for store in stores:
            store.wait()

    anywhere = pl.BlockSpec(memory_space=pl.ANY)
    return pl.pallas_call(
        kernel,
        out_shape=[jax.ShapeDtypeStruct(dims, jnp.float32) for dims in (shape, last.shape, previous.shape)],
        in_specs=[anywhere] * 3,
        out_specs=[anywhere] * 3,
        scratch_shapes=[
            *[pltpu.VMEM(dims, jnp.float32) for dims in (slabs.shape, last.shape, previous.shape, shape)],
            pltpu.SemaphoreType.DMA((3,)),
            pltpu.SemaphoreType.DMA((4,)),
        ],
        compiler_params=pltpu.CompilerParams(vmem_limit_bytes=56 * 1024 * 1024),
    )(slabs, last, previous)


def per_device(
    fwd_now, fwd_before, adj_now, adj_before, velocity, log_density,
    observed, rec_cells, rec_counts, src_cell, wavelet,
):
    tile_i, tile_x, depth = fwd_now.shape
    steps = wavelet.shape[0]
    n_xline = lax.axis_size("xline")
    full_x = tile_x * n_xline
    n_i, n_x = tile_i // 2, tile_x * 2
    rows = n_i * n_x
    slots = rec_cells.shape[1]
    n_group = 2 * n_xline
    dz = depth // n_xline
    fused = dz >= 8 and 128 % dz == 0 and depth % 128 == 0 and n_i % (128 // dz) == 0
    group = 128 // dz if fused else 1
    layers = depth // 128

    block = (n_i, n_x, depth)
    vmem = pl.BlockSpec(memory_space=pltpu.VMEM)
    anywhere = pl.BlockSpec(memory_space=pl.ANY)
    dma = pltpu.SemaphoreType.DMA
    kernel = functools.partial(wave_kernel, (tile_i, tile_x, n_i, n_x, depth, steps, n_xline, fused))
    grad_shape = (2, n_i // group, full_x, 128) if fused else block
    slab_shape = (n_xline, n_i // group, n_x, 128) if fused else (8, 128)
    small_shapes = [observed, rec_cells, rec_counts, src_cell[None, :], wavelet]
    raw, last, previous = pl.pallas_call(
        kernel,
        out_shape=[
            jax.ShapeDtypeStruct(grad_shape, jnp.float32),
            jax.ShapeDtypeStruct(fwd_now.shape, jnp.float32),
            jax.ShapeDtypeStruct(fwd_now.shape, jnp.float32),
        ],
        in_specs=[anywhere] * 11,
        out_specs=[anywhere if fused else vmem, anywhere, anywhere],
        scratch_shapes=[
            pltpu.VMEM((5, n_i + 8, n_x + 16, depth), jnp.float32),
            pltpu.VMEM(block, jnp.float32),
            pltpu.VMEM((5, 2, layers, n_i, 4, 128), jnp.float32),
            pltpu.VMEM((5, 2, layers, n_i, 4, 128), jnp.float32),
            pltpu.VMEM((5, 2, layers, 2, 4, tile_x, 128), jnp.float32),
            pltpu.VMEM((5, 2, layers, 2, 4, tile_x, 128), jnp.float32),
            pltpu.VMEM((steps,) + block, jnp.float32),
            pltpu.VMEM(block, jnp.float32),
            pltpu.VMEM(block, jnp.float32),
            pltpu.VMEM((3,) + block, jnp.float32),
            pltpu.VMEM(block, jnp.float32),
            pltpu.VMEM((4,) + block, jnp.float32),
            pltpu.VMEM((rows, 2 * slots), jnp.float32),
            pltpu.VMEM((depth, 2 * slots), jnp.bfloat16),
            pltpu.VMEM((depth, 2 * depth), jnp.bfloat16),
            pltpu.VMEM((steps, 1, 2 * slots), jnp.float32),
            pltpu.VMEM((steps, 2 * slots), jnp.float32),
            pltpu.VMEM((8, slots), jnp.int32),
            pltpu.VMEM((2, 8, slots), jnp.int32),
            pltpu.VMEM((n_group,) + observed.shape, jnp.float32),
            pltpu.VMEM(slab_shape, jnp.float32),
            *[pltpu.VMEM(value.shape, value.dtype) for value in small_shapes],
            pltpu.VMEM((3 * rows, rows), jnp.bfloat16),
            pltpu.VMEM((3 * rows, depth), jnp.float32),
            pltpu.VMEM((rows, 2 * depth), jnp.float32),
            dma((5, 2)), dma((5, 2, 2, layers)), dma((5, 2)), dma((5, 2, 2, layers)),
            dma((6, 2)), dma((6, 2)), dma((6,)),
            dma((2,)), dma((2,)),
            dma((n_group,)), dma((n_group,)),
            dma((2, 2)), dma((2, 2)), dma((2,)),
            dma((n_xline,)), dma((2, n_xline // 2)), dma((1,)), dma((5,)),
            dma((6,)), dma((6,)),
        ],
        compiler_params=pltpu.CompilerParams(
            collective_id=0, has_side_effects=True, vmem_limit_bytes=56 * 1024 * 1024
        ),
    )(
        log_density, fwd_now, velocity, fwd_before, adj_now, adj_before,
        *small_shapes,
    )
    if fused:
        return finish_kernel((dz, tile_i, full_x), raw, last, previous)

    places = []
    for xl in range(n_xline):
        for core in range(2):
            y, plane = xl % 2, xl // 2
            cp = (core + plane % 2) % 2
            places.append((xl * 2 + core, (2 * plane + cp) * 2 + y))
    raw = lax.ppermute(raw, ("xline", "inline"), places)
    columns = lax.all_to_all(
        raw.reshape(n_i, n_x, n_xline, dz).transpose(2, 0, 1, 3),
        "xline", split_axis=0, concat_axis=0, tiled=True,
    ).reshape(n_xline // 2, 2, n_i, n_x, dz)
    positions = jnp.arange(full_x).astype(jnp.float32)
    weights = jnp.exp(-jnp.abs(positions[:, None] - positions[None, :]) / SMOOTH)
    weights = weights / jnp.sum(weights, axis=1, keepdims=True)
    gradient = jnp.einsum(
        "phixz,ypx->zhiy", columns, weights.reshape(full_x, n_xline // 2, n_x),
        precision=lax.Precision.HIGHEST,
    ).reshape(dz, tile_i, full_x)
    return gradient, last, previous


def solution(mesh):
    return jax.shard_map(
        per_device,
        mesh=mesh,
        in_specs=(
            P(("shots", "inline"), "xline", None),
            P(("shots", "inline"), "xline", None),
            P(("shots", "inline"), "xline", None),
            P(("shots", "inline"), "xline", None),
            P("inline", "xline", None),
            P("inline", "xline", None),
            P("shots", ("xline", "inline")),
            P(("xline", "inline"), None),
            P(("xline", "inline"), None),
            P("shots"),
            P("shots", None),
        ),
        out_specs=(
            P(("shots", "xline"), "inline", None),
            P(("shots", "inline"), "xline", None),
            P(("shots", "inline"), "xline", None),
        ),
        check_vma=False,
    )
```

```python
import functools

import jax
import jax.numpy as jnp
from jax import lax
from jax.experimental import pallas as pl
from jax.experimental.pallas import tpu as pltpu
from jax.sharding import PartitionSpec as P

CAP = 8
SMOOTH = 16
MESH = pl.DeviceIdType.MESH

SECOND_COEFFS = (-205.0 / 72.0, 8.0 / 5.0, -1.0 / 5.0, 8.0 / 315.0, -1.0 / 560.0)
FIRST_COEFFS = (4.0 / 5.0, -1.0 / 5.0, 4.0 / 105.0, -1.0 / 280.0)
LEFT, RIGHT, UP, DOWN = 0, 1, 2, 3
DENSITY = 4
RHO, NOW, SPEED, BEFORE, ADJ_NOW, ADJ_BEFORE = range(6)


def split_bf16(value):
    high = value.astype(jnp.bfloat16)
    low = (value - high.astype(jnp.float32)).astype(jnp.bfloat16)
    return high, low


def dot(a, b):
    return jnp.dot(a, b, preferred_element_type=jnp.float32)


def dot_nt(a, b):
    return lax.dot_general(a, b, (((1,), (1,)), ((), ())), preferred_element_type=jnp.float32)


def dot_tn_exact(a, b):
    dims = (((0,), (0,)), ((), ()))
    ah, al = split_bf16(a)
    bh, bl = split_bf16(b)
    one = lax.dot_general(ah, bh, dims, preferred_element_type=jnp.float32)
    two = lax.dot_general(al, bh, dims, preferred_element_type=jnp.float32)
    three = lax.dot_general(ah, bl, dims, preferred_element_type=jnp.float32)
    return one + (two + three)


def div(value, n):
    return lax.shift_right_arithmetic(value, jnp.full_like(value, n.bit_length() - 1))


def mod(value, n):
    return value & (n - 1)


def wave_kernel(
    sizes,
    log_density, fwd_now, velocity, fwd_before, adj_now, adj_before,
    given_observed, given_cells, given_counts, given_src, given_wavelet,
    grad_out, last_out, previous_out,
    field, vel, x_in, x_out, i_in, i_out, accel, base, image, slopes, speed_sq, wx,
    row_map, zmap_t, z_mat, residual_ref, traces, list_out, list_in, obs_in, g_send,
    held_observed, held_cells, held_counts, held_src, held_wavelet, row_mat, wide, deep,
    x_send, x_recv, i_send, i_recv, rt_send, rt_recv, rt_local, list_send, list_recv, obs_send, obs_recv,
    ret_send, ret_recv, ret_local, g_ssem, g_rsem, g_local, small_sem, pass_send, pass_recv,
):
    tile_i, tile_x, n_i, n_x, depth, steps, n_xline, fused = sizes
    rows = n_i * n_x
    small_in = (given_observed, given_cells, given_counts, given_src, given_wavelet)
    small_held = (held_observed, held_cells, held_counts, held_src, held_wavelet)
    slots = held_cells.shape[1]
    n_group = 2 * n_xline
    xl = lax.axis_index("xline")
    core = lax.axis_index("inline")
    me = xl * 2 + core
    y = lax.rem(xl, 2)
    plane = xl // 2
    z_odd = lax.rem(plane, 2)
    mate = xl + 1 - 2 * y
    cp = lax.rem(core + z_odd, 2)
    origin = y
    q = 2 * y + cp
    stays = y == core
    has = (xl >= 2, xl < n_xline - 2, q > 0, q < 3)
    other_core = 1 - core
    shot = lax.axis_index("shots")
    shares = (RHO, SPEED) if lax.axis_size("shots") == 2 else ()
    target = (
        {"xline": xl - 2, "inline": other_core},
        {"xline": xl + 2, "inline": other_core},
        {"xline": jnp.where(q == 2, mate, xl), "inline": other_core},
        {"xline": jnp.where(q == 1, mate, xl), "inline": other_core},
    )
    inner_i = pl.ds(4, n_i)
    inner_x = pl.ds(8, n_x)
    middle = n_i // 2

    barrier = pltpu.get_barrier_semaphore()

    def greet(device):
        pl.semaphore_signal(barrier, inc=1, device_id=device, device_id_type=MESH)

    near = n_xline // 2 <= 4
    if near:
        greet({"inline": other_core})
        greet({"xline": mate})
        greet({"xline": mate, "inline": other_core})
        for way in (LEFT, RIGHT):
            @pl.when(has[way])
            def _():
                greet(target[way])
        greeted = 3 + has[LEFT].astype(jnp.int32) + has[RIGHT].astype(jnp.int32)
    else:
        @pl.loop(1, n_group)
        def _(r):
            peer = lax.rem(me + r, n_group)
            greet({"xline": peer // 2, "inline": lax.rem(peer, 2)})
        greeted = n_group - 1
    if shares:
        greet({"shots": 1 - shot})
        greeted = greeted + 1

    small = [
        pltpu.make_async_copy(given, held, small_sem.at[n])
        for n, (given, held) in enumerate(zip(small_in, small_held))
    ]
    for copy in small:
        copy.start()
    observed, rec_cells, rec_counts, src_cell, wavelet = small_held

    layers = depth // 128
    half_x = n_x // 2

    def beside(idx, way, part, d):
        part_rows = pl.ds(part * middle, middle)
        return pltpu.make_async_remote_copy(
            src_ref=x_out.at[idx, way, d, part_rows], dst_ref=x_in.at[idx, 1 - way, d, part_rows],
            send_sem=x_send.at[idx, way], recv_sem=x_recv.at[idx, way, part, d],
            device_id=target[way], device_id_type=MESH,
        )

    def above(idx, part, c, d, arriving):
        up = part == 0
        return pltpu.make_async_remote_copy(
            src_ref=i_out.at[idx, part, d, c],
            dst_ref=i_in.at[idx, part if arriving else 1 - part, d, c],
            send_sem=i_send.at[idx, part],
            recv_sem=i_recv.at[idx, 1 - part if arriving else part, c, d],
            device_id={
                "xline": jnp.where(up, target[UP]["xline"], target[DOWN]["xline"]), "inline": other_core
            },
            device_id_type=MESH,
        )

    def has_row(part):
        return jnp.where(part == 0, q, 3 - q) > 0

    def send(idx, part, d, c):
        @pl.when(has[c])
        def _():
            beside(idx, c, part, d).start()

        @pl.when(has_row(part))
        def _():
            above(idx, part, c, d, False).start()

    def finish(idx, part, d, c):
        @pl.when(has[c])
        def _():
            beside(idx, 1 - c, part, d).wait_recv()

        @pl.when(has_row(part))
        def _():
            above(idx, part, c, d, True).wait_recv()

    def sent(idx):
        for n in range(2):
            @pl.when(has[n])
            def _():
                pltpu.make_async_remote_copy(
                    src_ref=x_out.at[idx, n], dst_ref=x_in.at[idx, 1 - n],
                    send_sem=x_send.at[idx, n], recv_sem=x_recv.at[idx, n, 0, 0],
                    device_id=target[n], device_id_type=MESH,
                ).wait_send()

            @pl.when(has[UP + n])
            def _():
                pltpu.make_async_remote_copy(
                    src_ref=i_out.at[idx, n], dst_ref=i_in.at[idx, 1 - n],
                    send_sem=i_send.at[idx, n], recv_sem=i_recv.at[idx, n, 0, 0],
                    device_id=target[UP + n], device_id_type=MESH,
                ).wait_send()

    def send_all(idx):
        for part, d, c in pieces:
            rows_at = pl.ds(part * middle, middle)
            x_out[idx, c, d, rows_at] = field[
                idx, pl.ds(4 + part * middle, middle), pl.ds(8 + c * (n_x - 4), 4), pl.ds(d * 128, 128)
            ]
            i_out[idx, part, d, c] = field[
                idx, pl.ds(4 + part * (n_i - 4), 4), pl.ds(8 + c * half_x, half_x), pl.ds(d * 128, 128)
            ]
            send(idx, part, d, c)

    halves = (1 - y, y)
    pieces = [(part, d, c) for part in halves for d in range(layers) for c in range(2)]

    sources = (log_density, fwd_now, velocity, fwd_before, adj_now, adj_before)
    places = (DENSITY, 0, None, 1, 2, 3)

    def landing(n, from_y):
        columns = pl.multiple_of(from_y * tile_x, tile_x)
        if n == SPEED:
            return vel.at[:, pl.ds(columns, tile_x), :]
        return field.at[places[n], inner_i, pl.ds(pl.multiple_of(8 + columns, 8), tile_x), :]

    def tile_copy(n, a):
        return pltpu.make_async_remote_copy(
            src_ref=sources[n].at[pl.ds(a * n_i, n_i)], dst_ref=landing(n, y),
            send_sem=rt_send.at[n, a], recv_sem=rt_recv.at[n, y],
            device_id={"xline": 2 * plane + core, "inline": lax.rem(a + z_odd, 2)},
            device_id_type=MESH,
        )

    def tile_arrival(n, from_y):
        return pltpu.make_async_remote_copy(
            src_ref=sources[n].at[pl.ds(0, n_i)], dst_ref=landing(n, from_y),
            send_sem=rt_send.at[n, 0], recv_sem=rt_recv.at[n, from_y],
            device_id={"xline": mate}, device_id_type=MESH,
        )

    def own_copy(n):
        return pltpu.make_async_copy(
            sources[n].at[pl.ds(cp * n_i, n_i)], landing(n, y), rt_local.at[n]
        )

    def leaves(a):
        return jnp.logical_not(jnp.logical_and(stays, cp == a))

    def arrives(from_y):
        return jnp.logical_not(jnp.logical_and(stays, y == from_y))

    def tile_start(n):
        for a in range(2):
            @pl.when(jnp.logical_and(stays, cp != a) if n in shares else leaves(a))
            def _():
                tile_copy(n, a).start()

        if n in shares:
            for a in range(2):
                @pl.when(jnp.logical_not(stays))
                def _():
                    half_copy(n, a).start()

        @pl.when(stays)
        def _():
            own_copy(n).start()

    def tile_finish(n):
        for from_y in range(2):
            @pl.when(jnp.logical_and(arrives(from_y), y == from_y) if n in shares else arrives(from_y))
            def _():
                tile_arrival(n, from_y).wait_recv()
        for a in range(2):
            @pl.when(jnp.logical_and(stays, cp != a) if n in shares else leaves(a))
            def _():
                tile_copy(n, a).wait_send()

        @pl.when(stays)
        def _():
            own_copy(n).wait()

        if n in shares:
            for a in range(2):
                @pl.when(jnp.logical_not(stays))
                def _():
                    half_copy(n, a).wait_send()
            pass_on(n).wait_send()
            passed_on(n).wait_recv()

    def quarter_start(n, which):
        for a in range(2):
            @pl.when(leaves(a))
            def _():
                pltpu.make_async_remote_copy(
                    src_ref=sources[n].at[pl.ds(a * n_i + which * middle, middle)], dst_ref=half_landing(n, y, which),
                    send_sem=rt_send.at[n, a], recv_sem=rt_recv.at[n, y],
                    device_id={"xline": 2 * plane + core, "inline": lax.rem(a + z_odd, 2)},
                    device_id_type=MESH,
                ).start()

        if which == 0:
            @pl.when(stays)
            def _():
                own_copy(n).start()

    def half_landing(n, from_y, which):
        columns = pl.multiple_of(from_y * tile_x, tile_x)
        if n == SPEED:
            return vel.at[pl.ds(which * middle, middle), pl.ds(columns, tile_x), :]
        return field.at[
            places[n], pl.ds(4 + which * middle, middle), pl.ds(pl.multiple_of(8 + columns, 8), tile_x), :
        ]

    def half_copy(n, a):
        return pltpu.make_async_remote_copy(
            src_ref=sources[n].at[pl.ds(a * n_i + shot * middle, middle)], dst_ref=half_landing(n, y, shot),
            send_sem=rt_send.at[n, a], recv_sem=rt_recv.at[n, y],
            device_id={"xline": mate, "inline": lax.rem(a + z_odd, 2)}, device_id_type=MESH,
        )

    def half_arrival(n):
        return pltpu.make_async_remote_copy(
            src_ref=sources[n].at[pl.ds(0, middle)], dst_ref=half_landing(n, 1 - y, shot),
            send_sem=rt_send.at[n, 0], recv_sem=rt_recv.at[n, 1 - y],
            device_id={"xline": mate}, device_id_type=MESH,
        )

    def pass_on(n):
        return pltpu.make_async_remote_copy(
            src_ref=half_landing(n, 1 - y, shot), dst_ref=half_landing(n, 1 - y, shot),
            send_sem=pass_send.at[n], recv_sem=pass_recv.at[n],
            device_id={"shots": 1 - shot}, device_id_type=MESH,
        )

    def passed_on(n):
        return pltpu.make_async_remote_copy(
            src_ref=half_landing(n, 1 - y, shot), dst_ref=half_landing(n, 1 - y, 1 - shot),
            send_sem=pass_send.at[n], recv_sem=pass_recv.at[n],
            device_id={"shots": 1 - shot}, device_id_type=MESH,
        )

    def list_copy(a):
        return pltpu.make_async_remote_copy(
            src_ref=list_out, dst_ref=list_in.at[y],
            send_sem=list_send.at[a], recv_sem=list_recv.at[y],
            device_id={"xline": 2 * plane + core, "inline": lax.rem(a + z_odd, 2)},
            device_id_type=MESH,
        )

    def list_arrival(from_y):
        return pltpu.make_async_remote_copy(
            src_ref=list_out, dst_ref=list_in.at[from_y],
            send_sem=list_send.at[0], recv_sem=list_recv.at[from_y],
            device_id={"xline": mate}, device_id_type=MESH,
        )

    def obs_copy(peer, slot):
        return pltpu.make_async_remote_copy(
            src_ref=observed, dst_ref=obs_in.at[slot],
            send_sem=obs_send.at[peer], recv_sem=obs_recv.at[slot],
            device_id={"xline": peer // 2, "inline": lax.rem(peer, 2)}, device_id_type=MESH,
        )

    finals = (previous_out, last_out)
    final_idx = (2 + (steps - 1) % 2, 2 + steps % 2)

    def home_copy(n, to_y):
        return pltpu.make_async_remote_copy(
            src_ref=field.at[final_idx[n], inner_i, pl.ds(8 + to_y * tile_x, tile_x), :],
            dst_ref=finals[n].at[pl.ds(cp * n_i, n_i)],
            send_sem=ret_send.at[n, to_y], recv_sem=ret_recv.at[n, cp],
            device_id={"xline": 2 * plane + to_y, "inline": origin}, device_id_type=MESH,
        )

    def home_arrival(n, a):
        return pltpu.make_async_remote_copy(
            src_ref=field.at[final_idx[n], inner_i, pl.ds(8, tile_x), :],
            dst_ref=finals[n].at[pl.ds(a * n_i, n_i)],
            send_sem=ret_send.at[n, 0], recv_sem=ret_recv.at[n, a],
            device_id={"xline": mate}, device_id_type=MESH,
        )

    def home_own(n):
        columns = pl.multiple_of(8 + y * tile_x, 8)
        return pltpu.make_async_copy(
            field.at[final_idx[n], inner_i, pl.ds(columns, tile_x), :],
            finals[n].at[pl.ds(cp * n_i, n_i)], ret_local.at[n],
        )

    def home_start(n):
        for to_y in range(2):
            @pl.when(arrives(to_y))
            def _():
                home_copy(n, to_y).start()

        @pl.when(stays)
        def _():
            home_own(n).start()

    def home_finish(n):
        for to_y in range(2):
            @pl.when(arrives(to_y))
            def _():
                home_copy(n, to_y).wait_send()
        for a in range(2):
            @pl.when(leaves(a))
            def _():
                home_arrival(n, a).wait_recv()

        @pl.when(stays)
        def _():
            home_own(n).wait()

    dz = depth // n_xline
    planes_n = n_xline // 2

    def slab_copy(d):
        return pltpu.make_async_remote_copy(
            src_ref=g_send.at[d],
            dst_ref=grad_out.at[cp, :, pl.ds(pl.multiple_of(plane * n_x, 8), n_x), :],
            send_sem=g_ssem.at[d], recv_sem=g_rsem.at[cp, plane],
            device_id={"xline": d, "inline": origin}, device_id_type=MESH,
        )

    def own_slab():
        return pltpu.make_async_copy(
            g_send.at[xl], grad_out.at[cp, :, pl.ds(pl.multiple_of(plane * n_x, 8), n_x), :], g_local.at[0]
        )

    def slab_arrival(a, p):
        return pltpu.make_async_remote_copy(
            src_ref=g_send.at[0],
            dst_ref=grad_out.at[a, :, pl.ds(pl.multiple_of(p * n_x, 8), n_x), :],
            send_sem=g_ssem.at[0], recv_sem=g_rsem.at[a, p],
            device_id={"xline": mate}, device_id_type=MESH,
        )

    def fused_gradient():
        group = 128 // dz
        lane = div(lax.broadcasted_iota(jnp.int32, (n_x, 128), 1), dz)
        for chunk in range(depth // 128):
            for ig in range(n_i // group):
                planes = [image[ig * group + j, :, pl.ds(chunk * 128, 128)] for j in range(group)]
                for dd in range(group):
                    out = None
                    for j in range(group):
                        shift = (j - dd) * dz % 128
                        moved = pltpu.roll(planes[j], shift, axis=1) if shift else planes[j]
                        out = moved if out is None else jnp.where(lane == j, moved, out)
                    g_send[chunk * group + dd, ig] = out

        @pl.loop(1, n_xline + 1)
        def _(r):
            d = lax.rem(xl + r, n_xline)

            @pl.when(jnp.logical_or(d != xl, origin != core))
            def _():
                slab_copy(d).start()

        home_start(1)

        @pl.when(origin == core)
        def _():
            own_slab().start()

        @pl.loop(0, n_xline)
        def _(r):
            a, p = lax.rem(r, 2), r // 2
            mine = jnp.logical_and(origin == core, jnp.logical_and(a == cp, p == plane))

            @pl.when(jnp.logical_not(mine))
            def _():
                slab_arrival(a, p).wait_recv()

        @pl.when(origin == core)
        def _():
            own_slab().wait()

        @pl.loop(1, n_xline + 1)
        def _(r):
            d = lax.rem(xl + r, n_xline)

            @pl.when(jnp.logical_or(d != xl, origin != core))
            def _():
                slab_copy(d).wait_send()

    for way in (LEFT, RIGHT, UP, DOWN):
        @pl.when(jnp.logical_not(has[way]))
        def _():
            halo = x_in if way < UP else i_in
            halo[:, way % 2] = jnp.zeros(halo.shape[:1] + halo.shape[2:], jnp.float32)
    image[...] = jnp.zeros(image.shape, jnp.float32)

    for copy in small:
        copy.wait()
    n_counts = rec_counts.shape[1]
    spread = (
        div(lax.broadcasted_iota(jnp.int32, (n_counts, slots), 1), CAP)
        == lax.broadcasted_iota(jnp.int32, (n_counts, slots), 0)
    ).astype(jnp.float32).astype(jnp.bfloat16)
    counts = jnp.broadcast_to(rec_counts[...].astype(jnp.float32), (8, n_counts)).astype(jnp.bfloat16)
    live = dot(counts, spread)
    place = mod(lax.broadcasted_iota(jnp.int32, (8, slots), 1), CAP).astype(jnp.float32)
    list_out[...] = jnp.where(place < live, jnp.broadcast_to(rec_cells[...], (8, slots)), -1)

    pl.semaphore_wait(barrier, greeted)

    for a in range(2):
        @pl.when(leaves(a))
        def _():
            list_copy(a).start()

    for n in (RHO, SPEED, NOW):
        tile_start(n)
    tile_start(BEFORE)

    obs_in[me] = observed[...]

    @pl.when(stays)
    def _():
        list_in[y] = list_out[...]

    offset = lax.broadcasted_iota(jnp.int32, (depth, depth), 0) - lax.broadcasted_iota(jnp.int32, (depth, depth), 1)
    second = jnp.zeros((depth, depth), jnp.float32)
    first = jnp.zeros((depth, depth), jnp.float32)
    for k in range(1, 5):
        second = jnp.where((offset == k) | (offset == -k), SECOND_COEFFS[k] / SECOND_COEFFS[1], second)
        first = jnp.where(offset == k, FIRST_COEFFS[k - 1] / FIRST_COEFFS[0], first)
        first = jnp.where(offset == -k, -FIRST_COEFFS[k - 1] / FIRST_COEFFS[0], first)
    z_mat[:, pl.ds(0, depth)] = second.astype(jnp.bfloat16)
    z_mat[:, pl.ds(depth, depth)] = first.astype(jnp.bfloat16)

    at = lax.broadcasted_iota(jnp.int32, (rows, rows), 0)
    to = lax.broadcasted_iota(jnp.int32, (rows, rows), 1)
    step_i = div(to, n_x) - div(at, n_x)
    step_x = mod(to, n_x) - mod(at, n_x)
    lateral_lap = jnp.zeros((rows, rows), jnp.float32)
    for n, (along, still) in enumerate(((step_i, step_x), (step_x, step_i))):
        along = jnp.where(still == 0, along, 0)
        first = jnp.zeros((rows, rows), jnp.float32)
        for k in range(1, 5):
            lateral_lap = jnp.where((along == k) | (along == -k), SECOND_COEFFS[k] / SECOND_COEFFS[1], lateral_lap)
            first = jnp.where(along == k, FIRST_COEFFS[k - 1] / FIRST_COEFFS[0], first)
            first = jnp.where(along == -k, -FIRST_COEFFS[k - 1] / FIRST_COEFFS[0], first)
        row_mat[pl.ds((n + 1) * rows, rows), :] = first.astype(jnp.bfloat16)
    row_mat[pl.ds(0, rows), :] = lateral_lap.astype(jnp.bfloat16)

    full_x = tile_x * n_xline
    cells = src_cell[...]
    src_i = div(cells, full_x * depth) - q * n_i
    src_x = mod(div(cells, depth), full_x) - plane * n_x
    inside = (src_i >= 0) & (src_i < n_i) & (src_x >= 0) & (src_x < n_x)
    src_row = jnp.where(inside, src_i * n_x + src_x, -1)
    n_src = cells.shape[1]
    src_rows = (lax.broadcasted_iota(jnp.int32, (rows, n_src), 0) == src_row).astype(jnp.float32)
    src_cols = (lax.broadcasted_iota(jnp.int32, (depth, n_src), 0) == mod(cells, depth)).astype(jnp.float32).astype(jnp.bfloat16)

    def flat(idx):
        return field[idx, inner_i, inner_x, :].reshape(rows, depth)

    def differences(idx):
        high, low = split_bf16(flat(idx))
        wide[...] = dot(row_mat[...], high) + dot(row_mat[...], low)
        deep[...] = dot(high, z_mat[...]) + dot(low, z_mat[...])

    def operator(idx, i):
        def line(n):
            return pl.ds(pl.multiple_of(n * rows + i * n_x, n_x), n_x)

        center = field[idx, i + 4, inner_x, :]
        return center, (
            3.0 * SECOND_COEFFS[0] * center
            + SECOND_COEFFS[1] * (wide[line(0), :] + deep[line(0), pl.ds(0, depth)])
            - slopes[0, i] * wide[line(1), :] - slopes[1, i] * wide[line(2), :]
            - slopes[2, i] * deep[line(0), pl.ds(depth, depth)]
        )

    def across(idx, i):
        lap = slope_i = slope_x = None
        for k in range(1, 5):
            plus_i = field[idx, i + 4 + k, inner_x, :]
            minus_i = field[idx, i + 4 - k, inner_x, :]
            plus_x = field[idx, i + 4, pl.ds(8 + k, n_x), :]
            minus_x = field[idx, i + 4, pl.ds(8 - k, n_x), :]
            terms = (
                SECOND_COEFFS[k] * ((plus_i + minus_i) + (plus_x + minus_x)),
                FIRST_COEFFS[k - 1] * (plus_i - minus_i),
                FIRST_COEFFS[k - 1] * (plus_x - minus_x),
            )
            if lap is None:
                lap, slope_i, slope_x = terms
            else:
                lap, slope_i, slope_x = lap + terms[0], slope_i + terms[1], slope_x + terms[2]
        return lap, slope_i, slope_x

    for n in shares:
        half_arrival(n).wait_recv()
        pass_on(n).start()
    tile_finish(RHO)
    send_all(DENSITY)
    tile_finish(NOW)
    send_all(0)

    high, low = split_bf16(flat(DENSITY))
    deep[...] = dot(high, z_mat[...]) + dot(low, z_mat[...])
    slopes[2] = ((FIRST_COEFFS[0] * FIRST_COEFFS[0]) * deep[:, pl.ds(depth, depth)]).reshape(n_i, n_x, depth)
    differences(0)

    def inject_sources(t):
        high, low = split_bf16(src_rows * wavelet[pl.ds(t, 1), :])
        return dot_nt(high, src_cols) + dot_nt(low, src_cols)

    accel[0] = inject_sources(0).reshape(n_i, n_x, depth)

    for from_y in range(2):
        @pl.when(arrives(from_y))
        def _():
            list_arrival(from_y).wait_recv()
    for a in range(2):
        @pl.when(leaves(a))
        def _():
            list_copy(a).wait_send()
    for from_y in range(2):
        spot = list_in[from_y][:1]
        cell_i = div(spot, tile_x * depth) - cp * n_i
        cell_x = mod(div(spot, depth), tile_x) + from_y * tile_x
        row = jnp.where((spot >= 0) & (cell_i >= 0) & (cell_i < n_i), cell_i * n_x + cell_x, -1)
        columns = pl.ds(from_y * slots, slots)
        row_map[:, columns] = (lax.broadcasted_iota(jnp.int32, (rows, slots), 0) == row).astype(jnp.float32)
        zmap_t[:, columns] = (
            lax.broadcasted_iota(jnp.int32, (depth, slots), 0) == mod(spot, depth)
        ).astype(jnp.float32).astype(jnp.bfloat16)

    for part, d, c in pieces:
        finish(DENSITY, part, d, c)
    sent(DENSITY)
    for d in range(layers):
        lanes = pl.ds(d * 128, 128)
        for side in range(2):
            for c in range(2):
                field[DENSITY, pl.ds(side * (n_i + 4), 4), pl.ds(8 + c * half_x, half_x), lanes] = i_in[DENSITY, side, d, c]
            field[DENSITY, inner_i, pl.ds(4 + side * (n_x + 4), 4), lanes] = x_in[DENSITY, side, d]

    @pl.loop(0, n_i)
    def _(i):
        _, slope_i, slope_x = across(DENSITY, i)
        slopes[0, i] = FIRST_COEFFS[0] * slope_i
        slopes[1, i] = FIRST_COEFFS[0] * slope_x

    tile_finish(SPEED)
    column = lax.broadcasted_iota(jnp.int32, (n_x, depth), 0)

    @pl.loop(0, n_i)
    def _(i):
        square = vel[i] * vel[i]
        speed_sq[i] = square
        accel[0, i] += square * operator(0, i)[1]
        for k in range(1, 5):
            weight = jnp.where(
                column < k, SECOND_COEFFS[k] + (FIRST_COEFFS[k - 1] / FIRST_COEFFS[0]) * slopes[1, i],
                jnp.where(
                    column >= n_x - k, SECOND_COEFFS[k] - (FIRST_COEFFS[k - 1] / FIRST_COEFFS[0]) * slopes[1, i], 0.0
                ),
            )
            wx[k - 1, i] = square * weight

    tile_finish(BEFORE)

    @pl.loop(0, n_i)
    def _(i):
        field[1, i + 4, inner_x, :] = (
            2.0 * field[0, i + 4, inner_x, :] - field[1, i + 4, inner_x, :] + accel[0, i]
        )

    def start_traces(third):
        @pl.loop(1 + (n_group - 1) * third // 3, 1 + (n_group - 1) * (third + 1) // 3)
        def _(r):
            obs_copy(lax.rem(me + r, n_group), me).start()

    def make_traces(from_y):
        @pl.loop(1, n_group)
        def _(r):
            peer = lax.rem(me + r, n_group)
            if from_y == 0:
                obs_copy(peer, peer).wait_recv()
            else:
                obs_copy(peer, me).wait_send()

        lane = div(lax.broadcasted_iota(jnp.int32, (8, slots), 1), CAP)
        owner = (2 * plane + from_y) * 2 + origin

        def place_one(s, total):
            moved = pltpu.roll(obs_in[s], lax.rem(s - owner + n_group, n_group) * CAP, axis=1)
            return jnp.where(lane == s, moved, total)

        traces[:, pl.ds(from_y * slots, slots)] = lax.fori_loop(
            0, n_group, place_one, jnp.zeros((8, slots), jnp.float32)
        )

    def prepare(idx, term):
        base[...] = term.reshape(n_i, n_x, depth)
        differences(idx)

    def interior(now, other, i):
        center, value = operator(now, i)
        change = base[i] + speed_sq[i] * value
        field[other, i + 4, inner_x, :] = 2.0 * center - field[other, i + 4, inner_x, :] + change
        return center, change

    def correct(now, other, part, d, c, t):
        up = part == 0
        sign = jnp.where(up, 1.0, -1.0)
        columns, lanes = pl.ds(c * half_x, half_x), pl.ds(d * 128, 128)
        for r in range(middle):
            i = jnp.where(up, r, n_i - 1 - r)
            halo = x_in[now, c, d, i]
            pair = jnp.concatenate([halo] * (half_x // 4), axis=0)
            change = wx[3, i, columns, lanes] * pair
            for k in range(1, 4):
                change += wx[k - 1, i, columns, lanes] * pltpu.roll(pair, half_x - k if c else k, axis=0)
            lap = None
            for h in range(4 - r):
                k = r + 1 + h
                halo = i_in[now, part, d, c, jnp.where(up, 3 - h, h)]
                terms = SECOND_COEFFS[k] * halo, (FIRST_COEFFS[k - 1] / FIRST_COEFFS[0]) * halo
                lap, slope = terms if lap is None else (lap + terms[0], slope + terms[1])
            if lap is not None:
                change += speed_sq[i, columns, lanes] * (lap + (sign * slopes[0, i, columns, lanes]) * slope)
            spot = (other, i + 4, pl.ds(8 + c * half_x, half_x), lanes)
            fresh = field[spot] + change
            field[spot] = fresh
            x_out[other, c, d, i] = fresh[half_x - 4:] if c else fresh[:4]
            if r < 4:
                i_out[other, part, d, c, jnp.where(up, r, 3 - r)] = fresh
            if t is not None:
                accel[t, i, columns, lanes] += change

    def sample(idx, t):
        high, low = split_bf16(flat(idx))
        picked = dot(high, zmap_t[...]) + dot(low, zmap_t[...])
        predicted = jnp.sum(picked * row_map[...], axis=0, keepdims=True)
        residual_ref[t] = predicted

    def task_first():
        quarter_start(ADJ_NOW, 0)

    def task_second():
        quarter_start(ADJ_NOW, 1)

    def task_third():
        quarter_start(ADJ_BEFORE, 0)

    def task_fourth():
        quarter_start(ADJ_BEFORE, 1)
        start_traces(0)
        start_traces(1)

    def task_halos():
        start_traces(2)
        tile_finish(ADJ_NOW)
        send_all(2)

    def task_adjoint():
        tile_finish(ADJ_BEFORE)
        differences(2)
        vel[...] = (2.0 / steps) / vel[...]

        @pl.loop(0, n_i, unroll=2)
        def _(i):
            center, value = operator(2, i)
            field[3, i + 4, inner_x, :] = (
                2.0 * center - field[3, i + 4, inner_x, :] + speed_sq[i] * value
            )

    tasks = [task_first, task_second, task_third, task_fourth, task_halos, functools.partial(make_traces, 0), functools.partial(make_traces, 1), task_adjoint]
    times = [n * steps // 8 for n in (0, 1, 2, 3, 4, 6, 7, 5)]

    @pl.loop(0, steps)
    def _(t):
        now = lax.rem(t, 2)
        other = 1 - now

        @pl.when(t > 0)
        def _():
            prepare(now, inject_sources(t))

            @pl.loop(0, n_i, unroll=2)
            def _(i):
                _, change = interior(now, other, i)
                accel[t, i] = change

        for at, task in zip(times, tasks):
            pl.when(t == at)(task)

        @pl.when(t >= 1)
        def _():
            sample(now, t - 1)
            sent(other)

        for part, d, c in pieces:
            finish(now, part, d, c)
            correct(now, other, part, d, c, t)

            @pl.when(t < steps - 1)
            def _():
                send(other, part, d, c)

    sent((steps - 1) % 2)
    sample(steps % 2, steps - 1)

    @pl.loop(0, steps)
    def _(j):
        now = 2 + lax.rem(j, 2)
        other = 5 - now
        t = steps - 1 - j
        high, low = split_bf16(row_map[...] * (residual_ref[t] - traces[pl.ds(t, 1), :]))
        injected = dot_nt(high, zmap_t[...]) + dot_nt(low, zmap_t[...])

        @pl.when(j == 0)
        def _():
            field[3, inner_i, inner_x, :] += injected.reshape(n_i, n_x, depth)

        @pl.when(j > 0)
        def _():
            prepare(now, injected)

            @pl.loop(0, n_i, unroll=2)
            def _(i):
                center, _ = interior(now, other, i)
                image[i] += center * accel[t + 1, i]

            sent(other)

        @pl.when(j == steps - 1)
        def _():
            home_start(0)

        for part, d, c in pieces:
            finish(now, part, d, c)
            correct(now, other, part, d, c, None)

            @pl.when(j < steps - 1)
            def _():
                send(other, part, d, c)

    sent(2 + (steps - 1) % 2)

    @pl.loop(0, n_i, unroll=4)
    def _(i):
        image[i] = (image[i] + field[final_idx[1], i + 4, inner_x, :] * accel[0, i]) * vel[i]

    if fused:
        fused_gradient()
    else:
        grad_out[...] = image[...]
        home_start(1)
    home_finish(0)
    home_finish(1)


def finish_kernel(shape, slabs, last, previous):
    dz, tile_i, full_x = shape
    _, n_groups, _, lanes = slabs.shape
    group = lanes // dz

    def kernel(
        slabs_in, last_in, previous_in, gradient, last_out, previous_out,
        slabs_held, last_held, previous_held, lines_held, in_sem, out_sem,
    ):
        loads = [
            pltpu.make_async_copy(slabs_in, slabs_held, in_sem.at[0]),
            pltpu.make_async_copy(last_in, last_held, in_sem.at[1]),
            pltpu.make_async_copy(previous_in, previous_held, in_sem.at[2]),
        ]
        for load in loads:
            load.start()
        far = (
            lax.broadcasted_iota(jnp.int32, (full_x, full_x), 0) - lax.broadcasted_iota(jnp.int32, (full_x, full_x), 1)
        ).astype(jnp.float32)
        weights = jnp.exp(-jnp.abs(far) / SMOOTH)
        weights = weights / jnp.sum(weights, axis=0, keepdims=True)
        stores = [
            pltpu.make_async_copy(last_held, last_out, out_sem.at[0]),
            pltpu.make_async_copy(previous_held, previous_out, out_sem.at[1]),
        ]
        for load, store in zip(loads[1:], stores):
            load.wait()
            store.start()
        loads[0].wait()
        for a in range(2):
            for ig in range(n_groups):
                lines = dot_tn_exact(slabs_held[a, ig], weights)
                for j in range(group):
                    lines_held[:, (a * n_groups + ig) * group + j, :] = lines[j * dz:(j + 1) * dz]
            span = pl.ds(a * (tile_i // 2), tile_i // 2)
            store = pltpu.make_async_copy(lines_held.at[:, span, :], gradient.at[:, span, :], out_sem.at[2 + a])
            store.start()
            stores.append(store)
        for store in stores:
            store.wait()

    anywhere = pl.BlockSpec(memory_space=pl.ANY)
    return pl.pallas_call(
        kernel,
        out_shape=[jax.ShapeDtypeStruct(dims, jnp.float32) for dims in (shape, last.shape, previous.shape)],
        in_specs=[anywhere] * 3,
        out_specs=[anywhere] * 3,
        scratch_shapes=[
            *[pltpu.VMEM(dims, jnp.float32) for dims in (slabs.shape, last.shape, previous.shape, shape)],
            pltpu.SemaphoreType.DMA((3,)),
            pltpu.SemaphoreType.DMA((4,)),
        ],
        compiler_params=pltpu.CompilerParams(vmem_limit_bytes=56 * 1024 * 1024),
    )(slabs, last, previous)


def per_device(
    fwd_now, fwd_before, adj_now, adj_before, velocity, log_density,
    observed, rec_cells, rec_counts, src_cell, wavelet,
):
    tile_i, tile_x, depth = fwd_now.shape
    steps = wavelet.shape[0]
    n_xline = lax.axis_size("xline")
    full_x = tile_x * n_xline
    n_i, n_x = tile_i // 2, tile_x * 2
    rows = n_i * n_x
    slots = rec_cells.shape[1]
    n_group = 2 * n_xline
    dz = depth // n_xline
    fused = dz >= 8 and 128 % dz == 0 and depth % 128 == 0 and n_i % (128 // dz) == 0
    group = 128 // dz if fused else 1
    layers = depth // 128

    block = (n_i, n_x, depth)
    vmem = pl.BlockSpec(memory_space=pltpu.VMEM)
    anywhere = pl.BlockSpec(memory_space=pl.ANY)
    dma = pltpu.SemaphoreType.DMA
    kernel = functools.partial(wave_kernel, (tile_i, tile_x, n_i, n_x, depth, steps, n_xline, fused))
    grad_shape = (2, n_i // group, full_x, 128) if fused else block
    slab_shape = (n_xline, n_i // group, n_x, 128) if fused else (8, 128)
    small_shapes = [observed, rec_cells, rec_counts, src_cell[None, :], wavelet]
    raw, last, previous = pl.pallas_call(
        kernel,
        out_shape=[
            jax.ShapeDtypeStruct(grad_shape, jnp.float32),
            jax.ShapeDtypeStruct(fwd_now.shape, jnp.float32),
            jax.ShapeDtypeStruct(fwd_now.shape, jnp.float32),
        ],
        in_specs=[anywhere] * 11,
        out_specs=[anywhere if fused else vmem, anywhere, anywhere],
        scratch_shapes=[
            pltpu.VMEM((5, n_i + 8, n_x + 16, depth), jnp.float32),
            pltpu.VMEM(block, jnp.float32),
            pltpu.VMEM((5, 2, layers, n_i, 4, 128), jnp.float32),
            pltpu.VMEM((5, 2, layers, n_i, 4, 128), jnp.float32),
            pltpu.VMEM((5, 2, layers, 2, 4, tile_x, 128), jnp.float32),
            pltpu.VMEM((5, 2, layers, 2, 4, tile_x, 128), jnp.float32),
            pltpu.VMEM((steps,) + block, jnp.float32),
            pltpu.VMEM(block, jnp.float32),
            pltpu.VMEM(block, jnp.float32),
            pltpu.VMEM((3,) + block, jnp.float32),
            pltpu.VMEM(block, jnp.float32),
            pltpu.VMEM((4,) + block, jnp.float32),
            pltpu.VMEM((rows, 2 * slots), jnp.float32),
            pltpu.VMEM((depth, 2 * slots), jnp.bfloat16),
            pltpu.VMEM((depth, 2 * depth), jnp.bfloat16),
            pltpu.VMEM((steps, 1, 2 * slots), jnp.float32),
            pltpu.VMEM((steps, 2 * slots), jnp.float32),
            pltpu.VMEM((8, slots), jnp.int32),
            pltpu.VMEM((2, 8, slots), jnp.int32),
            pltpu.VMEM((n_group,) + observed.shape, jnp.float32),
            pltpu.VMEM(slab_shape, jnp.float32),
            *[pltpu.VMEM(value.shape, value.dtype) for value in small_shapes],
            pltpu.VMEM((3 * rows, rows), jnp.bfloat16),
            pltpu.VMEM((3 * rows, depth), jnp.float32),
            pltpu.VMEM((rows, 2 * depth), jnp.float32),
            dma((5, 2)), dma((5, 2, 2, layers)), dma((5, 2)), dma((5, 2, 2, layers)),
            dma((6, 2)), dma((6, 2)), dma((6,)),
            dma((2,)), dma((2,)),
            dma((n_group,)), dma((n_group,)),
            dma((2, 2)), dma((2, 2)), dma((2,)),
            dma((n_xline,)), dma((2, n_xline // 2)), dma((1,)), dma((5,)),
            dma((6,)), dma((6,)),
        ],
        compiler_params=pltpu.CompilerParams(
            collective_id=0, has_side_effects=True, vmem_limit_bytes=56 * 1024 * 1024
        ),
    )(
        log_density, fwd_now, velocity, fwd_before, adj_now, adj_before,
        *small_shapes,
    )
    if fused:
        return finish_kernel((dz, tile_i, full_x), raw, last, previous)

    places = []
    for xl in range(n_xline):
        for core in range(2):
            y, plane = xl % 2, xl // 2
            cp = (core + plane % 2) % 2
            places.append((xl * 2 + core, (2 * plane + cp) * 2 + y))
    raw = lax.ppermute(raw, ("xline", "inline"), places)
    columns = lax.all_to_all(
        raw.reshape(n_i, n_x, n_xline, dz).transpose(2, 0, 1, 3),
        "xline", split_axis=0, concat_axis=0, tiled=True,
    ).reshape(n_xline // 2, 2, n_i, n_x, dz)
    positions = jnp.arange(full_x).astype(jnp.float32)
    weights = jnp.exp(-jnp.abs(positions[:, None] - positions[None, :]) / SMOOTH)
    weights = weights / jnp.sum(weights, axis=1, keepdims=True)
    gradient = jnp.einsum(
        "phixz,ypx->zhiy", columns, weights.reshape(full_x, n_xline // 2, n_x),
        precision=lax.Precision.HIGHEST,
    ).reshape(dz, tile_i, full_x)
    return gradient, last, previous


def solution(mesh):
    return jax.shard_map(
        per_device,
        mesh=mesh,
        in_specs=(
            P(("shots", "inline"), "xline", None),
            P(("shots", "inline"), "xline", None),
            P(("shots", "inline"), "xline", None),
            P(("shots", "inline"), "xline", None),
            P("inline", "xline", None),
            P("inline", "xline", None),
            P("shots", ("xline", "inline")),
            P(("xline", "inline"), None),
            P(("xline", "inline"), None),
            P("shots"),
            P("shots", None),
        ),
        out_specs=(
            P(("shots", "xline"), "inline", None),
            P(("shots", "inline"), "xline", None),
            P(("shots", "inline"), "xline", None),
        ),
        check_vma=False,
    )
```

```python
import functools

import jax
import jax.numpy as jnp
from jax import lax
from jax.experimental import pallas as pl
from jax.experimental.pallas import tpu as pltpu
from jax.sharding import PartitionSpec as P

CAP = 8
SMOOTH = 16
MESH = pl.DeviceIdType.MESH

SECOND_COEFFS = (-205.0 / 72.0, 8.0 / 5.0, -1.0 / 5.0, 8.0 / 315.0, -1.0 / 560.0)
FIRST_COEFFS = (4.0 / 5.0, -1.0 / 5.0, 4.0 / 105.0, -1.0 / 280.0)
LEFT, RIGHT, UP, DOWN = 0, 1, 2, 3
DENSITY = 4
RHO, NOW, SPEED, BEFORE, ADJ_NOW, ADJ_BEFORE = range(6)


def split_bf16(value):
    high = value.astype(jnp.bfloat16)
    low = (value - high.astype(jnp.float32)).astype(jnp.bfloat16)
    return high, low


def dot(a, b):
    return jnp.dot(a, b, preferred_element_type=jnp.float32)


def dot_nt(a, b):
    return lax.dot_general(a, b, (((1,), (1,)), ((), ())), preferred_element_type=jnp.float32)


def dot_tn_exact(a, b):
    dims = (((0,), (0,)), ((), ()))
    ah, al = split_bf16(a)
    bh, bl = split_bf16(b)
    one = lax.dot_general(ah, bh, dims, preferred_element_type=jnp.float32)
    two = lax.dot_general(al, bh, dims, preferred_element_type=jnp.float32)
    three = lax.dot_general(ah, bl, dims, preferred_element_type=jnp.float32)
    return one + (two + three)


def div(value, n):
    return lax.shift_right_arithmetic(value, jnp.full_like(value, n.bit_length() - 1))


def mod(value, n):
    return value & (n - 1)


def wave_kernel(
    sizes,
    log_density, fwd_now, velocity, fwd_before, adj_now, adj_before,
    given_observed, given_cells, given_counts, given_src, given_wavelet,
    grad_out, last_out, previous_out,
    field, vel, x_in, x_out, i_in, i_out, accel, base, image, slopes, speed_sq, wx,
    row_map, zmap_t, zmap, z_mat, residual_ref, traces, list_out, list_in, obs_in, g_send,
    held_observed, held_cells, held_counts, held_src, held_wavelet, row_mat, wide, deep,
    x_send, x_recv, i_send, i_recv, rt_send, rt_recv, rt_local, list_send, list_recv, obs_send, obs_recv,
    ret_send, ret_recv, ret_local, g_ssem, g_rsem, g_local, small_sem, pass_send, pass_recv,
):
    tile_i, tile_x, n_i, n_x, depth, steps, n_xline, fused = sizes
    rows = n_i * n_x
    small_in = (given_observed, given_cells, given_counts, given_src, given_wavelet)
    small_held = (held_observed, held_cells, held_counts, held_src, held_wavelet)
    slots = held_cells.shape[1]
    n_group = 2 * n_xline
    xl = lax.axis_index("xline")
    core = lax.axis_index("inline")
    me = xl * 2 + core
    y = lax.rem(xl, 2)
    plane = xl // 2
    z_odd = lax.rem(plane, 2)
    mate = xl + 1 - 2 * y
    cp = lax.rem(core + z_odd, 2)
    origin = y
    q = 2 * y + cp
    stays = y == core
    has = (xl >= 2, xl < n_xline - 2, q > 0, q < 3)
    other_core = 1 - core
    shot = lax.axis_index("shots")
    shares = (RHO, SPEED) if lax.axis_size("shots") == 2 else ()
    target = (
        {"xline": xl - 2, "inline": other_core},
        {"xline": xl + 2, "inline": other_core},
        {"xline": jnp.where(q == 2, mate, xl), "inline": other_core},
        {"xline": jnp.where(q == 1, mate, xl), "inline": other_core},
    )
    inner_i = pl.ds(4, n_i)
    inner_x = pl.ds(8, n_x)
    middle = n_i // 2

    barrier = pltpu.get_barrier_semaphore()

    def greet(device):
        pl.semaphore_signal(barrier, inc=1, device_id=device, device_id_type=MESH)

    near = n_xline // 2 <= 4
    if near:
        greet({"inline": other_core})
        greet({"xline": mate})
        greet({"xline": mate, "inline": other_core})
        for way in (LEFT, RIGHT):
            @pl.when(has[way])
            def _():
                greet(target[way])
        greeted = 3 + has[LEFT].astype(jnp.int32) + has[RIGHT].astype(jnp.int32)
    else:
        @pl.loop(1, n_group)
        def _(r):
            peer = lax.rem(me + r, n_group)
            greet({"xline": peer // 2, "inline": lax.rem(peer, 2)})
        greeted = n_group - 1
    if shares:
        greet({"shots": 1 - shot})
        greeted = greeted + 1

    small = [
        pltpu.make_async_copy(given, held, small_sem.at[n])
        for n, (given, held) in enumerate(zip(small_in, small_held))
    ]
    for copy in small:
        copy.start()
    observed, rec_cells, rec_counts, src_cell, wavelet = small_held

    layers = depth // 128
    half_x = n_x // 2

    def beside(idx, way, part, d):
        part_rows = pl.ds(part * middle, middle)
        return pltpu.make_async_remote_copy(
            src_ref=x_out.at[idx, way, d, part_rows], dst_ref=x_in.at[idx, 1 - way, d, part_rows],
            send_sem=x_send.at[idx, way], recv_sem=x_recv.at[idx, way, part, d],
            device_id=target[way], device_id_type=MESH,
        )

    def above(idx, part, c, d, arriving):
        up = part == 0
        return pltpu.make_async_remote_copy(
            src_ref=i_out.at[idx, part, d, c],
            dst_ref=i_in.at[idx, part if arriving else 1 - part, d, c],
            send_sem=i_send.at[idx, part],
            recv_sem=i_recv.at[idx, 1 - part if arriving else part, c, d],
            device_id={
                "xline": jnp.where(up, target[UP]["xline"], target[DOWN]["xline"]), "inline": other_core
            },
            device_id_type=MESH,
        )

    def has_row(part):
        return jnp.where(part == 0, q, 3 - q) > 0

    def send(idx, part, d, c):
        @pl.when(has[c])
        def _():
            beside(idx, c, part, d).start()

        @pl.when(has_row(part))
        def _():
            above(idx, part, c, d, False).start()

    def finish(idx, part, d, c):
        @pl.when(has[c])
        def _():
            beside(idx, 1 - c, part, d).wait_recv()

        @pl.when(has_row(part))
        def _():
            above(idx, part, c, d, True).wait_recv()

    def sent(idx):
        for n in range(2):
            @pl.when(has[n])
            def _():
                pltpu.make_async_remote_copy(
                    src_ref=x_out.at[idx, n], dst_ref=x_in.at[idx, 1 - n],
                    send_sem=x_send.at[idx, n], recv_sem=x_recv.at[idx, n, 0, 0],
                    device_id=target[n], device_id_type=MESH,
                ).wait_send()

            @pl.when(has[UP + n])
            def _():
                pltpu.make_async_remote_copy(
                    src_ref=i_out.at[idx, n], dst_ref=i_in.at[idx, 1 - n],
                    send_sem=i_send.at[idx, n], recv_sem=i_recv.at[idx, n, 0, 0],
                    device_id=target[UP + n], device_id_type=MESH,
                ).wait_send()

    def send_all(idx):
        for part, d, c in pieces:
            rows_at = pl.ds(part * middle, middle)
            x_out[idx, c, d, rows_at] = field[
                idx, pl.ds(4 + part * middle, middle), pl.ds(8 + c * (n_x - 4), 4), pl.ds(d * 128, 128)
            ]
            i_out[idx, part, d, c] = field[
                idx, pl.ds(4 + part * (n_i - 4), 4), pl.ds(8 + c * half_x, half_x), pl.ds(d * 128, 128)
            ]
            send(idx, part, d, c)

    halves = (1 - y, y)
    pieces = [(part, d, c) for part in halves for d in range(layers) for c in range(2)]

    sources = (log_density, fwd_now, velocity, fwd_before, adj_now, adj_before)
    places = (DENSITY, 0, None, 1, 2, 3)

    def landing(n, from_y):
        columns = pl.multiple_of(from_y * tile_x, tile_x)
        if n == SPEED:
            return vel.at[:, pl.ds(columns, tile_x), :]
        return field.at[places[n], inner_i, pl.ds(pl.multiple_of(8 + columns, 8), tile_x), :]

    def tile_copy(n, a):
        return pltpu.make_async_remote_copy(
            src_ref=sources[n].at[pl.ds(a * n_i, n_i)], dst_ref=landing(n, y),
            send_sem=rt_send.at[n, a], recv_sem=rt_recv.at[n, y],
            device_id={"xline": 2 * plane + core, "inline": lax.rem(a + z_odd, 2)},
            device_id_type=MESH,
        )

    def tile_arrival(n, from_y):
        return pltpu.make_async_remote_copy(
            src_ref=sources[n].at[pl.ds(0, n_i)], dst_ref=landing(n, from_y),
            send_sem=rt_send.at[n, 0], recv_sem=rt_recv.at[n, from_y],
            device_id={"xline": mate}, device_id_type=MESH,
        )

    def own_copy(n):
        return pltpu.make_async_copy(
            sources[n].at[pl.ds(cp * n_i, n_i)], landing(n, y), rt_local.at[n]
        )

    def leaves(a):
        return jnp.logical_not(jnp.logical_and(stays, cp == a))

    def arrives(from_y):
        return jnp.logical_not(jnp.logical_and(stays, y == from_y))

    def tile_start(n):
        for a in range(2):
            @pl.when(jnp.logical_and(stays, cp != a) if n in shares else leaves(a))
            def _():
                tile_copy(n, a).start()

        if n in shares:
            for a in range(2):
                @pl.when(jnp.logical_not(stays))
                def _():
                    half_copy(n, a).start()

        @pl.when(stays)
        def _():
            own_copy(n).start()

    def tile_finish(n):
        for from_y in range(2):
            @pl.when(jnp.logical_and(arrives(from_y), y == from_y) if n in shares else arrives(from_y))
            def _():
                tile_arrival(n, from_y).wait_recv()
        for a in range(2):
            @pl.when(jnp.logical_and(stays, cp != a) if n in shares else leaves(a))
            def _():
                tile_copy(n, a).wait_send()

        @pl.when(stays)
        def _():
            own_copy(n).wait()

        if n in shares:
            for a in range(2):
                @pl.when(jnp.logical_not(stays))
                def _():
                    half_copy(n, a).wait_send()
            pass_on(n).wait_send()
            passed_on(n).wait_recv()

    def quarter_start(n, which):
        for a in range(2):
            @pl.when(leaves(a))
            def _():
                pltpu.make_async_remote_copy(
                    src_ref=sources[n].at[pl.ds(a * n_i + which * middle, middle)], dst_ref=half_landing(n, y, which),
                    send_sem=rt_send.at[n, a], recv_sem=rt_recv.at[n, y],
                    device_id={"xline": 2 * plane + core, "inline": lax.rem(a + z_odd, 2)},
                    device_id_type=MESH,
                ).start()

        if which == 0:
            @pl.when(stays)
            def _():
                own_copy(n).start()

    def half_landing(n, from_y, which):
        columns = pl.multiple_of(from_y * tile_x, tile_x)
        if n == SPEED:
            return vel.at[pl.ds(which * middle, middle), pl.ds(columns, tile_x), :]
        return field.at[
            places[n], pl.ds(4 + which * middle, middle), pl.ds(pl.multiple_of(8 + columns, 8), tile_x), :
        ]

    def half_copy(n, a):
        return pltpu.make_async_remote_copy(
            src_ref=sources[n].at[pl.ds(a * n_i + shot * middle, middle)], dst_ref=half_landing(n, y, shot),
            send_sem=rt_send.at[n, a], recv_sem=rt_recv.at[n, y],
            device_id={"xline": mate, "inline": lax.rem(a + z_odd, 2)}, device_id_type=MESH,
        )

    def half_arrival(n):
        return pltpu.make_async_remote_copy(
            src_ref=sources[n].at[pl.ds(0, middle)], dst_ref=half_landing(n, 1 - y, shot),
            send_sem=rt_send.at[n, 0], recv_sem=rt_recv.at[n, 1 - y],
            device_id={"xline": mate}, device_id_type=MESH,
        )

    def pass_on(n):
        return pltpu.make_async_remote_copy(
            src_ref=half_landing(n, 1 - y, shot), dst_ref=half_landing(n, 1 - y, shot),
            send_sem=pass_send.at[n], recv_sem=pass_recv.at[n],
            device_id={"shots": 1 - shot}, device_id_type=MESH,
        )

    def passed_on(n):
        return pltpu.make_async_remote_copy(
            src_ref=half_landing(n, 1 - y, shot), dst_ref=half_landing(n, 1 - y, 1 - shot),
            send_sem=pass_send.at[n], recv_sem=pass_recv.at[n],
            device_id={"shots": 1 - shot}, device_id_type=MESH,
        )

    def list_copy(a):
        return pltpu.make_async_remote_copy(
            src_ref=list_out, dst_ref=list_in.at[y],
            send_sem=list_send.at[a], recv_sem=list_recv.at[y],
            device_id={"xline": 2 * plane + core, "inline": lax.rem(a + z_odd, 2)},
            device_id_type=MESH,
        )

    def list_arrival(from_y):
        return pltpu.make_async_remote_copy(
            src_ref=list_out, dst_ref=list_in.at[from_y],
            send_sem=list_send.at[0], recv_sem=list_recv.at[from_y],
            device_id={"xline": mate}, device_id_type=MESH,
        )

    def obs_copy(peer, slot):
        return pltpu.make_async_remote_copy(
            src_ref=observed, dst_ref=obs_in.at[slot],
            send_sem=obs_send.at[peer], recv_sem=obs_recv.at[slot],
            device_id={"xline": peer // 2, "inline": lax.rem(peer, 2)}, device_id_type=MESH,
        )

    finals = (previous_out, last_out)
    final_idx = (2 + (steps - 1) % 2, 2 + steps % 2)

    def home_copy(n, to_y):
        return pltpu.make_async_remote_copy(
            src_ref=field.at[final_idx[n], inner_i, pl.ds(8 + to_y * tile_x, tile_x), :],
            dst_ref=finals[n].at[pl.ds(cp * n_i, n_i)],
            send_sem=ret_send.at[n, to_y], recv_sem=ret_recv.at[n, cp],
            device_id={"xline": 2 * plane + to_y, "inline": origin}, device_id_type=MESH,
        )

    def home_arrival(n, a):
        return pltpu.make_async_remote_copy(
            src_ref=field.at[final_idx[n], inner_i, pl.ds(8, tile_x), :],
            dst_ref=finals[n].at[pl.ds(a * n_i, n_i)],
            send_sem=ret_send.at[n, 0], recv_sem=ret_recv.at[n, a],
            device_id={"xline": mate}, device_id_type=MESH,
        )

    def home_own(n):
        columns = pl.multiple_of(8 + y * tile_x, 8)
        return pltpu.make_async_copy(
            field.at[final_idx[n], inner_i, pl.ds(columns, tile_x), :],
            finals[n].at[pl.ds(cp * n_i, n_i)], ret_local.at[n],
        )

    def home_start(n):
        for to_y in range(2):
            @pl.when(arrives(to_y))
            def _():
                home_copy(n, to_y).start()

        @pl.when(stays)
        def _():
            home_own(n).start()

    def home_finish(n):
        for to_y in range(2):
            @pl.when(arrives(to_y))
            def _():
                home_copy(n, to_y).wait_send()
        for a in range(2):
            @pl.when(leaves(a))
            def _():
                home_arrival(n, a).wait_recv()

        @pl.when(stays)
        def _():
            home_own(n).wait()

    dz = depth // n_xline
    planes_n = n_xline // 2

    def slab_copy(d):
        return pltpu.make_async_remote_copy(
            src_ref=g_send.at[d],
            dst_ref=grad_out.at[cp, :, pl.ds(pl.multiple_of(plane * n_x, 8), n_x), :],
            send_sem=g_ssem.at[d], recv_sem=g_rsem.at[cp, plane],
            device_id={"xline": d, "inline": origin}, device_id_type=MESH,
        )

    def own_slab():
        return pltpu.make_async_copy(
            g_send.at[xl], grad_out.at[cp, :, pl.ds(pl.multiple_of(plane * n_x, 8), n_x), :], g_local.at[0]
        )

    def slab_arrival(a, p):
        return pltpu.make_async_remote_copy(
            src_ref=g_send.at[0],
            dst_ref=grad_out.at[a, :, pl.ds(pl.multiple_of(p * n_x, 8), n_x), :],
            send_sem=g_ssem.at[0], recv_sem=g_rsem.at[a, p],
            device_id={"xline": mate}, device_id_type=MESH,
        )

    def fused_gradient():
        group = 128 // dz
        lane = div(lax.broadcasted_iota(jnp.int32, (n_x, 128), 1), dz)
        for chunk in range(depth // 128):
            for ig in range(n_i // group):
                planes = [image[ig * group + j, :, pl.ds(chunk * 128, 128)] for j in range(group)]
                for dd in range(group):
                    out = None
                    for j in range(group):
                        shift = (j - dd) * dz % 128
                        moved = pltpu.roll(planes[j], shift, axis=1) if shift else planes[j]
                        out = moved if out is None else jnp.where(lane == j, moved, out)
                    g_send[chunk * group + dd, ig] = out

        @pl.loop(1, n_xline + 1)
        def _(r):
            d = lax.rem(xl + r, n_xline)

            @pl.when(jnp.logical_or(d != xl, origin != core))
            def _():
                slab_copy(d).start()

        home_start(1)

        @pl.when(origin == core)
        def _():
            own_slab().start()

        @pl.loop(0, n_xline)
        def _(r):
            a, p = lax.rem(r, 2), r // 2
            mine = jnp.logical_and(origin == core, jnp.logical_and(a == cp, p == plane))

            @pl.when(jnp.logical_not(mine))
            def _():
                slab_arrival(a, p).wait_recv()

        @pl.when(origin == core)
        def _():
            own_slab().wait()

        @pl.loop(1, n_xline + 1)
        def _(r):
            d = lax.rem(xl + r, n_xline)

            @pl.when(jnp.logical_or(d != xl, origin != core))
            def _():
                slab_copy(d).wait_send()

    for way in (LEFT, RIGHT, UP, DOWN):
        @pl.when(jnp.logical_not(has[way]))
        def _():
            halo = x_in if way < UP else i_in
            halo[:, way % 2] = jnp.zeros(halo.shape[:1] + halo.shape[2:], jnp.float32)
    image[...] = jnp.zeros(image.shape, jnp.float32)

    for copy in small:
        copy.wait()
    n_counts = rec_counts.shape[1]
    spread = (
        div(lax.broadcasted_iota(jnp.int32, (n_counts, slots), 1), CAP)
        == lax.broadcasted_iota(jnp.int32, (n_counts, slots), 0)
    ).astype(jnp.float32).astype(jnp.bfloat16)
    counts = jnp.broadcast_to(rec_counts[...].astype(jnp.float32), (8, n_counts)).astype(jnp.bfloat16)
    live = dot(counts, spread)
    place = mod(lax.broadcasted_iota(jnp.int32, (8, slots), 1), CAP).astype(jnp.float32)
    list_out[...] = jnp.where(place < live, jnp.broadcast_to(rec_cells[...], (8, slots)), -1)

    pl.semaphore_wait(barrier, greeted)

    for a in range(2):
        @pl.when(leaves(a))
        def _():
            list_copy(a).start()

    for n in (RHO, SPEED, NOW):
        tile_start(n)
    tile_start(BEFORE)

    obs_in[me] = observed[...]

    @pl.when(stays)
    def _():
        list_in[y] = list_out[...]

    offset = lax.broadcasted_iota(jnp.int32, (depth, depth), 0) - lax.broadcasted_iota(jnp.int32, (depth, depth), 1)
    second = jnp.zeros((depth, depth), jnp.float32)
    first = jnp.zeros((depth, depth), jnp.float32)
    for k in range(1, 5):
        second = jnp.where((offset == k) | (offset == -k), SECOND_COEFFS[k] / SECOND_COEFFS[1], second)
        first = jnp.where(offset == k, FIRST_COEFFS[k - 1] / FIRST_COEFFS[0], first)
        first = jnp.where(offset == -k, -FIRST_COEFFS[k - 1] / FIRST_COEFFS[0], first)
    z_mat[:, pl.ds(0, depth)] = second.astype(jnp.bfloat16)
    z_mat[:, pl.ds(depth, depth)] = first.astype(jnp.bfloat16)

    at = lax.broadcasted_iota(jnp.int32, (rows, rows), 0)
    to = lax.broadcasted_iota(jnp.int32, (rows, rows), 1)
    step_i = div(to, n_x) - div(at, n_x)
    step_x = mod(to, n_x) - mod(at, n_x)
    lateral_lap = jnp.zeros((rows, rows), jnp.float32)
    for n, (along, still) in enumerate(((step_i, step_x), (step_x, step_i))):
        along = jnp.where(still == 0, along, 0)
        first = jnp.zeros((rows, rows), jnp.float32)
        for k in range(1, 5):
            lateral_lap = jnp.where((along == k) | (along == -k), SECOND_COEFFS[k] / SECOND_COEFFS[1], lateral_lap)
            first = jnp.where(along == k, FIRST_COEFFS[k - 1] / FIRST_COEFFS[0], first)
            first = jnp.where(along == -k, -FIRST_COEFFS[k - 1] / FIRST_COEFFS[0], first)
        row_mat[pl.ds((n + 1) * rows, rows), :] = first.astype(jnp.bfloat16)
    row_mat[pl.ds(0, rows), :] = lateral_lap.astype(jnp.bfloat16)

    full_x = tile_x * n_xline
    cells = src_cell[...]
    src_i = div(cells, full_x * depth) - q * n_i
    src_x = mod(div(cells, depth), full_x) - plane * n_x
    inside = (src_i >= 0) & (src_i < n_i) & (src_x >= 0) & (src_x < n_x)
    src_row = jnp.where(inside, src_i * n_x + src_x, -1)
    n_src = cells.shape[1]
    src_rows = (lax.broadcasted_iota(jnp.int32, (rows, n_src), 0) == src_row).astype(jnp.float32)
    src_cols = (lax.broadcasted_iota(jnp.int32, (depth, n_src), 0) == mod(cells, depth)).astype(jnp.float32).astype(jnp.bfloat16)

    def flat(idx):
        return field[idx, inner_i, inner_x, :].reshape(rows, depth)

    def differences(idx):
        high, low = split_bf16(flat(idx))
        wide[...] = dot(row_mat[...], high) + dot(row_mat[...], low)
        deep[...] = dot(high, z_mat[...]) + dot(low, z_mat[...])

    def operator(idx, i):
        def line(n):
            return pl.ds(pl.multiple_of(n * rows + i * n_x, n_x), n_x)

        center = field[idx, i + 4, inner_x, :]
        return center, (
            3.0 * SECOND_COEFFS[0] * center
            + SECOND_COEFFS[1] * (wide[line(0), :] + deep[line(0), pl.ds(0, depth)])
            - slopes[0, i] * wide[line(1), :] - slopes[1, i] * wide[line(2), :]
            - slopes[2, i] * deep[line(0), pl.ds(depth, depth)]
        )

    def across(idx, i):
        lap = slope_i = slope_x = None
        for k in range(1, 5):
            plus_i = field[idx, i + 4 + k, inner_x, :]
            minus_i = field[idx, i + 4 - k, inner_x, :]
            plus_x = field[idx, i + 4, pl.ds(8 + k, n_x), :]
            minus_x = field[idx, i + 4, pl.ds(8 - k, n_x), :]
            terms = (
                SECOND_COEFFS[k] * ((plus_i + minus_i) + (plus_x + minus_x)),
                FIRST_COEFFS[k - 1] * (plus_i - minus_i),
                FIRST_COEFFS[k - 1] * (plus_x - minus_x),
            )
            if lap is None:
                lap, slope_i, slope_x = terms
            else:
                lap, slope_i, slope_x = lap + terms[0], slope_i + terms[1], slope_x + terms[2]
        return lap, slope_i, slope_x

    for n in shares:
        half_arrival(n).wait_recv()
        pass_on(n).start()
    tile_finish(RHO)
    send_all(DENSITY)
    tile_finish(NOW)
    send_all(0)

    high, low = split_bf16(flat(DENSITY))
    deep[...] = dot(high, z_mat[...]) + dot(low, z_mat[...])
    slopes[2] = ((FIRST_COEFFS[0] * FIRST_COEFFS[0]) * deep[:, pl.ds(depth, depth)]).reshape(n_i, n_x, depth)
    differences(0)

    def inject_sources(t):
        high, low = split_bf16(src_rows * wavelet[pl.ds(t, 1), :])
        return dot_nt(high, src_cols) + dot_nt(low, src_cols)

    accel[0] = inject_sources(0).reshape(n_i, n_x, depth)

    for from_y in range(2):
        @pl.when(arrives(from_y))
        def _():
            list_arrival(from_y).wait_recv()
    for a in range(2):
        @pl.when(leaves(a))
        def _():
            list_copy(a).wait_send()
    for from_y in range(2):
        spot = list_in[from_y][:1]
        cell_i = div(spot, tile_x * depth) - cp * n_i
        cell_x = mod(div(spot, depth), tile_x) + from_y * tile_x
        row = jnp.where((spot >= 0) & (cell_i >= 0) & (cell_i < n_i), cell_i * n_x + cell_x, -1)
        columns = pl.ds(from_y * slots, slots)
        row_map[:, columns] = (lax.broadcasted_iota(jnp.int32, (rows, slots), 0) == row).astype(jnp.float32)
        zmap_t[:, columns] = (
            lax.broadcasted_iota(jnp.int32, (depth, slots), 0) == mod(spot, depth)
        ).astype(jnp.float32).astype(jnp.bfloat16)

    zmap[...] = zmap_t[...].astype(jnp.float32).T.astype(jnp.bfloat16)

    for part, d, c in pieces:
        finish(DENSITY, part, d, c)
    sent(DENSITY)
    for d in range(layers):
        lanes = pl.ds(d * 128, 128)
        for side in range(2):
            for c in range(2):
                field[DENSITY, pl.ds(side * (n_i + 4), 4), pl.ds(8 + c * half_x, half_x), lanes] = i_in[DENSITY, side, d, c]
            field[DENSITY, inner_i, pl.ds(4 + side * (n_x + 4), 4), lanes] = x_in[DENSITY, side, d]

    @pl.loop(0, n_i)
    def _(i):
        _, slope_i, slope_x = across(DENSITY, i)
        slopes[0, i] = FIRST_COEFFS[0] * slope_i
        slopes[1, i] = FIRST_COEFFS[0] * slope_x

    tile_finish(SPEED)
    column = lax.broadcasted_iota(jnp.int32, (n_x, depth), 0)

    @pl.loop(0, n_i)
    def _(i):
        square = vel[i] * vel[i]
        speed_sq[i] = square
        accel[0, i] += square * operator(0, i)[1]
        for k in range(1, 5):
            weight = jnp.where(
                column < k, SECOND_COEFFS[k] + (FIRST_COEFFS[k - 1] / FIRST_COEFFS[0]) * slopes[1, i],
                jnp.where(
                    column >= n_x - k, SECOND_COEFFS[k] - (FIRST_COEFFS[k - 1] / FIRST_COEFFS[0]) * slopes[1, i], 0.0
                ),
            )
            wx[k - 1, i] = square * weight

    tile_finish(BEFORE)

    @pl.loop(0, n_i)
    def _(i):
        field[1, i + 4, inner_x, :] = (
            2.0 * field[0, i + 4, inner_x, :] - field[1, i + 4, inner_x, :] + accel[0, i]
        )

    def start_traces(third):
        @pl.loop(1 + (n_group - 1) * third // 3, 1 + (n_group - 1) * (third + 1) // 3)
        def _(r):
            obs_copy(lax.rem(me + r, n_group), me).start()

    def make_traces(from_y):
        @pl.loop(1, n_group)
        def _(r):
            peer = lax.rem(me + r, n_group)
            if from_y == 0:
                obs_copy(peer, peer).wait_recv()
            else:
                obs_copy(peer, me).wait_send()

        lane = div(lax.broadcasted_iota(jnp.int32, (8, slots), 1), CAP)
        owner = (2 * plane + from_y) * 2 + origin

        def place_one(s, total):
            moved = pltpu.roll(obs_in[s], lax.rem(s - owner + n_group, n_group) * CAP, axis=1)
            return jnp.where(lane == s, moved, total)

        traces[:, pl.ds(from_y * slots, slots)] = lax.fori_loop(
            0, n_group, place_one, jnp.zeros((8, slots), jnp.float32)
        )

    def prepare(idx, term):
        base[...] = term.reshape(n_i, n_x, depth)
        differences(idx)

    def interior(now, other, i):
        center, value = operator(now, i)
        change = base[i] + speed_sq[i] * value
        field[other, i + 4, inner_x, :] = 2.0 * center - field[other, i + 4, inner_x, :] + change
        return center, change

    def correct(now, other, part, d, c, t):
        up = part == 0
        sign = jnp.where(up, 1.0, -1.0)
        columns, lanes = pl.ds(c * half_x, half_x), pl.ds(d * 128, 128)
        for r in range(middle):
            i = jnp.where(up, r, n_i - 1 - r)
            halo = x_in[now, c, d, i]
            pair = jnp.concatenate([halo] * (half_x // 4), axis=0)
            change = wx[3, i, columns, lanes] * pair
            for k in range(1, 4):
                change += wx[k - 1, i, columns, lanes] * pltpu.roll(pair, half_x - k if c else k, axis=0)
            lap = None
            for h in range(4 - r):
                k = r + 1 + h
                halo = i_in[now, part, d, c, jnp.where(up, 3 - h, h)]
                terms = SECOND_COEFFS[k] * halo, (FIRST_COEFFS[k - 1] / FIRST_COEFFS[0]) * halo
                lap, slope = terms if lap is None else (lap + terms[0], slope + terms[1])
            if lap is not None:
                change += speed_sq[i, columns, lanes] * (lap + (sign * slopes[0, i, columns, lanes]) * slope)
            spot = (other, i + 4, pl.ds(8 + c * half_x, half_x), lanes)
            fresh = field[spot] + change
            field[spot] = fresh
            x_out[other, c, d, i] = fresh[half_x - 4:] if c else fresh[:4]
            if r < 4:
                i_out[other, part, d, c, jnp.where(up, r, 3 - r)] = fresh
            if t is not None:
                accel[t, i, columns, lanes] += change

    def sample(idx, t):
        high, low = split_bf16(flat(idx))
        picked = dot(high, zmap_t[...]) + dot(low, zmap_t[...])
        predicted = jnp.sum(picked * row_map[...], axis=0, keepdims=True)
        residual_ref[t] = predicted

    def task_first():
        quarter_start(ADJ_NOW, 0)

    def task_second():
        quarter_start(ADJ_NOW, 1)

    def task_third():
        quarter_start(ADJ_BEFORE, 0)

    def task_fourth():
        quarter_start(ADJ_BEFORE, 1)
        start_traces(0)
        start_traces(1)
        start_traces(2)

    def task_halos():
        tile_finish(ADJ_NOW)
        send_all(2)

    def task_adjoint():
        tile_finish(ADJ_BEFORE)
        differences(2)
        vel[...] = (2.0 / steps) / vel[...]

        @pl.loop(0, n_i, unroll=2)
        def _(i):
            center, value = operator(2, i)
            field[3, i + 4, inner_x, :] = (
                2.0 * center - field[3, i + 4, inner_x, :] + speed_sq[i] * value
            )

    tasks = [task_first, task_second, task_third, task_fourth, task_halos, functools.partial(make_traces, 0), functools.partial(make_traces, 1), task_adjoint]
    times = [n * steps // 8 for n in (0, 1, 2, 3, 4, 6, 7, 5)]

    @pl.loop(0, steps)
    def _(t):
        now = lax.rem(t, 2)
        other = 1 - now

        @pl.when(t > 0)
        def _():
            prepare(now, inject_sources(t))

            @pl.loop(0, n_i, unroll=8)
            def _(i):
                _, change = interior(now, other, i)
                accel[t, i] = change

        for at, task in zip(times, tasks):
            pl.when(t == at)(task)

        @pl.when(t >= 1)
        def _():
            sample(now, t - 1)
            sent(other)

        for part, d, c in pieces:
            finish(now, part, d, c)
            correct(now, other, part, d, c, t)

            @pl.when(t < steps - 1)
            def _():
                send(other, part, d, c)

    sent((steps - 1) % 2)
    sample(steps % 2, steps - 1)

    @pl.loop(0, steps)
    def _(j):
        now = 2 + lax.rem(j, 2)
        other = 5 - now
        t = steps - 1 - j
        high, low = split_bf16(row_map[...] * (residual_ref[t] - traces[pl.ds(t, 1), :]))
        injected = dot(high, zmap[...]) + dot(low, zmap[...])

        @pl.when(j == 0)
        def _():
            field[3, inner_i, inner_x, :] += injected.reshape(n_i, n_x, depth)

        @pl.when(j > 0)
        def _():
            prepare(now, injected)

            @pl.loop(0, n_i, unroll=8)
            def _(i):
                center, _ = interior(now, other, i)
                image[i] += center * accel[t + 1, i]

            sent(other)

        @pl.when(j == steps - 1)
        def _():
            home_start(0)

        for part, d, c in pieces:
            finish(now, part, d, c)
            correct(now, other, part, d, c, None)

            @pl.when(j < steps - 1)
            def _():
                send(other, part, d, c)

    sent(2 + (steps - 1) % 2)

    @pl.loop(0, n_i, unroll=4)
    def _(i):
        image[i] = (image[i] + field[final_idx[1], i + 4, inner_x, :] * accel[0, i]) * vel[i]

    if fused:
        fused_gradient()
    else:
        grad_out[...] = image[...]
        home_start(1)
    home_finish(0)
    home_finish(1)


def finish_kernel(shape, slabs, last, previous):
    dz, tile_i, full_x = shape
    _, n_groups, _, lanes = slabs.shape
    group = lanes // dz

    def kernel(
        slabs_in, last_in, previous_in, gradient, last_out, previous_out,
        slabs_held, last_held, previous_held, lines_held, in_sem, out_sem,
    ):
        loads = [
            pltpu.make_async_copy(slabs_in, slabs_held, in_sem.at[0]),
            pltpu.make_async_copy(last_in, last_held, in_sem.at[1]),
            pltpu.make_async_copy(previous_in, previous_held, in_sem.at[2]),
        ]
        for load in loads:
            load.start()
        far = (
            lax.broadcasted_iota(jnp.int32, (full_x, full_x), 0) - lax.broadcasted_iota(jnp.int32, (full_x, full_x), 1)
        ).astype(jnp.float32)
        weights = jnp.exp(-jnp.abs(far) / SMOOTH)
        weights = weights / jnp.sum(weights, axis=0, keepdims=True)
        stores = [
            pltpu.make_async_copy(last_held, last_out, out_sem.at[0]),
            pltpu.make_async_copy(previous_held, previous_out, out_sem.at[1]),
        ]
        for load, store in zip(loads[1:], stores):
            load.wait()
            store.start()
        loads[0].wait()
        for a in range(2):
            for ig in range(n_groups):
                lines = dot_tn_exact(slabs_held[a, ig], weights)
                for j in range(group):
                    lines_held[:, (a * n_groups + ig) * group + j, :] = lines[j * dz:(j + 1) * dz]
            span = pl.ds(a * (tile_i // 2), tile_i // 2)
            store = pltpu.make_async_copy(lines_held.at[:, span, :], gradient.at[:, span, :], out_sem.at[2 + a])
            store.start()
            stores.append(store)
        for store in stores:
            store.wait()

    anywhere = pl.BlockSpec(memory_space=pl.ANY)
    return pl.pallas_call(
        kernel,
        out_shape=[jax.ShapeDtypeStruct(dims, jnp.float32) for dims in (shape, last.shape, previous.shape)],
        in_specs=[anywhere] * 3,
        out_specs=[anywhere] * 3,
        scratch_shapes=[
            *[pltpu.VMEM(dims, jnp.float32) for dims in (slabs.shape, last.shape, previous.shape, shape)],
            pltpu.SemaphoreType.DMA((3,)),
            pltpu.SemaphoreType.DMA((4,)),
        ],
        compiler_params=pltpu.CompilerParams(vmem_limit_bytes=56 * 1024 * 1024),
    )(slabs, last, previous)


def per_device(
    fwd_now, fwd_before, adj_now, adj_before, velocity, log_density,
    observed, rec_cells, rec_counts, src_cell, wavelet,
):
    tile_i, tile_x, depth = fwd_now.shape
    steps = wavelet.shape[0]
    n_xline = lax.axis_size("xline")
    full_x = tile_x * n_xline
    n_i, n_x = tile_i // 2, tile_x * 2
    rows = n_i * n_x
    slots = rec_cells.shape[1]
    n_group = 2 * n_xline
    dz = depth // n_xline
    fused = dz >= 8 and 128 % dz == 0 and depth % 128 == 0 and n_i % (128 // dz) == 0
    group = 128 // dz if fused else 1
    layers = depth // 128

    block = (n_i, n_x, depth)
    vmem = pl.BlockSpec(memory_space=pltpu.VMEM)
    anywhere = pl.BlockSpec(memory_space=pl.ANY)
    dma = pltpu.SemaphoreType.DMA
    kernel = functools.partial(wave_kernel, (tile_i, tile_x, n_i, n_x, depth, steps, n_xline, fused))
    grad_shape = (2, n_i // group, full_x, 128) if fused else block
    slab_shape = (n_xline, n_i // group, n_x, 128) if fused else (8, 128)
    small_shapes = [observed, rec_cells, rec_counts, src_cell[None, :], wavelet]
    raw, last, previous = pl.pallas_call(
        kernel,
        out_shape=[
            jax.ShapeDtypeStruct(grad_shape, jnp.float32),
            jax.ShapeDtypeStruct(fwd_now.shape, jnp.float32),
            jax.ShapeDtypeStruct(fwd_now.shape, jnp.float32),
        ],
        in_specs=[anywhere] * 11,
        out_specs=[anywhere if fused else vmem, anywhere, anywhere],
        scratch_shapes=[
            pltpu.VMEM((5, n_i + 8, n_x + 16, depth), jnp.float32),
            pltpu.VMEM(block, jnp.float32),
            pltpu.VMEM((5, 2, layers, n_i, 4, 128), jnp.float32),
            pltpu.VMEM((5, 2, layers, n_i, 4, 128), jnp.float32),
            pltpu.VMEM((5, 2, layers, 2, 4, tile_x, 128), jnp.float32),
            pltpu.VMEM((5, 2, layers, 2, 4, tile_x, 128), jnp.float32),
            pltpu.VMEM((steps,) + block, jnp.float32),
            pltpu.VMEM(block, jnp.float32),
            pltpu.VMEM(block, jnp.float32),
            pltpu.VMEM((3,) + block, jnp.float32),
            pltpu.VMEM(block, jnp.float32),
            pltpu.VMEM((4,) + block, jnp.float32),
            pltpu.VMEM((rows, 2 * slots), jnp.float32),
            pltpu.VMEM((depth, 2 * slots), jnp.bfloat16),
            pltpu.VMEM((2 * slots, depth), jnp.bfloat16),
            pltpu.VMEM((depth, 2 * depth), jnp.bfloat16),
            pltpu.VMEM((steps, 1, 2 * slots), jnp.float32),
            pltpu.VMEM((steps, 2 * slots), jnp.float32),
            pltpu.VMEM((8, slots), jnp.int32),
            pltpu.VMEM((2, 8, slots), jnp.int32),
            pltpu.VMEM((n_group,) + observed.shape, jnp.float32),
            pltpu.VMEM(slab_shape, jnp.float32),
            *[pltpu.VMEM(value.shape, value.dtype) for value in small_shapes],
            pltpu.VMEM((3 * rows, rows), jnp.bfloat16),
            pltpu.VMEM((3 * rows, depth), jnp.float32),
            pltpu.VMEM((rows, 2 * depth), jnp.float32),
            dma((5, 2)), dma((5, 2, 2, layers)), dma((5, 2)), dma((5, 2, 2, layers)),
            dma((6, 2)), dma((6, 2)), dma((6,)),
            dma((2,)), dma((2,)),
            dma((n_group,)), dma((n_group,)),
            dma((2, 2)), dma((2, 2)), dma((2,)),
            dma((n_xline,)), dma((2, n_xline // 2)), dma((1,)), dma((5,)),
            dma((6,)), dma((6,)),
        ],
        compiler_params=pltpu.CompilerParams(
            collective_id=0, has_side_effects=True, vmem_limit_bytes=56 * 1024 * 1024
        ),
    )(
        log_density, fwd_now, velocity, fwd_before, adj_now, adj_before,
        *small_shapes,
    )
    if fused:
        return finish_kernel((dz, tile_i, full_x), raw, last, previous)

    places = []
    for xl in range(n_xline):
        for core in range(2):
            y, plane = xl % 2, xl // 2
            cp = (core + plane % 2) % 2
            places.append((xl * 2 + core, (2 * plane + cp) * 2 + y))
    raw = lax.ppermute(raw, ("xline", "inline"), places)
    columns = lax.all_to_all(
        raw.reshape(n_i, n_x, n_xline, dz).transpose(2, 0, 1, 3),
        "xline", split_axis=0, concat_axis=0, tiled=True,
    ).reshape(n_xline // 2, 2, n_i, n_x, dz)
    positions = jnp.arange(full_x).astype(jnp.float32)
    weights = jnp.exp(-jnp.abs(positions[:, None] - positions[None, :]) / SMOOTH)
    weights = weights / jnp.sum(weights, axis=1, keepdims=True)
    gradient = jnp.einsum(
        "phixz,ypx->zhiy", columns, weights.reshape(full_x, n_xline // 2, n_x),
        precision=lax.Precision.HIGHEST,
    ).reshape(dz, tile_i, full_x)
    return gradient, last, previous


def solution(mesh):
    return jax.shard_map(
        per_device,
        mesh=mesh,
        in_specs=(
            P(("shots", "inline"), "xline", None),
            P(("shots", "inline"), "xline", None),
            P(("shots", "inline"), "xline", None),
            P(("shots", "inline"), "xline", None),
            P("inline", "xline", None),
            P("inline", "xline", None),
            P("shots", ("xline", "inline")),
            P(("xline", "inline"), None),
            P(("xline", "inline"), None),
            P("shots"),
            P("shots", None),
        ),
        out_specs=(
            P(("shots", "xline"), "inline", None),
            P(("shots", "inline"), "xline", None),
            P(("shots", "inline"), "xline", None),
        ),
        check_vma=False,
    )
```

```python
import functools

import jax
import jax.numpy as jnp
from jax import lax
from jax.experimental import pallas as pl
from jax.experimental.pallas import tpu as pltpu
from jax.sharding import PartitionSpec as P

CAP = 8
SMOOTH = 16
MESH = pl.DeviceIdType.MESH

SECOND_COEFFS = (-205.0 / 72.0, 8.0 / 5.0, -1.0 / 5.0, 8.0 / 315.0, -1.0 / 560.0)
FIRST_COEFFS = (4.0 / 5.0, -1.0 / 5.0, 4.0 / 105.0, -1.0 / 280.0)
LEFT, RIGHT, UP, DOWN = 0, 1, 2, 3
DENSITY = 4
RHO, NOW, SPEED, BEFORE, ADJ_NOW, ADJ_BEFORE = range(6)


def split_bf16(value):
    high = value.astype(jnp.bfloat16)
    low = (value - high.astype(jnp.float32)).astype(jnp.bfloat16)
    return high, low


def dot(a, b):
    return jnp.dot(a, b, preferred_element_type=jnp.float32)


def dot_nt(a, b):
    return lax.dot_general(a, b, (((1,), (1,)), ((), ())), preferred_element_type=jnp.float32)


def dot_tn_exact(a, b):
    dims = (((0,), (0,)), ((), ()))
    ah, al = split_bf16(a)
    bh, bl = split_bf16(b)
    one = lax.dot_general(ah, bh, dims, preferred_element_type=jnp.float32)
    two = lax.dot_general(al, bh, dims, preferred_element_type=jnp.float32)
    three = lax.dot_general(ah, bl, dims, preferred_element_type=jnp.float32)
    return one + (two + three)


def div(value, n):
    return lax.shift_right_arithmetic(value, jnp.full_like(value, n.bit_length() - 1))


def mod(value, n):
    return value & (n - 1)


def wave_kernel(
    sizes,
    log_density, fwd_now, velocity, fwd_before, adj_now, adj_before,
    given_observed, given_cells, given_counts, given_src, given_wavelet,
    grad_out, last_out, previous_out,
    field, vel, x_in, x_out, i_in, i_out, accel, base, image, slopes, speed_sq, wx,
    row_map, zmap_t, zmap, z_mat, residual_ref, traces, list_out, list_in, obs_in, g_send,
    held_observed, held_cells, held_counts, held_src, held_wavelet, row_mat, wide, deep,
    x_send, x_recv, i_send, i_recv, rt_send, rt_recv, rt_local, list_send, list_recv, obs_send, obs_recv,
    ret_send, ret_recv, ret_local, g_ssem, g_rsem, g_local, small_sem, pass_send, pass_recv,
):
    tile_i, tile_x, n_i, n_x, depth, steps, n_xline, fused = sizes
    rows = n_i * n_x
    small_in = (given_observed, given_cells, given_counts, given_src, given_wavelet)
    small_held = (held_observed, held_cells, held_counts, held_src, held_wavelet)
    slots = held_cells.shape[1]
    n_group = 2 * n_xline
    xl = lax.axis_index("xline")
    core = lax.axis_index("inline")
    me = xl * 2 + core
    y = lax.rem(xl, 2)
    plane = xl // 2
    z_odd = lax.rem(plane, 2)
    mate = xl + 1 - 2 * y
    cp = lax.rem(core + z_odd, 2)
    origin = y
    q = 2 * y + cp
    stays = y == core
    has = (xl >= 2, xl < n_xline - 2, q > 0, q < 3)
    other_core = 1 - core
    shot = lax.axis_index("shots")
    shares = (RHO, SPEED) if lax.axis_size("shots") == 2 else ()
    target = (
        {"xline": xl - 2, "inline": other_core},
        {"xline": xl + 2, "inline": other_core},
        {"xline": jnp.where(q == 2, mate, xl), "inline": other_core},
        {"xline": jnp.where(q == 1, mate, xl), "inline": other_core},
    )
    inner_i = pl.ds(4, n_i)
    inner_x = pl.ds(8, n_x)
    middle = n_i // 2

    barrier = pltpu.get_barrier_semaphore()

    def greet(device):
        pl.semaphore_signal(barrier, inc=1, device_id=device, device_id_type=MESH)

    near = n_xline // 2 <= 4
    if near:
        greet({"inline": other_core})
        greet({"xline": mate})
        greet({"xline": mate, "inline": other_core})
        for way in (LEFT, RIGHT):
            @pl.when(has[way])
            def _():
                greet(target[way])
        greeted = 3 + has[LEFT].astype(jnp.int32) + has[RIGHT].astype(jnp.int32)
    else:
        @pl.loop(1, n_group)
        def _(r):
            peer = lax.rem(me + r, n_group)
            greet({"xline": peer // 2, "inline": lax.rem(peer, 2)})
        greeted = n_group - 1
    if shares:
        greet({"shots": 1 - shot})
        greeted = greeted + 1

    small = [
        pltpu.make_async_copy(given, held, small_sem.at[n])
        for n, (given, held) in enumerate(zip(small_in, small_held))
    ]
    for copy in small:
        copy.start()
    observed, rec_cells, rec_counts, src_cell, wavelet = small_held

    layers = depth // 128
    half_x = n_x // 2

    def beside(idx, way, part, d):
        part_rows = pl.ds(part * middle, middle)
        return pltpu.make_async_remote_copy(
            src_ref=x_out.at[idx, way, d, part_rows], dst_ref=x_in.at[idx, 1 - way, d, part_rows],
            send_sem=x_send.at[idx, way], recv_sem=x_recv.at[idx, way, part, d],
            device_id=target[way], device_id_type=MESH,
        )

    def above(idx, part, c, d, arriving):
        up = part == 0
        return pltpu.make_async_remote_copy(
            src_ref=i_out.at[idx, part, d, c],
            dst_ref=i_in.at[idx, part if arriving else 1 - part, d, c],
            send_sem=i_send.at[idx, part],
            recv_sem=i_recv.at[idx, 1 - part if arriving else part, c, d],
            device_id={
                "xline": jnp.where(up, target[UP]["xline"], target[DOWN]["xline"]), "inline": other_core
            },
            device_id_type=MESH,
        )

    def has_row(part):
        return jnp.where(part == 0, q, 3 - q) > 0

    def send(idx, part, d, c):
        @pl.when(has[c])
        def _():
            beside(idx, c, part, d).start()

        @pl.when(has_row(part))
        def _():
            above(idx, part, c, d, False).start()

    def finish(idx, part, d, c):
        @pl.when(has[c])
        def _():
            beside(idx, 1 - c, part, d).wait_recv()

        @pl.when(has_row(part))
        def _():
            above(idx, part, c, d, True).wait_recv()

    def sent(idx):
        for n in range(2):
            @pl.when(has[n])
            def _():
                pltpu.make_async_remote_copy(
                    src_ref=x_out.at[idx, n], dst_ref=x_in.at[idx, 1 - n],
                    send_sem=x_send.at[idx, n], recv_sem=x_recv.at[idx, n, 0, 0],
                    device_id=target[n], device_id_type=MESH,
                ).wait_send()

            @pl.when(has[UP + n])
            def _():
                pltpu.make_async_remote_copy(
                    src_ref=i_out.at[idx, n], dst_ref=i_in.at[idx, 1 - n],
                    send_sem=i_send.at[idx, n], recv_sem=i_recv.at[idx, n, 0, 0],
                    device_id=target[UP + n], device_id_type=MESH,
                ).wait_send()

    def send_all(idx):
        for part, d, c in pieces:
            rows_at = pl.ds(part * middle, middle)
            x_out[idx, c, d, rows_at] = field[
                idx, pl.ds(4 + part * middle, middle), pl.ds(8 + c * (n_x - 4), 4), pl.ds(d * 128, 128)
            ]
            i_out[idx, part, d, c] = field[
                idx, pl.ds(4 + part * (n_i - 4), 4), pl.ds(8 + c * half_x, half_x), pl.ds(d * 128, 128)
            ]
            send(idx, part, d, c)

    halves = (1 - y, y)
    pieces = [(part, d, c) for part in halves for d in range(layers) for c in range(2)]

    sources = (log_density, fwd_now, velocity, fwd_before, adj_now, adj_before)
    places = (DENSITY, 0, None, 1, 2, 3)

    def landing(n, from_y):
        columns = pl.multiple_of(from_y * tile_x, tile_x)
        if n == SPEED:
            return vel.at[:, pl.ds(columns, tile_x), :]
        return field.at[places[n], inner_i, pl.ds(pl.multiple_of(8 + columns, 8), tile_x), :]

    def tile_copy(n, a):
        return pltpu.make_async_remote_copy(
            src_ref=sources[n].at[pl.ds(a * n_i, n_i)], dst_ref=landing(n, y),
            send_sem=rt_send.at[n, a], recv_sem=rt_recv.at[n, y],
            device_id={"xline": 2 * plane + core, "inline": lax.rem(a + z_odd, 2)},
            device_id_type=MESH,
        )

    def tile_arrival(n, from_y):
        return pltpu.make_async_remote_copy(
            src_ref=sources[n].at[pl.ds(0, n_i)], dst_ref=landing(n, from_y),
            send_sem=rt_send.at[n, 0], recv_sem=rt_recv.at[n, from_y],
            device_id={"xline": mate}, device_id_type=MESH,
        )

    def own_copy(n):
        return pltpu.make_async_copy(
            sources[n].at[pl.ds(cp * n_i, n_i)], landing(n, y), rt_local.at[n]
        )

    def leaves(a):
        return jnp.logical_not(jnp.logical_and(stays, cp == a))

    def arrives(from_y):
        return jnp.logical_not(jnp.logical_and(stays, y == from_y))

    def tile_start(n):
        for a in range(2):
            @pl.when(jnp.logical_and(stays, cp != a) if n in shares else leaves(a))
            def _():
                tile_copy(n, a).start()

        if n in shares:
            for a in range(2):
                @pl.when(jnp.logical_not(stays))
                def _():
                    half_copy(n, a).start()

        @pl.when(stays)
        def _():
            own_copy(n).start()

    def tile_finish(n):
        for from_y in range(2):
            @pl.when(jnp.logical_and(arrives(from_y), y == from_y) if n in shares else arrives(from_y))
            def _():
                tile_arrival(n, from_y).wait_recv()
        for a in range(2):
            @pl.when(jnp.logical_and(stays, cp != a) if n in shares else leaves(a))
            def _():
                tile_copy(n, a).wait_send()

        @pl.when(stays)
        def _():
            own_copy(n).wait()

        if n in shares:
            for a in range(2):
                @pl.when(jnp.logical_not(stays))
                def _():
                    half_copy(n, a).wait_send()
            pass_on(n).wait_send()
            passed_on(n).wait_recv()

    def quarter_start(n, which):
        for a in range(2):
            @pl.when(leaves(a))
            def _():
                pltpu.make_async_remote_copy(
                    src_ref=sources[n].at[pl.ds(a * n_i + which * middle, middle)], dst_ref=half_landing(n, y, which),
                    send_sem=rt_send.at[n, a], recv_sem=rt_recv.at[n, y],
                    device_id={"xline": 2 * plane + core, "inline": lax.rem(a + z_odd, 2)},
                    device_id_type=MESH,
                ).start()

        if which == 0:
            @pl.when(stays)
            def _():
                own_copy(n).start()

    def half_landing(n, from_y, which):
        columns = pl.multiple_of(from_y * tile_x, tile_x)
        if n == SPEED:
            return vel.at[pl.ds(which * middle, middle), pl.ds(columns, tile_x), :]
        return field.at[
            places[n], pl.ds(4 + which * middle, middle), pl.ds(pl.multiple_of(8 + columns, 8), tile_x), :
        ]

    def half_copy(n, a):
        return pltpu.make_async_remote_copy(
            src_ref=sources[n].at[pl.ds(a * n_i + shot * middle, middle)], dst_ref=half_landing(n, y, shot),
            send_sem=rt_send.at[n, a], recv_sem=rt_recv.at[n, y],
            device_id={"xline": mate, "inline": lax.rem(a + z_odd, 2)}, device_id_type=MESH,
        )

    def half_arrival(n):
        return pltpu.make_async_remote_copy(
            src_ref=sources[n].at[pl.ds(0, middle)], dst_ref=half_landing(n, 1 - y, shot),
            send_sem=rt_send.at[n, 0], recv_sem=rt_recv.at[n, 1 - y],
            device_id={"xline": mate}, device_id_type=MESH,
        )

    def pass_on(n):
        return pltpu.make_async_remote_copy(
            src_ref=half_landing(n, 1 - y, shot), dst_ref=half_landing(n, 1 - y, shot),
            send_sem=pass_send.at[n], recv_sem=pass_recv.at[n],
            device_id={"shots": 1 - shot}, device_id_type=MESH,
        )

    def passed_on(n):
        return pltpu.make_async_remote_copy(
            src_ref=half_landing(n, 1 - y, shot), dst_ref=half_landing(n, 1 - y, 1 - shot),
            send_sem=pass_send.at[n], recv_sem=pass_recv.at[n],
            device_id={"shots": 1 - shot}, device_id_type=MESH,
        )

    def list_copy(a):
        return pltpu.make_async_remote_copy(
            src_ref=list_out, dst_ref=list_in.at[y],
            send_sem=list_send.at[a], recv_sem=list_recv.at[y],
            device_id={"xline": 2 * plane + core, "inline": lax.rem(a + z_odd, 2)},
            device_id_type=MESH,
        )

    def list_arrival(from_y):
        return pltpu.make_async_remote_copy(
            src_ref=list_out, dst_ref=list_in.at[from_y],
            send_sem=list_send.at[0], recv_sem=list_recv.at[from_y],
            device_id={"xline": mate}, device_id_type=MESH,
        )

    def obs_copy(peer, slot):
        return pltpu.make_async_remote_copy(
            src_ref=observed, dst_ref=obs_in.at[slot],
            send_sem=obs_send.at[peer], recv_sem=obs_recv.at[slot],
            device_id={"xline": peer // 2, "inline": lax.rem(peer, 2)}, device_id_type=MESH,
        )

    finals = (previous_out, last_out)
    final_idx = (2 + (steps - 1) % 2, 2 + steps % 2)

    def home_copy(n, to_y):
        return pltpu.make_async_remote_copy(
            src_ref=field.at[final_idx[n], inner_i, pl.ds(8 + to_y * tile_x, tile_x), :],
            dst_ref=finals[n].at[pl.ds(cp * n_i, n_i)],
            send_sem=ret_send.at[n, to_y], recv_sem=ret_recv.at[n, cp],
            device_id={"xline": 2 * plane + to_y, "inline": origin}, device_id_type=MESH,
        )

    def home_arrival(n, a):
        return pltpu.make_async_remote_copy(
            src_ref=field.at[final_idx[n], inner_i, pl.ds(8, tile_x), :],
            dst_ref=finals[n].at[pl.ds(a * n_i, n_i)],
            send_sem=ret_send.at[n, 0], recv_sem=ret_recv.at[n, a],
            device_id={"xline": mate}, device_id_type=MESH,
        )

    def home_own(n):
        columns = pl.multiple_of(8 + y * tile_x, 8)
        return pltpu.make_async_copy(
            field.at[final_idx[n], inner_i, pl.ds(columns, tile_x), :],
            finals[n].at[pl.ds(cp * n_i, n_i)], ret_local.at[n],
        )

    def home_start(n):
        for to_y in range(2):
            @pl.when(arrives(to_y))
            def _():
                home_copy(n, to_y).start()

        @pl.when(stays)
        def _():
            home_own(n).start()

    def home_finish(n):
        for to_y in range(2):
            @pl.when(arrives(to_y))
            def _():
                home_copy(n, to_y).wait_send()
        for a in range(2):
            @pl.when(leaves(a))
            def _():
                home_arrival(n, a).wait_recv()

        @pl.when(stays)
        def _():
            home_own(n).wait()

    dz = depth // n_xline
    planes_n = n_xline // 2

    def slab_copy(d):
        return pltpu.make_async_remote_copy(
            src_ref=g_send.at[d],
            dst_ref=grad_out.at[cp, :, pl.ds(pl.multiple_of(plane * n_x, 8), n_x), :],
            send_sem=g_ssem.at[d], recv_sem=g_rsem.at[cp, plane],
            device_id={"xline": d, "inline": origin}, device_id_type=MESH,
        )

    def own_slab():
        return pltpu.make_async_copy(
            g_send.at[xl], grad_out.at[cp, :, pl.ds(pl.multiple_of(plane * n_x, 8), n_x), :], g_local.at[0]
        )

    def slab_arrival(a, p):
        return pltpu.make_async_remote_copy(
            src_ref=g_send.at[0],
            dst_ref=grad_out.at[a, :, pl.ds(pl.multiple_of(p * n_x, 8), n_x), :],
            send_sem=g_ssem.at[0], recv_sem=g_rsem.at[a, p],
            device_id={"xline": mate}, device_id_type=MESH,
        )

    def fused_gradient():
        group = 128 // dz
        lane = div(lax.broadcasted_iota(jnp.int32, (n_x, 128), 1), dz)
        for chunk in range(depth // 128):
            for ig in range(n_i // group):
                planes = [image[ig * group + j, :, pl.ds(chunk * 128, 128)] for j in range(group)]
                for dd in range(group):
                    out = None
                    for j in range(group):
                        shift = (j - dd) * dz % 128
                        moved = pltpu.roll(planes[j], shift, axis=1) if shift else planes[j]
                        out = moved if out is None else jnp.where(lane == j, moved, out)
                    g_send[chunk * group + dd, ig] = out

        @pl.loop(1, n_xline + 1)
        def _(r):
            d = lax.rem(xl + r, n_xline)

            @pl.when(jnp.logical_or(d != xl, origin != core))
            def _():
                slab_copy(d).start()

        home_start(1)

        @pl.when(origin == core)
        def _():
            own_slab().start()

        @pl.loop(0, n_xline)
        def _(r):
            a, p = lax.rem(r, 2), r // 2
            mine = jnp.logical_and(origin == core, jnp.logical_and(a == cp, p == plane))

            @pl.when(jnp.logical_not(mine))
            def _():
                slab_arrival(a, p).wait_recv()

        @pl.when(origin == core)
        def _():
            own_slab().wait()

        @pl.loop(1, n_xline + 1)
        def _(r):
            d = lax.rem(xl + r, n_xline)

            @pl.when(jnp.logical_or(d != xl, origin != core))
            def _():
                slab_copy(d).wait_send()

    for way in (LEFT, RIGHT, UP, DOWN):
        @pl.when(jnp.logical_not(has[way]))
        def _():
            halo = x_in if way < UP else i_in
            halo[:, way % 2] = jnp.zeros(halo.shape[:1] + halo.shape[2:], jnp.float32)
    image[...] = jnp.zeros(image.shape, jnp.float32)

    for copy in small:
        copy.wait()
    n_counts = rec_counts.shape[1]
    spread = (
        div(lax.broadcasted_iota(jnp.int32, (n_counts, slots), 1), CAP)
        == lax.broadcasted_iota(jnp.int32, (n_counts, slots), 0)
    ).astype(jnp.float32).astype(jnp.bfloat16)
    counts = jnp.broadcast_to(rec_counts[...].astype(jnp.float32), (8, n_counts)).astype(jnp.bfloat16)
    live = dot(counts, spread)
    place = mod(lax.broadcasted_iota(jnp.int32, (8, slots), 1), CAP).astype(jnp.float32)
    list_out[...] = jnp.where(place < live, jnp.broadcast_to(rec_cells[...], (8, slots)), -1)

    pl.semaphore_wait(barrier, greeted)

    for a in range(2):
        @pl.when(leaves(a))
        def _():
            list_copy(a).start()

    for n in (RHO, SPEED, NOW):
        tile_start(n)
    tile_start(BEFORE)

    obs_in[me] = observed[...]

    @pl.when(stays)
    def _():
        list_in[y] = list_out[...]

    offset = lax.broadcasted_iota(jnp.int32, (depth, depth), 0) - lax.broadcasted_iota(jnp.int32, (depth, depth), 1)
    second = jnp.zeros((depth, depth), jnp.float32)
    first = jnp.zeros((depth, depth), jnp.float32)
    for k in range(1, 5):
        second = jnp.where((offset == k) | (offset == -k), SECOND_COEFFS[k] / SECOND_COEFFS[1], second)
        first = jnp.where(offset == k, FIRST_COEFFS[k - 1] / FIRST_COEFFS[0], first)
        first = jnp.where(offset == -k, -FIRST_COEFFS[k - 1] / FIRST_COEFFS[0], first)
    z_mat[:, pl.ds(0, depth)] = second.astype(jnp.bfloat16)
    z_mat[:, pl.ds(depth, depth)] = first.astype(jnp.bfloat16)

    at = lax.broadcasted_iota(jnp.int32, (rows, rows), 0)
    to = lax.broadcasted_iota(jnp.int32, (rows, rows), 1)
    step_i = div(to, n_x) - div(at, n_x)
    step_x = mod(to, n_x) - mod(at, n_x)
    lateral_lap = jnp.zeros((rows, rows), jnp.float32)
    for n, (along, still) in enumerate(((step_i, step_x), (step_x, step_i))):
        along = jnp.where(still == 0, along, 0)
        first = jnp.zeros((rows, rows), jnp.float32)
        for k in range(1, 5):
            lateral_lap = jnp.where((along == k) | (along == -k), SECOND_COEFFS[k] / SECOND_COEFFS[1], lateral_lap)
            first = jnp.where(along == k, FIRST_COEFFS[k - 1] / FIRST_COEFFS[0], first)
            first = jnp.where(along == -k, -FIRST_COEFFS[k - 1] / FIRST_COEFFS[0], first)
        row_mat[pl.ds((n + 1) * rows, rows), :] = first.astype(jnp.bfloat16)
    row_mat[pl.ds(0, rows), :] = lateral_lap.astype(jnp.bfloat16)

    full_x = tile_x * n_xline
    cells = src_cell[...]
    src_i = div(cells, full_x * depth) - q * n_i
    src_x = mod(div(cells, depth), full_x) - plane * n_x
    inside = (src_i >= 0) & (src_i < n_i) & (src_x >= 0) & (src_x < n_x)
    src_row = jnp.where(inside, src_i * n_x + src_x, -1)
    n_src = cells.shape[1]
    src_rows = (lax.broadcasted_iota(jnp.int32, (rows, n_src), 0) == src_row).astype(jnp.float32)
    src_cols = (lax.broadcasted_iota(jnp.int32, (depth, n_src), 0) == mod(cells, depth)).astype(jnp.float32).astype(jnp.bfloat16)

    def flat(idx):
        return field[idx, inner_i, inner_x, :].reshape(rows, depth)

    def differences(idx):
        high, low = split_bf16(flat(idx))
        wide[...] = dot(row_mat[...], high) + dot(row_mat[...], low)
        deep[...] = dot(high, z_mat[...]) + dot(low, z_mat[...])

    def operator(idx, i):
        def line(n):
            return pl.ds(pl.multiple_of(n * rows + i * n_x, n_x), n_x)

        center = field[idx, i + 4, inner_x, :]
        return center, (
            3.0 * SECOND_COEFFS[0] * center
            + SECOND_COEFFS[1] * (wide[line(0), :] + deep[line(0), pl.ds(0, depth)])
            - slopes[0, i] * wide[line(1), :] - slopes[1, i] * wide[line(2), :]
            - slopes[2, i] * deep[line(0), pl.ds(depth, depth)]
        )

    def across(idx, i):
        lap = slope_i = slope_x = None
        for k in range(1, 5):
            plus_i = field[idx, i + 4 + k, inner_x, :]
            minus_i = field[idx, i + 4 - k, inner_x, :]
            plus_x = field[idx, i + 4, pl.ds(8 + k, n_x), :]
            minus_x = field[idx, i + 4, pl.ds(8 - k, n_x), :]
            terms = (
                SECOND_COEFFS[k] * ((plus_i + minus_i) + (plus_x + minus_x)),
                FIRST_COEFFS[k - 1] * (plus_i - minus_i),
                FIRST_COEFFS[k - 1] * (plus_x - minus_x),
            )
            if lap is None:
                lap, slope_i, slope_x = terms
            else:
                lap, slope_i, slope_x = lap + terms[0], slope_i + terms[1], slope_x + terms[2]
        return lap, slope_i, slope_x

    for n in shares:
        half_arrival(n).wait_recv()
        pass_on(n).start()
    tile_finish(RHO)
    send_all(DENSITY)
    tile_finish(NOW)
    send_all(0)

    high, low = split_bf16(flat(DENSITY))
    deep[...] = dot(high, z_mat[...]) + dot(low, z_mat[...])
    slopes[2] = ((FIRST_COEFFS[0] * FIRST_COEFFS[0]) * deep[:, pl.ds(depth, depth)]).reshape(n_i, n_x, depth)
    differences(0)

    def inject_sources(t):
        high, low = split_bf16(src_rows * wavelet[pl.ds(t, 1), :])
        return dot_nt(high, src_cols) + dot_nt(low, src_cols)

    accel[0] = inject_sources(0).reshape(n_i, n_x, depth)

    for from_y in range(2):
        @pl.when(arrives(from_y))
        def _():
            list_arrival(from_y).wait_recv()
    for a in range(2):
        @pl.when(leaves(a))
        def _():
            list_copy(a).wait_send()
    for from_y in range(2):
        spot = list_in[from_y][:1]
        cell_i = div(spot, tile_x * depth) - cp * n_i
        cell_x = mod(div(spot, depth), tile_x) + from_y * tile_x
        row = jnp.where((spot >= 0) & (cell_i >= 0) & (cell_i < n_i), cell_i * n_x + cell_x, -1)
        columns = pl.ds(from_y * slots, slots)
        row_map[:, columns] = (lax.broadcasted_iota(jnp.int32, (rows, slots), 0) == row).astype(jnp.float32)
        zmap_t[:, columns] = (
            lax.broadcasted_iota(jnp.int32, (depth, slots), 0) == mod(spot, depth)
        ).astype(jnp.float32).astype(jnp.bfloat16)

    zmap[...] = zmap_t[...].astype(jnp.float32).T.astype(jnp.bfloat16)

    for part, d, c in pieces:
        finish(DENSITY, part, d, c)
    sent(DENSITY)
    for d in range(layers):
        lanes = pl.ds(d * 128, 128)
        for side in range(2):
            for c in range(2):
                field[DENSITY, pl.ds(side * (n_i + 4), 4), pl.ds(8 + c * half_x, half_x), lanes] = i_in[DENSITY, side, d, c]
            field[DENSITY, inner_i, pl.ds(4 + side * (n_x + 4), 4), lanes] = x_in[DENSITY, side, d]

    @pl.loop(0, n_i)
    def _(i):
        _, slope_i, slope_x = across(DENSITY, i)
        slopes[0, i] = FIRST_COEFFS[0] * slope_i
        slopes[1, i] = FIRST_COEFFS[0] * slope_x

    tile_finish(SPEED)
    column = lax.broadcasted_iota(jnp.int32, (n_x, depth), 0)

    @pl.loop(0, n_i)
    def _(i):
        square = vel[i] * vel[i]
        speed_sq[i] = square
        accel[0, i] += square * operator(0, i)[1]
        for k in range(1, 5):
            weight = jnp.where(
                column < k, SECOND_COEFFS[k] + (FIRST_COEFFS[k - 1] / FIRST_COEFFS[0]) * slopes[1, i],
                jnp.where(
                    column >= n_x - k, SECOND_COEFFS[k] - (FIRST_COEFFS[k - 1] / FIRST_COEFFS[0]) * slopes[1, i], 0.0
                ),
            )
            wx[k - 1, i] = square * weight

    tile_finish(BEFORE)

    @pl.loop(0, n_i)
    def _(i):
        field[1, i + 4, inner_x, :] = (
            2.0 * field[0, i + 4, inner_x, :] - field[1, i + 4, inner_x, :] + accel[0, i]
        )

    def start_traces(third):
        @pl.loop(1 + (n_group - 1) * third // 3, 1 + (n_group - 1) * (third + 1) // 3)
        def _(r):
            obs_copy(lax.rem(me + r, n_group), me).start()

    def make_traces(from_y):
        @pl.loop(1, n_group)
        def _(r):
            peer = lax.rem(me + r, n_group)
            if from_y == 0:
                obs_copy(peer, peer).wait_recv()
            else:
                obs_copy(peer, me).wait_send()

        lane = div(lax.broadcasted_iota(jnp.int32, (8, slots), 1), CAP)
        owner = (2 * plane + from_y) * 2 + origin

        def place_one(s, total):
            moved = pltpu.roll(obs_in[s], lax.rem(s - owner + n_group, n_group) * CAP, axis=1)
            return jnp.where(lane == s, moved, total)

        traces[:, pl.ds(from_y * slots, slots)] = lax.fori_loop(
            0, n_group, place_one, jnp.zeros((8, slots), jnp.float32)
        )

    def prepare(idx, term):
        base[...] = term.reshape(n_i, n_x, depth)
        differences(idx)

    def interior(now, other, i):
        center, value = operator(now, i)
        change = base[i] + speed_sq[i] * value
        field[other, i + 4, inner_x, :] = 2.0 * center - field[other, i + 4, inner_x, :] + change
        return center, change

    def correct(now, other, part, d, c, t):
        up = part == 0
        sign = jnp.where(up, 1.0, -1.0)
        columns, lanes = pl.ds(c * half_x, half_x), pl.ds(d * 128, 128)
        for r in range(middle):
            i = jnp.where(up, r, n_i - 1 - r)
            halo = x_in[now, c, d, i]
            pair = jnp.concatenate([halo] * (half_x // 4), axis=0)
            change = wx[3, i, columns, lanes] * pair
            for k in range(1, 4):
                change += wx[k - 1, i, columns, lanes] * pltpu.roll(pair, half_x - k if c else k, axis=0)
            lap = None
            for h in range(4 - r):
                k = r + 1 + h
                halo = i_in[now, part, d, c, jnp.where(up, 3 - h, h)]
                terms = SECOND_COEFFS[k] * halo, (FIRST_COEFFS[k - 1] / FIRST_COEFFS[0]) * halo
                lap, slope = terms if lap is None else (lap + terms[0], slope + terms[1])
            if lap is not None:
                change += speed_sq[i, columns, lanes] * (lap + (sign * slopes[0, i, columns, lanes]) * slope)
            spot = (other, i + 4, pl.ds(8 + c * half_x, half_x), lanes)
            fresh = field[spot] + change
            field[spot] = fresh
            x_out[other, c, d, i] = fresh[half_x - 4:] if c else fresh[:4]
            if r < 4:
                i_out[other, part, d, c, jnp.where(up, r, 3 - r)] = fresh
            if t is not None:
                accel[t, i, columns, lanes] += change

    def sample(idx, t):
        high, low = split_bf16(flat(idx))
        picked = dot(high, zmap_t[...]) + dot(low, zmap_t[...])
        predicted = jnp.sum(picked * row_map[...], axis=0, keepdims=True)
        residual_ref[t] = predicted

    def task_first():
        quarter_start(ADJ_NOW, 0)

    def task_second():
        quarter_start(ADJ_NOW, 1)

    def task_third():
        quarter_start(ADJ_BEFORE, 0)

    def task_fourth():
        quarter_start(ADJ_BEFORE, 1)
        start_traces(0)
        start_traces(1)
        start_traces(2)

    def task_halos():
        tile_finish(ADJ_NOW)
        send_all(2)

    def task_adjoint():
        tile_finish(ADJ_BEFORE)
        differences(2)
        vel[...] = (2.0 / steps) / vel[...]

        @pl.loop(0, n_i, unroll=8)
        def _(i):
            center, value = operator(2, i)
            field[3, i + 4, inner_x, :] = (
                2.0 * center - field[3, i + 4, inner_x, :] + speed_sq[i] * value
            )

    tasks = [task_first, task_second, task_third, task_fourth, task_halos, functools.partial(make_traces, 0), functools.partial(make_traces, 1), task_adjoint]
    times = [n * steps // 8 for n in (0, 1, 2, 3, 4, 6, 7, 5)]

    @pl.loop(0, steps)
    def _(t):
        now = lax.rem(t, 2)
        other = 1 - now

        @pl.when(t > 0)
        def _():
            prepare(now, inject_sources(t))

            @pl.loop(0, n_i, unroll=16)
            def _(i):
                _, change = interior(now, other, i)
                accel[t, i] = change

        for at, task in zip(times, tasks):
            pl.when(t == at)(task)

        @pl.when(t >= 1)
        def _():
            sample(now, t - 1)
            sent(other)

        for part, d, c in pieces:
            finish(now, part, d, c)
            correct(now, other, part, d, c, t)

            @pl.when(t < steps - 1)
            def _():
                send(other, part, d, c)

    sent((steps - 1) % 2)
    sample(steps % 2, steps - 1)

    @pl.loop(0, steps)
    def _(j):
        now = 2 + lax.rem(j, 2)
        other = 5 - now
        t = steps - 1 - j
        high, low = split_bf16(row_map[...] * (residual_ref[t] - traces[pl.ds(t, 1), :]))
        injected = dot(high, zmap[...]) + dot(low, zmap[...])

        @pl.when(j == 0)
        def _():
            field[3, inner_i, inner_x, :] += injected.reshape(n_i, n_x, depth)

        @pl.when(j > 0)
        def _():
            prepare(now, injected)

            @pl.loop(0, n_i, unroll=16)
            def _(i):
                center, _ = interior(now, other, i)
                image[i] += center * accel[t + 1, i]

            sent(other)

        @pl.when(j == steps - 1)
        def _():
            home_start(0)

        for part, d, c in pieces:
            finish(now, part, d, c)
            correct(now, other, part, d, c, None)

            @pl.when(j < steps - 1)
            def _():
                send(other, part, d, c)

    sent(2 + (steps - 1) % 2)

    @pl.loop(0, n_i, unroll=16)
    def _(i):
        image[i] = (image[i] + field[final_idx[1], i + 4, inner_x, :] * accel[0, i]) * vel[i]

    if fused:
        fused_gradient()
    else:
        grad_out[...] = image[...]
        home_start(1)
    home_finish(0)
    home_finish(1)


def finish_kernel(shape, slabs, last, previous):
    dz, tile_i, full_x = shape
    _, n_groups, _, lanes = slabs.shape
    group = lanes // dz

    def kernel(
        slabs_in, last_in, previous_in, gradient, last_out, previous_out,
        slabs_held, last_held, previous_held, lines_held, in_sem, out_sem,
    ):
        loads = [
            pltpu.make_async_copy(slabs_in, slabs_held, in_sem.at[0]),
            pltpu.make_async_copy(last_in, last_held, in_sem.at[1]),
            pltpu.make_async_copy(previous_in, previous_held, in_sem.at[2]),
        ]
        for load in loads:
            load.start()
        far = (
            lax.broadcasted_iota(jnp.int32, (full_x, full_x), 0) - lax.broadcasted_iota(jnp.int32, (full_x, full_x), 1)
        ).astype(jnp.float32)
        weights = jnp.exp(-jnp.abs(far) / SMOOTH)
        weights = weights / jnp.sum(weights, axis=0, keepdims=True)
        stores = [
            pltpu.make_async_copy(last_held, last_out, out_sem.at[0]),
            pltpu.make_async_copy(previous_held, previous_out, out_sem.at[1]),
        ]
        for load, store in zip(loads[1:], stores):
            load.wait()
            store.start()
        loads[0].wait()
        for a in range(2):
            for ig in range(n_groups):
                lines = dot_tn_exact(slabs_held[a, ig], weights)
                for j in range(group):
                    lines_held[:, (a * n_groups + ig) * group + j, :] = lines[j * dz:(j + 1) * dz]
            span = pl.ds(a * (tile_i // 2), tile_i // 2)
            store = pltpu.make_async_copy(lines_held.at[:, span, :], gradient.at[:, span, :], out_sem.at[2 + a])
            store.start()
            stores.append(store)
        for store in stores:
            store.wait()

    anywhere = pl.BlockSpec(memory_space=pl.ANY)
    return pl.pallas_call(
        kernel,
        out_shape=[jax.ShapeDtypeStruct(dims, jnp.float32) for dims in (shape, last.shape, previous.shape)],
        in_specs=[anywhere] * 3,
        out_specs=[anywhere] * 3,
        scratch_shapes=[
            *[pltpu.VMEM(dims, jnp.float32) for dims in (slabs.shape, last.shape, previous.shape, shape)],
            pltpu.SemaphoreType.DMA((3,)),
            pltpu.SemaphoreType.DMA((4,)),
        ],
        compiler_params=pltpu.CompilerParams(vmem_limit_bytes=56 * 1024 * 1024),
    )(slabs, last, previous)


def per_device(
    fwd_now, fwd_before, adj_now, adj_before, velocity, log_density,
    observed, rec_cells, rec_counts, src_cell, wavelet,
):
    tile_i, tile_x, depth = fwd_now.shape
    steps = wavelet.shape[0]
    n_xline = lax.axis_size("xline")
    full_x = tile_x * n_xline
    n_i, n_x = tile_i // 2, tile_x * 2
    rows = n_i * n_x
    slots = rec_cells.shape[1]
    n_group = 2 * n_xline
    dz = depth // n_xline
    fused = dz >= 8 and 128 % dz == 0 and depth % 128 == 0 and n_i % (128 // dz) == 0
    group = 128 // dz if fused else 1
    layers = depth // 128

    block = (n_i, n_x, depth)
    vmem = pl.BlockSpec(memory_space=pltpu.VMEM)
    anywhere = pl.BlockSpec(memory_space=pl.ANY)
    dma = pltpu.SemaphoreType.DMA
    kernel = functools.partial(wave_kernel, (tile_i, tile_x, n_i, n_x, depth, steps, n_xline, fused))
    grad_shape = (2, n_i // group, full_x, 128) if fused else block
    slab_shape = (n_xline, n_i // group, n_x, 128) if fused else (8, 128)
    small_shapes = [observed, rec_cells, rec_counts, src_cell[None, :], wavelet]
    raw, last, previous = pl.pallas_call(
        kernel,
        out_shape=[
            jax.ShapeDtypeStruct(grad_shape, jnp.float32),
            jax.ShapeDtypeStruct(fwd_now.shape, jnp.float32),
            jax.ShapeDtypeStruct(fwd_now.shape, jnp.float32),
        ],
        in_specs=[anywhere] * 11,
        out_specs=[anywhere if fused else vmem, anywhere, anywhere],
        scratch_shapes=[
            pltpu.VMEM((5, n_i + 8, n_x + 16, depth), jnp.float32),
            pltpu.VMEM(block, jnp.float32),
            pltpu.VMEM((5, 2, layers, n_i, 4, 128), jnp.float32),
            pltpu.VMEM((5, 2, layers, n_i, 4, 128), jnp.float32),
            pltpu.VMEM((5, 2, layers, 2, 4, tile_x, 128), jnp.float32),
            pltpu.VMEM((5, 2, layers, 2, 4, tile_x, 128), jnp.float32),
            pltpu.VMEM((steps,) + block, jnp.float32),
            pltpu.VMEM(block, jnp.float32),
            pltpu.VMEM(block, jnp.float32),
            pltpu.VMEM((3,) + block, jnp.float32),
            pltpu.VMEM(block, jnp.float32),
            pltpu.VMEM((4,) + block, jnp.float32),
            pltpu.VMEM((rows, 2 * slots), jnp.float32),
            pltpu.VMEM((depth, 2 * slots), jnp.bfloat16),
            pltpu.VMEM((2 * slots, depth), jnp.bfloat16),
            pltpu.VMEM((depth, 2 * depth), jnp.bfloat16),
            pltpu.VMEM((steps, 1, 2 * slots), jnp.float32),
            pltpu.VMEM((steps, 2 * slots), jnp.float32),
            pltpu.VMEM((8, slots), jnp.int32),
            pltpu.VMEM((2, 8, slots), jnp.int32),
            pltpu.VMEM((n_group,) + observed.shape, jnp.float32),
            pltpu.VMEM(slab_shape, jnp.float32),
            *[pltpu.VMEM(value.shape, value.dtype) for value in small_shapes],
            pltpu.VMEM((3 * rows, rows), jnp.bfloat16),
            pltpu.VMEM((3 * rows, depth), jnp.float32),
            pltpu.VMEM((rows, 2 * depth), jnp.float32),
            dma((5, 2)), dma((5, 2, 2, layers)), dma((5, 2)), dma((5, 2, 2, layers)),
            dma((6, 2)), dma((6, 2)), dma((6,)),
            dma((2,)), dma((2,)),
            dma((n_group,)), dma((n_group,)),
            dma((2, 2)), dma((2, 2)), dma((2,)),
            dma((n_xline,)), dma((2, n_xline // 2)), dma((1,)), dma((5,)),
            dma((6,)), dma((6,)),
        ],
        compiler_params=pltpu.CompilerParams(
            collective_id=0, has_side_effects=True, vmem_limit_bytes=56 * 1024 * 1024
        ),
    )(
        log_density, fwd_now, velocity, fwd_before, adj_now, adj_before,
        *small_shapes,
    )
    if fused:
        return finish_kernel((dz, tile_i, full_x), raw, last, previous)

    places = []
    for xl in range(n_xline):
        for core in range(2):
            y, plane = xl % 2, xl // 2
            cp = (core + plane % 2) % 2
            places.append((xl * 2 + core, (2 * plane + cp) * 2 + y))
    raw = lax.ppermute(raw, ("xline", "inline"), places)
    columns = lax.all_to_all(
        raw.reshape(n_i, n_x, n_xline, dz).transpose(2, 0, 1, 3),
        "xline", split_axis=0, concat_axis=0, tiled=True,
    ).reshape(n_xline // 2, 2, n_i, n_x, dz)
    positions = jnp.arange(full_x).astype(jnp.float32)
    weights = jnp.exp(-jnp.abs(positions[:, None] - positions[None, :]) / SMOOTH)
    weights = weights / jnp.sum(weights, axis=1, keepdims=True)
    gradient = jnp.einsum(
        "phixz,ypx->zhiy", columns, weights.reshape(full_x, n_xline // 2, n_x),
        precision=lax.Precision.HIGHEST,
    ).reshape(dz, tile_i, full_x)
    return gradient, last, previous


def solution(mesh):
    return jax.shard_map(
        per_device,
        mesh=mesh,
        in_specs=(
            P(("shots", "inline"), "xline", None),
            P(("shots", "inline"), "xline", None),
            P(("shots", "inline"), "xline", None),
            P(("shots", "inline"), "xline", None),
            P("inline", "xline", None),
            P("inline", "xline", None),
            P("shots", ("xline", "inline")),
            P(("xline", "inline"), None),
            P(("xline", "inline"), None),
            P("shots"),
            P("shots", None),
        ),
        out_specs=(
            P(("shots", "xline"), "inline", None),
            P(("shots", "inline"), "xline", None),
            P(("shots", "inline"), "xline", None),
        ),
        check_vma=False,
    )
```
